32 devices in a mesh: space: 8 (over z, y), elem: 4 (over x, core).
Axes of the slice: x: 2, y: 2, z: 4, core: 2. Of those that a mesh axis runs over, the one named last changes fastest.
Arguments:
- features: bfloat16 [3, 8192, 256], P(None, ('space', 'elem')), may hold values from -6 to 6
- charges: float32 [3, 2, 8192], P(None, None, ('space', 'elem')), may hold values from -3 to 3
- elements: int32 [3, 8192], P(None, ('space', 'elem')), may hold values from 0 to 7, as said below
- neighbours: int32 [3, 32, 8192], P(None, None, ('space', 'elem')), may hold values from 0 to 319, as said below
- counts: int32 [3, 8192], P(None, ('space', 'elem')), may hold values from 16 to 32, as said below
- distances: float32 [3, 32, 8192], P(None, None, ('space', 'elem')), may hold values from 0.8 to 4.9
- radial: float32 [2, 16, 256], replicated, may hold values from -1 to 1
- radial_mom: float32 [2, 16, 256], replicated, may hold values from -512 to 512
- mixing: float32 [2, 2, 256], replicated, may hold values from -4 to 4
- mixing_mom: float32 [2, 2, 256], replicated, may hold values from -96 to 96
- w_in: float32 [2, 8, 512, 380], P(None, 'elem'), may hold values from -0.25 to 0.25
- w_mid: float32 [2, 8, 380, 380], P(None, 'elem'), may hold values from -0.3125 to 0.3125
- w_out: float32 [2, 8, 380, 256], P(None, 'elem'), may hold values from -0.625 to 0.625
- mom_in: float32 [2, 8, 512, 380], P(None, 'elem'), may hold values from -128 to 128
- mom_mid: float32 [2, 8, 380, 380], P(None, 'elem'), may hold values from -128 to 128
- mom_out: float32 [2, 8, 380, 256], P(None, 'elem'), may hold values from -160 to 160
- cot_features: bfloat16 [3, 8192, 256], P(None, ('space', 'elem')), may hold values from -6 to 6
- cot_charges: float32 [3, 2, 8192], P(None, None, ('space', 'elem')), may hold values from -6 to 6
Outputs:
- features_out: float32 [3, 8192, 256], P(None, ('space', 'elem'))
- charges_out: float32 [3, 2, 8192], P(None, None, ('space', 'elem'))
- grad_features: float32 [3, 8192, 256], P(None, ('space', 'elem'))
- grad_charges: float32 [3, 2, 8192], P(None, None, ('space', 'elem'))
- new_w_in: float32 [2, 8, 512, 380], P(None, 'elem')
- new_w_mid: float32 [2, 8, 380, 380], P(None, 'elem')
- new_w_out: float32 [2, 8, 380, 256], P(None, 'elem')
- new_mom_in: float32 [2, 8, 512, 380], P(None, 'elem')
- new_mom_mid: float32 [2, 8, 380, 380], P(None, 'elem')
- new_mom_out: float32 [2, 8, 380, 256], P(None, 'elem')
- new_radial: float32 [2, 16, 256], replicated
- new_radial_mom: float32 [2, 16, 256], replicated
- new_mixing: float32 [2, 2, 256], replicated
- new_mixing_mom: float32 [2, 2, 256], replicated
The draws below stay inside these ranges and needn't reach their ends.
Inputs may be any that keep to these rules, and one draw needn't show every extreme that they name: `elements`: on one device at most 64 atoms have the same element, and on every device some element has exactly 64 atoms. `neighbours`: rows of a device's extended block: rows 0 to 31 are the last 32 atoms of the device before it along space+elem (cyclically), then its own 256 atoms (own index r at extended row r + 32), then the first 32 atoms of the device after it. The entries of the device's atom with own index r lie within r to r + 64 and are never r + 32. `counts`: every device has an atom with all 32 slots live.
All inputs are finite; a program needn't handle non-finite values.
Results may differ from the reference program's by a relative error of at most 0.014.
The reference program's roundings to bfloat16 on the way count: a program that leaves them out, or rounds other values in their place, can miss the bound.
Values may be sent and summed in bfloat16 or wider, within the bound.
No kernel may reach another device: no remote copies, remote signals or barrier semaphores. Data moves between devices by JAX's collectives and lax.ppermute only.
A program may use at most 192 MiB of HBM per device.

```python
import math
from functools import partial
import jax
import jax.numpy as jnp
from jax import lax

D = 256
HID = 380
SHELLS = 16
CHANNELS = 2
IN = 512
SLOTS = 32
ATOMS_DEV = 256
MICRO = 3
LAYERS = 2
OWNERS = 4
ELEMS = 8
CAP = 64
HALO = 32
ATOMS = 8192


def draw_elements(key, part):
    key = jax.random.fold_in(key, 11)
    group_count = ATOMS // (ATOMS_DEV * OWNERS)
    favour_key, block_key = jax.random.split(key)
    favoured = jax.random.randint(favour_key, (MICRO * group_count,), 0, ELEMS)
    favoured = jnp.repeat(favoured, OWNERS)
    block_keys = jax.random.split(block_key, MICRO * group_count * OWNERS)

    def one_device(device_key, favourite):
        pick_key, order_key = jax.random.split(device_key)
        others = jax.random.permutation(pick_key, (ELEMS - 1) * CAP)[:ATOMS_DEV - CAP] // CAP
        others = (others + (others >= favourite).astype(jnp.int32)).astype(jnp.int32)
        element_list = jnp.concatenate([jnp.full((CAP,), favourite, jnp.int32), others])
        return jax.random.permutation(order_key, element_list)
    devices = jax.vmap(one_device)(block_keys, favoured)
    return devices.reshape(MICRO, ATOMS).astype(jnp.int32)


def draw_neighbours(key, part):
    key = jax.random.fold_in(key, 12)
    choice_value = jax.random.randint(key, (MICRO, SLOTS, ATOMS), 0, 2 * HALO)
    offset = choice_value - HALO + (choice_value >= HALO).astype(jnp.int32)
    row_index = lax.broadcasted_iota(jnp.int32, (MICRO, SLOTS, ATOMS), 2) % ATOMS_DEV
    return (row_index + HALO + offset).astype(jnp.int32)


def draw_counts(key, part):
    key = jax.random.fold_in(key, 13)
    base_key, chosen_key = jax.random.split(key)
    device_count = ATOMS // ATOMS_DEV
    base_counts = jax.random.randint(base_key, (MICRO, device_count, ATOMS_DEV), SLOTS // 2, SLOTS + 1)
    chosen_row = jax.random.randint(chosen_key, (MICRO, device_count, 1), 0, ATOMS_DEV)
    row_index = lax.broadcasted_iota(jnp.int32, (MICRO, device_count, ATOMS_DEV), 2)
    filled = jnp.where(row_index == chosen_row, SLOTS, base_counts)
    return filled.reshape(MICRO, ATOMS).astype(jnp.int32)


def levels(own_key, shape, shards, low, largest):
    def one(dim, shards_of):
        draws = jax.random.uniform(jax.random.fold_in(jax.random.fold_in(own_key, 6), dim), (shards_of,), jnp.float32, low / len(shards), largest / len(shards))
        return jnp.repeat(jnp.exp(draws), shape[dim] // shards_of).reshape((-1,) + (1,) * (len(shape) - dim - 1))

    loudness = one(*shards[0])
    for cut in shards[1:]:
        loudness = loudness * one(*cut)
    return loudness


def centred(stream_key, shape, width, limit, shards=(), kind=jnp.bfloat16):
    drawn = jax.random.normal(stream_key, shape, jnp.float32) * width
    if len(shards) > 0:
        drawn = levels(stream_key, shape, shards, -0.22, 0.18) * drawn
    return jnp.clip(drawn, min=-limit, max=limit).astype(kind)


def setup_inputs(seed: int = 0) -> dict:
    splits = jax.random.split(jax.random.key(seed), 19)
    return {
        "features": centred(splits[0], (MICRO, ATOMS, D), 1.0, 6.0, ((1, 32),)),
        "charges": centred(splits[1], (MICRO, CHANNELS, ATOMS), 0.5, 3.0, ((2, 32),), jnp.float32),
        "elements": draw_elements(jax.random.fold_in(splits[18], 71), 0),
        "neighbours": draw_neighbours(jax.random.fold_in(splits[18], 71), 0),
        "counts": draw_counts(jax.random.fold_in(splits[18], 71), 0),
        "distances": jnp.clip(0.8 + 4.1 * jax.random.uniform(splits[5], (MICRO, SLOTS, ATOMS), jnp.float32) ** levels(splits[5], (MICRO, SLOTS, ATOMS), ((2, 32),), -0.2, 0.2), 0.8, 4.9),
        "radial": centred(splits[6], (LAYERS, SHELLS, D), SLOTS ** -0.5, 1.0, (), jnp.float32),
        "radial_mom": centred(splits[7], (LAYERS, SHELLS, D), (0.1 * (MICRO * ATOMS * SLOTS) ** 0.5), 512.0, (), jnp.float32),
        "mixing": centred(splits[8], (LAYERS, CHANNELS, D), 0.3, 4.0, (), jnp.float32),
        "mixing_mom": centred(splits[9], (LAYERS, CHANNELS, D), (0.1 * (MICRO * ATOMS) ** 0.5), 96.0, (), jnp.float32),
        "w_in": centred(splits[10], (LAYERS, ELEMS, IN, HID), IN ** -0.5, 0.25, ((1, 4),), jnp.float32),
        "w_mid": centred(splits[11], (LAYERS, ELEMS, HID, HID), HID ** -0.5, 0.3125, ((1, 4),), jnp.float32),
        "w_out": centred(splits[12], (LAYERS, ELEMS, HID, D), (HID // 4) ** -0.5, 0.625, ((1, 4),), jnp.float32),
        "mom_in": centred(splits[13], (LAYERS, ELEMS, IN, HID), (0.4 * (MICRO * ATOMS // ELEMS) ** 0.5), 128.0, ((1, 4),), jnp.float32),
        "mom_mid": centred(splits[14], (LAYERS, ELEMS, HID, HID), (0.4 * (MICRO * ATOMS // ELEMS) ** 0.5), 128.0, ((1, 4),), jnp.float32),
        "mom_out": centred(splits[15], (LAYERS, ELEMS, HID, D), (0.5 * (MICRO * ATOMS // ELEMS) ** 0.5), 160.0, ((1, 4),), jnp.float32),
        "cot_features": centred(splits[16], (MICRO, ATOMS, D), 1.0, 6.0, ((1, 32),)),
        "cot_charges": centred(splits[17], (MICRO, CHANNELS, ATOMS), 1.0, 6.0, ((2, 32),), jnp.float32),
    }


PRECISE = lax.Precision.HIGHEST
SHELL_START = 0.8
SHELL_SPACING = 0.28
SHELL_SHARPNESS = 8.0
CUTOFF_RADIUS = 5.0
MOMENTUM = 0.5
LEARNING_RATE = 0.25
NEWTON_A = 3.4445
NEWTON_B = -4.775
NEWTON_C = 2.0315

@jax.custom_vjp
def low(v):
    return lax.optimization_barrier(v.astype(jnp.bfloat16)).astype(jnp.float32)

@jax.custom_vjp
def low_back(v):
    return v

def low_keep(v):
    return (low(v), None)

def low_pass(kept, grad):
    return (grad,)

def back_keep(v):
    return (v, None)

def back_low(kept, grad):
    return (low(grad),)
low.defvjp(low_keep, low_pass)
low_back.defvjp(back_keep, back_low)

def shell_basis(distance, live_count, shells):
    slot_index = lax.broadcasted_iota(jnp.int32, distance.shape, 0)
    live_mask = (slot_index < live_count[None, :]).astype(distance.dtype)
    envelope = 0.5 * (jnp.cos(math.pi * distance / CUTOFF_RADIUS) + 1.0) * live_mask
    centres = SHELL_START + SHELL_SPACING * jnp.arange(shells, dtype=distance.dtype)
    spread_out = distance[:, None, :] - centres[None, :, None]
    return jnp.exp(-SHELL_SHARPNESS * spread_out * spread_out) * envelope[:, None, :]

def orthogonal(matrix):
    row_count, col_count = (matrix.shape[-2], matrix.shape[-1])
    frobenius = jnp.sqrt(lax.optimization_barrier(jnp.sum(matrix * matrix, axis=(-2, -1), keepdims=True)))
    current = matrix / (frobenius + 1e-07)
    for newton_step in range(5):
        if row_count > col_count:
            gram_matrix = jnp.einsum('...ri,...rj->...ij', current, current, precision=PRECISE)
            polynomial = NEWTON_B * gram_matrix + NEWTON_C * jnp.einsum('...ij,...jk->...ik', gram_matrix, gram_matrix, precision=PRECISE)
            current = NEWTON_A * current + jnp.einsum('...ri,...ij->...rj', current, polynomial, precision=PRECISE)
        else:
            gram_matrix = jnp.einsum('...ir,...jr->...ij', current, current, precision=PRECISE)
            polynomial = NEWTON_B * gram_matrix + NEWTON_C * jnp.einsum('...ij,...jk->...ik', gram_matrix, gram_matrix, precision=PRECISE)
            current = NEWTON_A * current + jnp.einsum('...ij,...jr->...ir', polynomial, current, precision=PRECISE)
    return current

def muon_step(weight, moment, gradient):
    new_moment = MOMENTUM * moment + gradient
    row_count, col_count = (weight.shape[-2], weight.shape[-1])
    new_weight = weight - LEARNING_RATE * 0.2 * math.sqrt(max(row_count, col_count)) * orthogonal(new_moment)
    return (new_weight, new_moment)

def edge_block(source, radial_w, block):
    neighbour_ids, distance, live_count = block
    radial_basis = shell_basis(distance, live_count, SHELLS)
    nearby = jnp.take(source, neighbour_ids, axis=0)
    filters = jnp.einsum('ksi,sf->kif', radial_basis, radial_w, precision=PRECISE)
    return lax.optimization_barrier(jnp.sum(filters * nearby, axis=0))

def kind_step(mlp_rows, element_of, running, stacked):
    first_w, middle_w, last_w, kind_id = stacked
    first_pre = low_back(jnp.dot(mlp_rows, low(first_w), precision=PRECISE))
    act_one = low(jax.nn.gelu(first_pre))
    second_pre = low_back(jnp.dot(act_one, low(middle_w), precision=PRECISE))
    act_two = low(jax.nn.gelu(second_pre))
    result = jnp.dot(act_two, low(last_w), precision=PRECISE)
    return (running + jnp.where((element_of == kind_id)[:, None], result, 0.0), None)

def micro_batch(params, inputs):
    radial_all, mixing_all, first_all, middle_all, last_all = params
    hidden, charge, element_of, blocks = inputs
    kind_ids = jnp.arange(ELEMS, dtype=jnp.int32)
    for layer_index in range(LAYERS):
        source = low(hidden + jnp.einsum('ci,cf->if', charge, mixing_all[layer_index], precision=PRECISE))
        pieces = lax.map(jax.checkpoint(partial(edge_block, source, radial_all[layer_index])), blocks)
        message = pieces.reshape(ATOMS, D)
        mlp_rows = low_back(low(jnp.concatenate([hidden, message], axis=1)))
        kind_scan = jax.checkpoint(partial(kind_step, mlp_rows, element_of))
        summed, unused = lax.scan(kind_scan, jnp.zeros((ATOMS, D), jnp.float32), (first_all[layer_index], middle_all[layer_index], last_all[layer_index], kind_ids))
        update = low_back(low(summed))
        hidden = hidden + update
        charge = charge + update[:, :CHANNELS].T
    return (hidden, charge)

def reference(features, charges, elements, neighbours, counts, distances, radial, radial_mom, mixing, mixing_mom, w_in, w_mid, w_out, mom_in, mom_mid, mom_out, cot_features, cot_charges):
    block_count = ATOMS // ATOMS_DEV
    column = lax.broadcasted_iota(jnp.int32, neighbours.shape, 2)
    global_index = ((column - column % ATOMS_DEV + neighbours - HALO) % ATOMS).astype(jnp.int32)

    def by_device(values):
        return jnp.transpose(values.reshape(MICRO, SLOTS, block_count, ATOMS_DEV), (0, 2, 1, 3))
    blocks = (by_device(global_index), by_device(distances), counts.reshape(MICRO, block_count, ATOMS_DEV))

    def forward(features_f32, charges_in, radial_w, mixing_w, first_all, middle_all, last_all):
        params = (radial_w, mixing_w, first_all, middle_all, last_all)
        return lax.map(jax.checkpoint(partial(micro_batch, params)), (features_f32, charges_in, elements, blocks))
    outputs, pullback = jax.vjp(forward, features.astype(jnp.float32), charges, radial, mixing, w_in, w_mid, w_out)
    gradients = pullback((cot_features.astype(jnp.float32), cot_charges))
    grad_feat, grad_charge, grad_radial, grad_mixing, grad_first, grad_middle, grad_last = gradients
    new_first, new_first_mom = muon_step(w_in, mom_in, grad_first)
    new_middle, new_middle_mom = muon_step(w_mid, mom_mid, grad_middle)
    new_last, new_last_mom = muon_step(w_out, mom_out, grad_last)
    new_radial_w, new_radial_m = muon_step(radial, radial_mom, grad_radial)
    new_mixing_w, new_mixing_m = muon_step(mixing, mixing_mom, grad_mixing)
    return (outputs[0], outputs[1], grad_feat, grad_charge, new_first, new_middle, new_last, new_first_mom, new_middle_mom, new_last_mom, new_radial_w, new_radial_m, new_mixing_w, new_mixing_m)
```

```python
import functools
import math

import jax
import jax.numpy as jnp
from jax import lax
from jax.experimental import pallas as pl
from jax.experimental.pallas import tpu as pltpu
from jax.sharding import PartitionSpec as P

EXACT = lax.Precision.HIGHEST
SHELL_START = 0.8
SHELL_SPACING = 0.28
SHELL_SHARPNESS = 8.0
CUTOFF_RADIUS = 5.0
MOMENTUM = 0.5
LEARNING_RATE = 0.25
NEWTON_A = 3.4445
NEWTON_B = -4.775
NEWTON_C = 2.0315
NEWTON_CENTRES = (0.0, 0.0, 0.5, 1.0, 1.0)
QUARTERS = 4
GROUP = 8
SOURCES = 2
LANES = 128
FAR = 100.0
VMEM_BYTES = 60 * 1024 * 1024
F32 = jnp.float32
BF16 = jnp.bfloat16
NN = (((1,), (0,)), ((), ()))
NT = (((1,), (1,)), ((), ()))
TN = (((0,), (0,)), ((), ()))


def dot(left, right, dims, precision=None):
    return lax.dot_general(left, right, dims, precision=precision, preferred_element_type=F32)


def iota(shape, dim):
    return lax.broadcasted_iota(jnp.int32, shape, dim)


def round_up(size, multiple):
    return -(-size // multiple) * multiple


def params():
    return pltpu.CompilerParams(vmem_limit_bytes=VMEM_BYTES)


def cost(flops, read_bytes):
    return pl.CostEstimate(flops=int(flops), bytes_accessed=int(read_bytes), transcendentals=0)


def shape_of(shape, dtype):
    return jax.ShapeDtypeStruct(shape, dtype)


def at_step(shape, axis):
    block = tuple(1 if dim == axis else size for dim, size in enumerate(shape))
    return pl.BlockSpec(block, lambda step: tuple(step if dim == axis else 0 for dim in range(len(shape))))


def whole(shape):
    return pl.BlockSpec(shape, lambda *step: (0,) * len(shape))


def columns(rows):
    count, atoms = rows.shape
    return jnp.concatenate([rows, jnp.zeros((LANES - count, atoms), F32)], axis=0).T


def eight_rows(rows):
    return jnp.concatenate([rows, jnp.zeros((8 - rows.shape[0], rows.shape[1]), F32)], axis=0)


def add_columns(values, first):
    return jnp.concatenate([values[:, :LANES] + first, values[:, LANES:]], axis=1)


def source_of(hidden, charge_cols, mixing, channels):
    for channel in range(channels):
        hidden = hidden + charge_cols[:, channel : channel + 1] * mixing[channel : channel + 1, :]
    return hidden.astype(BF16)


def store_source(source, source_ref, first_ref, last_ref):
    rim = first_ref.shape[1]
    source_ref[0] = source
    first_ref[0] = source[:rim]
    last_ref[0] = source[source.shape[0] - rim :]


def atom_spec(values, which=0):
    holders, _, _, cap, width = values.shape
    return pl.BlockSpec((holders, 1, 1, cap, width), lambda step: (0, which, step, 0, 0))


def start_kernel(
    sizes, elem_ref, feat_ref, charge_ref, cotf_ref, cotc_ref, mixing_ref,
    place_ref, place_t_ref, packed_ref, source_ref, first_ref, last_ref,
):
    owners, per_owner, cap = sizes
    slots, atoms = place_ref.shape[1:]
    channels = charge_ref.shape[1]
    row = elem_ref[pl.ds(pl.program_id(0), 1), :]
    before = iota((atoms, atoms), 0)
    after = iota((atoms, atoms), 1)
    hot = (iota((LANES, atoms), 0) == row).astype(F32)
    rank = dot(hot.astype(BF16), (before < after).astype(F32).astype(BF16), NN)
    rank = jnp.sum(rank * hot, axis=0, keepdims=True)
    holder = lax.rem(row, per_owner) * owners + lax.div(row, per_owner)
    slot = holder.astype(F32) * cap + rank
    place = (iota((slots, atoms), 0) == slot.astype(jnp.int32)).astype(F32).astype(BF16)
    slot_t = jnp.broadcast_to(slot, (LANES, atoms)).T[:, :1].astype(jnp.int32)
    place_t = (iota((atoms, slots), 1) == slot_t).astype(F32).astype(BF16)
    place_ref[0] = place
    place_t_ref[0] = place_t
    features = feat_ref[0]
    grad = add_columns(cotf_ref[0].astype(F32), columns(cotc_ref[0])).astype(BF16)
    holders, _, _, _, width = packed_ref.shape
    for which, values in enumerate((features, grad)):
        packed = dot(place, values, NN).astype(BF16)
        packed_ref[:, which] = packed.reshape(holders, 1, cap, width)
    store_source(
        source_of(features.astype(F32), columns(charge_ref[0]), mixing_ref[0], channels),
        source_ref, first_ref, last_ref,
    )


def start(elements, features, charges, cot_features, cot_charges, mixing, rim, sizes):
    batches, atoms, width = features.shape
    owners, per_owner, cap = sizes
    holders = owners * per_owner
    packed_shape = (holders, 2, batches, cap, width)
    args = (elements, features, charges, cot_features, cot_charges, mixing)
    outs = (
        shape_of((batches, holders * cap, atoms), BF16),
        shape_of((batches, atoms, holders * cap), BF16),
        shape_of(packed_shape, BF16),
        shape_of((batches, atoms, width), BF16),
        shape_of((batches, rim, width), BF16),
        shape_of((batches, rim, width), BF16),
    )
    return pl.pallas_call(
        functools.partial(start_kernel, sizes),
        grid=(batches,),
        in_specs=[whole(elements.shape)]
        + [at_step(arg.shape, 0) for arg in args[1:-1]]
        + [whole(mixing.shape)],
        out_specs=[
            at_step(outs[0].shape, 0),
            at_step(outs[1].shape, 0),
            at_step(packed_shape, 2),
        ]
        + [at_step(out.shape, 0) for out in outs[3:]],
        out_shape=outs,
        compiler_params=params(),
        cost_estimate=cost(6e8, 8e6),
        name="start",
    )(*args)


def bands_kernel(shells, dist_ref, near_ref, band_ref, band_t_ref):
    groups, pairs = dist_ref.shape[1:]
    slots = pairs // GROUP
    per_quarter = groups // QUARTERS
    window = band_ref.shape[2]
    rows = shells * GROUP
    sub = iota((GROUP, pairs), 0)
    lane = iota((GROUP, pairs), 1)
    own = ((lane >= sub * slots) & (lane < (sub + 1) * slots)).astype(F32)
    centres = SHELL_START + SHELL_SPACING * iota((shells, 1), 0).astype(F32)
    target = iota((window, pairs), 0)
    distance_all = dist_ref[0]
    envelope_all = 0.5 * (jnp.cos(math.pi * distance_all / CUTOFF_RADIUS) + 1.0)
    for group in range(groups):
        distance = distance_all[group : group + 1]
        spread = distance - centres
        basis = jnp.exp(-SHELL_SHARPNESS * spread * spread) * envelope_all[group : group + 1]
        spaced = (basis[:, None, :] * own[None]).reshape(rows, pairs).astype(BF16)
        hot = (target == near_ref[0, group : group + 1, :]).astype(F32).astype(BF16)
        band_ref[0, group * rows : (group + 1) * rows, :] = dot(spaced, hot, NT).astype(BF16)
        quarter, inner = group // per_quarter, group % per_quarter
        band_t_ref[0, quarter, :, inner * rows : (inner + 1) * rows] = dot(hot, spaced, NT).astype(BF16)


def make_bands(distances, neighbours, counts, shells, rim):
    batches, slots, atoms = distances.shape
    groups = atoms // GROUP
    block = atoms // QUARTERS
    window = block + 2 * rim
    live = iota(distances.shape, 1) < counts[:, None, :]
    distance = jnp.where(live, distances, FAR)
    local = neighbours - (iota(neighbours.shape, 2) // block) * block

    def grouped(values):
        return jnp.transpose(values, (0, 2, 1)).reshape(batches, groups, GROUP * slots)

    args = (grouped(distance), grouped(local))
    rows = shells * GROUP
    outs = (
        shape_of((batches, groups * rows, window), BF16),
        shape_of((batches, QUARTERS, window, groups // QUARTERS * rows), BF16),
    )
    return pl.pallas_call(
        functools.partial(bands_kernel, shells),
        grid=(batches,),
        in_specs=[at_step(arg.shape, 0) for arg in args],
        out_specs=[at_step(out.shape, 0) for out in outs],
        out_shape=outs,
        compiler_params=params(),
        cost_estimate=cost(3e9, 8e6),
        name="bands",
    )(*args)


def edge_forward_kernel(source_ref, left_ref, right_ref, band_ref, radial_ref, place_ref, packed_ref):
    atoms, width = source_ref.shape[1:]
    shells = radial_ref.shape[1]
    rim = left_ref.shape[1]
    block = atoms // QUARTERS
    window = block + 2 * rim
    per_quarter = block // GROUP
    extended = jnp.concatenate([left_ref[0], source_ref[0], right_ref[0]], axis=0)
    radial = jnp.broadcast_to(radial_ref[0][:, None, :], (shells, GROUP, width))
    rows = block * shells
    pieces = []
    for quarter in range(QUARTERS):
        near = extended[quarter * block : quarter * block + window]
        sums = dot(band_ref[0, quarter * rows : (quarter + 1) * rows, :], near, NN)
        sums = sums.reshape(per_quarter, shells, GROUP, width) * radial[None]
        pieces.append(jnp.sum(sums, axis=1).reshape(block, width))
    message = jnp.concatenate(pieces, axis=0).astype(BF16)
    packed = dot(place_ref[0], message, NN).astype(BF16)
    packed_ref[...] = packed.reshape(packed_ref.shape)


def edge_forward(source, left, right, band, radial, layer, place, sizes):
    batches, atoms, width = source.shape
    owners, per_owner, cap = sizes
    packed_shape = (owners * per_owner, 1, batches, cap, width)
    return pl.pallas_call(
        edge_forward_kernel,
        grid=(batches,),
        in_specs=[at_step(arg.shape, 0) for arg in (source, left, right, band)]
        + [pl.BlockSpec((1,) + radial.shape[1:], lambda step: (layer, 0, 0)), at_step(place.shape, 0)],
        out_specs=at_step(packed_shape, 2),
        out_shape=shape_of(packed_shape, BF16),
        compiler_params=params(),
        cost_estimate=cost(1.2e9, 6e6),
        name="edge_forward",
    )(source, left, right, band, radial, place)


def edge_backward_kernel(
    grad_ref, place_t_ref, source_ref, left_ref, right_ref, band_ref, band_t_ref, radial_ref,
    inner_ref, to_left_ref, to_right_ref, radial_grad_ref, total,
):
    atoms, width = source_ref.shape[1:]
    shells = radial_ref.shape[1]
    rim = left_ref.shape[1]
    block = atoms // QUARTERS
    window = block + 2 * rim
    per_quarter = block // GROUP
    rows = block * shells
    step = pl.program_id(0)
    slots = place_t_ref.shape[2]
    grad = dot(place_t_ref[0], grad_ref[...].reshape(slots, width), NN)
    extended = jnp.concatenate([left_ref[0], source_ref[0], right_ref[0]], axis=0)
    radial = jnp.broadcast_to(radial_ref[0][:, None, :], (shells, GROUP, width))
    total[...] = jnp.zeros_like(total)
    radial_sum = jnp.zeros((shells, GROUP, width), F32)
    for quarter in range(QUARTERS):
        near = extended[quarter * block : quarter * block + window]
        sums = dot(band_ref[0, quarter * rows : (quarter + 1) * rows, :], near, NN)
        piece = grad[quarter * block : (quarter + 1) * block].reshape(per_quarter, 1, GROUP, width)
        radial_sum = radial_sum + jnp.sum(
            sums.reshape(per_quarter, shells, GROUP, width) * piece, axis=0
        )
        scaled = (radial[None] * piece).reshape(rows, width).astype(BF16)
        total[quarter * block : quarter * block + window] += dot(band_t_ref[0, quarter], scaled, NN)
    inner_ref[0] = total[rim : rim + atoms]
    to_left_ref[0] = total[:rim].astype(BF16)
    to_right_ref[0] = total[rim + atoms :].astype(BF16)
    radial_here = jnp.sum(radial_sum, axis=1)

    @pl.when(step == 0)
    def _():
        radial_grad_ref[...] = radial_here

    @pl.when(step > 0)
    def _():
        radial_grad_ref[...] += radial_here


def edge_backward(grad, place_t, source, left, right, band, band_t, radial, layer):
    batches, atoms, width = source.shape
    rim = left.shape[1]
    shells = radial.shape[1]
    outs = (
        shape_of((batches, atoms, width), F32),
        shape_of(left.shape, BF16),
        shape_of(left.shape, BF16),
        shape_of((shells, width), F32),
    )
    return pl.pallas_call(
        edge_backward_kernel,
        grid=(batches,),
        in_specs=[atom_spec(grad), at_step(place_t.shape, 0)]
        + [at_step(arg.shape, 0) for arg in (source, left, right, band, band_t)]
        + [pl.BlockSpec((1,) + radial.shape[1:], lambda step: (layer, 0, 0))],
        out_specs=[at_step(out.shape, 0) for out in outs[:3]] + [whole(outs[3].shape)],
        out_shape=outs,
        scratch_shapes=[pltpu.VMEM((atoms + 2 * rim, width), F32)],
        compiler_params=params(),
        cost_estimate=cost(2.5e9, 10e6),
        name="edge_backward",
    )(grad, place_t, source, left, right, band, band_t, radial)


def update_kernel(back_ref, place_t_ref, hidden_ref, charge_ref, *rest):
    mixing_ref, hidden_out_ref, charge_out_ref, *sources = rest if len(rest) > 2 else (None, *rest)
    slots, width = place_t_ref.shape[2], hidden_ref.shape[2]
    channels = charge_ref.shape[1]
    update = dot(place_t_ref[0], back_ref[...].reshape(slots, width), NN)
    hidden = hidden_ref[0].astype(F32) + update
    charge = charge_ref[0] + update[:, :LANES].T[:channels]
    hidden_out_ref[0] = hidden
    charge_out_ref[0] = charge
    if sources:
        store_source(source_of(hidden, columns(charge), mixing_ref[0], channels), *sources)


def update_atoms(back, which, place_t, hidden, charge, mixing=None, layer=0, rim=0):
    batches, atoms, width = hidden.shape
    outs = [shape_of((batches, atoms, width), F32), shape_of(charge.shape, F32)]
    args = [back, place_t, hidden, charge]
    specs = [atom_spec(back, which)] + [at_step(arg.shape, 0) for arg in args[1:]]
    if mixing is not None:
        args.append(mixing)
        specs.append(pl.BlockSpec((1,) + mixing.shape[1:], lambda step: (layer, 0, 0)))
        outs += [shape_of((batches, rows, width), BF16) for rows in (atoms, rim, rim)]
    return pl.pallas_call(
        update_kernel,
        grid=(batches,),
        in_specs=specs,
        out_specs=[at_step(out.shape, 0) for out in outs],
        out_shape=outs,
        compiler_params=params(),
        cost_estimate=cost(2e8, 4e6),
        name="update_atoms",
    )(*args)


def finish_kernel(
    repack, inner_ref, from_left_ref, from_right_ref, back_ref, place_t_ref, grad_ref, grad_charge_ref,
    charge_ref, mixing_ref, radial_grad_ref, *rest,
):
    if repack:
        place_ref, grad_out_ref, charge_out_ref, small_ref, packed_ref = rest
    else:
        earlier_ref, late_ref, hidden_ref, late_charge_ref, *rest = rest
        grad_out_ref, charge_out_ref, copies_ref, hidden_out_ref, late_charge_out_ref, small_ref = rest
    atoms, width = inner_ref.shape[1:]
    rim = from_left_ref.shape[1]
    channels = charge_ref.shape[1]
    slots = place_t_ref.shape[2]
    shells = radial_grad_ref.shape[0]
    step = pl.program_id(0)
    inner = inner_ref[0]
    source_grad = jnp.concatenate(
        [
            inner[:rim] + from_left_ref[0].astype(F32),
            inner[rim : atoms - rim],
            inner[atoms - rim :] + from_right_ref[0].astype(F32),
        ],
        axis=0,
    )
    mixing_grad = dot(eight_rows(charge_ref[0]), source_grad, NN, EXACT)
    charge_term = dot(eight_rows(mixing_ref[0]), source_grad, NT, EXACT)
    joined = dot(place_t_ref[0], back_ref[...].reshape(slots, width), NN)
    grad = grad_ref[0].astype(F32) + joined + source_grad
    grad_charge = grad_charge_ref[0] + charge_term[:channels]
    grad_out_ref[0] = grad
    charge_out_ref[0] = grad_charge

    @pl.when(step == 0)
    def _():
        small_ref[:shells] = radial_grad_ref[...]
        small_ref[shells:] = mixing_grad

    @pl.when(step > 0)
    def _():
        small_ref[shells:] += mixing_grad

    if not repack:
        update = dot(place_t_ref[0], late_ref[...].reshape(slots, width), NN)
        hidden_out_ref[0] = hidden_ref[0] + update
        late_charge_out_ref[0] = late_charge_ref[0] + update[:, :LANES].T[:channels]

        @pl.when(step == pl.num_programs(0) - 1)
        def _():
            joined = jnp.concatenate([small_ref[...], earlier_ref[...]], axis=0).astype(BF16)
            for copy in range(copies_ref.shape[0]):
                copies_ref[copy] = joined

    else:
        sent = add_columns(grad, columns(grad_charge)).astype(BF16)
        packed = dot(place_ref[0], sent, NN).astype(BF16)
        packed_ref[...] = packed.reshape(packed_ref.shape)


def finish(inner, from_left, from_right, back, place_t, grad, grad_charge, charge, mixing, layer, radial_grad, place=None, last=None):
    batches, atoms, width = inner.shape
    args = [inner, from_left, from_right, back, place_t, grad, grad_charge, charge, mixing, radial_grad]
    specs = [at_step(arg.shape, 0) for arg in args]
    specs[3] = atom_spec(back)
    specs[8] = pl.BlockSpec((1,) + mixing.shape[1:], lambda step: (layer, 0, 0))
    specs[9] = whole(radial_grad.shape)
    small = (radial_grad.shape[0] + 8, width)
    outs = [shape_of(inner.shape, F32), shape_of(charge.shape, F32), shape_of(small, F32)]
    out_specs = [at_step(outs[0].shape, 0), at_step(outs[1].shape, 0), whole(small)]
    scratch = []
    if place is None:
        earlier, hidden, late_charge = last
        args += [earlier, back, hidden, late_charge]
        specs += [whole(earlier.shape), atom_spec(back, 1), at_step(hidden.shape, 0), at_step(charge.shape, 0)]
        copies = (back.shape[0], small[0] + earlier.shape[0], width)
        outs[2], out_specs[2] = shape_of(copies, BF16), whole(copies)
        outs += outs[:2]
        out_specs += out_specs[:2]
        scratch.append(pltpu.VMEM(small, F32))
    else:
        args.append(place)
        specs.append(at_step(place.shape, 0))
        outs.append(shape_of(back.shape[:1] + (1,) + back.shape[2:], BF16))
        out_specs.append(atom_spec(back))
    return pl.pallas_call(
        functools.partial(finish_kernel, place is not None),
        grid=(batches,),
        in_specs=specs,
        out_specs=out_specs,
        out_shape=outs,
        scratch_shapes=scratch,
        compiler_params=params(),
        cost_estimate=cost(6e8, 6e6),
        name="finish",
    )(*args)


def gelu_parts(value):
    scale = math.sqrt(2.0 / math.pi)
    square = value * value
    bent = jnp.tanh(scale * (value + 0.044715 * value * square))
    half = 0.5 * (1.0 + bent)
    slope = half + 0.5 * value * (1.0 - bent * bent) * scale * (1.0 + 3.0 * 0.044715 * square)
    return value * half, slope


def rows_spec(values, which=0, sources=SOURCES):
    _, _, rows, width = values.shape
    return pl.BlockSpec((sources, 1, rows, width), lambda step: (step, which, 0, 0))


def saved_spec(shape, steps):
    return pl.BlockSpec((shape[0] // steps, shape[1]), lambda step: (step, 0))


def weight_specs(weights, layer):
    return [pl.BlockSpec((1,) + w.shape[1:], lambda step: (layer, 0, 0)) for w in weights]


def forward_through(hidden, message, first_ref, middle_ref, last_ref):
    width = hidden.shape[1]
    pre_one = dot(hidden, first_ref[0, :, :width], NT) + dot(message, first_ref[0, :, width:], NT)
    act_one = gelu_parts(pre_one)[0].astype(BF16)
    pre_two = dot(act_one, middle_ref[0], NN)
    act_two = gelu_parts(pre_two)[0].astype(BF16)
    return dot(act_two, last_ref[0], NN).astype(BF16), pre_one, pre_two


def back_through(grad, pre_one, pre_two, first_ref, middle_ref, last_ref, span, outs):
    width = grad.shape[1]
    act_one_ref, act_two_ref, grad_one_ref, grad_two_ref = outs
    act_one, slope_one = gelu_parts(pre_one)
    act_two, slope_two = gelu_parts(pre_two)
    act_one_ref[span] = act_one.astype(BF16)
    act_two_ref[span] = act_two.astype(BF16)
    grad_two = (slope_two * dot(grad, last_ref[0], NT)).astype(BF16)
    grad_two_ref[span] = grad_two
    grad_one = (slope_one * dot(grad_two, middle_ref[0], NT)).astype(BF16)
    grad_one_ref[span] = grad_one
    return (
        dot(grad_one, first_ref[0, :, :width], NN).astype(BF16),
        dot(grad_one, first_ref[0, :, width:], NN).astype(BF16),
    )


def network_forward_kernel(
    feat_ref, message_ref, first_ref, middle_ref, last_ref, result_ref, pre_one_ref, pre_two_ref
):
    sources, _, rows, _ = feat_ref.shape
    for source in range(sources):
        span = slice(source * rows, (source + 1) * rows)
        result_ref[source, 0], pre_one_ref[span], pre_two_ref[span] = forward_through(
            feat_ref[source, 0], message_ref[source, 0], first_ref, middle_ref, last_ref
        )


def network_forward(arrived, message, weights, layer):
    holders, _, rows, width = message.shape
    steps = holders // SOURCES
    saved = (holders * rows, weights[1].shape[1])
    return pl.pallas_call(
        network_forward_kernel,
        grid=(steps,),
        in_specs=[rows_spec(arrived), rows_spec(message)] + weight_specs(weights, layer),
        out_specs=[rows_spec(message)] + [saved_spec(saved, steps)] * 2,
        out_shape=(shape_of(message.shape, BF16), shape_of(saved, F32), shape_of(saved, F32)),
        compiler_params=params(),
        cost_estimate=cost(1.4e9, 8e6),
        name="network_forward",
    )(arrived, message, *weights)


def network_turn_kernel(
    feat_ref, result_ref, message_ref, grad_ref, first_ref, middle_ref, last_ref,
    result_out_ref, rows_ref, grad_hidden_ref, grad_message_ref, *saved,
):
    sources, _, rows, _ = feat_ref.shape
    for source in range(sources):
        span = slice(source * rows, (source + 1) * rows)
        hidden = feat_ref[source, 0].astype(F32) + result_ref[source, 0].astype(F32)
        hidden = hidden.astype(BF16)
        rows_ref[source, 0] = hidden
        result_out_ref[source, 0], pre_one, pre_two = forward_through(
            hidden, message_ref[source, 0], first_ref, middle_ref, last_ref
        )
        grad_hidden_ref[source, 0], grad_message_ref[source, 0] = back_through(
            grad_ref[source, 0], pre_one, pre_two, first_ref, middle_ref, last_ref, span, saved
        )


def network_turn(arrived, result, message, weights, layer):
    holders, _, rows, width = message.shape
    steps = holders // SOURCES
    saved = (holders * rows, weights[1].shape[1])
    spec = rows_spec(message)
    return pl.pallas_call(
        network_turn_kernel,
        grid=(steps,),
        in_specs=[rows_spec(arrived), spec, spec, rows_spec(arrived, 1)] + weight_specs(weights, layer),
        out_specs=[spec] * 4 + [saved_spec(saved, steps)] * 4,
        out_shape=[shape_of(message.shape, BF16)] * 4 + [shape_of(saved, BF16)] * 4,
        compiler_params=params(),
        cost_estimate=cost(2.8e9, 12e6),
        name="network_turn",
    )(arrived, result, message, arrived, *weights)


def network_backward_kernel(
    grad_ref, pre_one_ref, pre_two_ref, late_ref, first_ref, middle_ref, last_ref,
    grad_message_ref, both_ref, *saved,
):
    sources, _, rows, _ = grad_ref.shape
    both_ref[:, 1] = late_ref[:, 0]
    for source in range(sources):
        span = slice(source * rows, (source + 1) * rows)
        both_ref[source, 0], grad_message_ref[source, 0] = back_through(
            grad_ref[source, 0], pre_one_ref[span], pre_two_ref[span],
            first_ref, middle_ref, last_ref, span, saved,
        )


def network_backward(grad, pre_one, pre_two, late, weights, layer):
    holders, _, rows, width = grad.shape
    steps = holders // SOURCES
    saved = pre_one.shape
    spec = rows_spec(grad)
    both = pl.BlockSpec((SOURCES, 2, rows, width), lambda step: (step, 0, 0, 0))
    return pl.pallas_call(
        network_backward_kernel,
        grid=(steps,),
        in_specs=[spec] + [saved_spec(saved, steps)] * 2 + [spec] + weight_specs(weights, layer),
        out_specs=[spec, both] + [saved_spec(saved, steps)] * 4,
        out_shape=[shape_of(grad.shape, BF16), shape_of((holders, 2, rows, width), BF16)]
        + [shape_of(saved, BF16)] * 4,
        compiler_params=params(),
        cost_estimate=cost(1.4e9, 12e6),
        name="network_backward",
    )(grad, pre_one, pre_two, late, *weights)


def flat_blocks(width, hidden_width):
    return 2 * width // LANES, hidden_width // LANES, width // LANES


def flat_blocks_of(flat_rows, padded):
    width_blocks = (flat_rows // padded - padded // LANES) // 3
    return 2 * width_blocks, padded // LANES, width_blocks


def store_blocks(ref, base, values):
    rows = values.shape[0]
    for block in range(values.shape[1] // LANES):
        ref[(base + block) * rows : (base + block + 1) * rows, :] = values[
            :, block * LANES : (block + 1) * LANES
        ].astype(ref.dtype)


def weight_grad_kernel(
    pieces, place_ref, hidden_ref, message_ref, grad_ref, act_one_ref, act_two_ref, grad_one_ref, grad_two_ref, *rest
):
    *out_refs, first_sum, middle_sum, last_sum, flat = rest
    sources, _, rows, width = hidden_ref.shape
    count = sources * rows
    step = pl.program_id(0)
    grad_one = grad_one_ref[...]
    parts = (
        (first_sum.at[:, :width], dot(grad_one, hidden_ref[...].reshape(count, width), TN)),
        (first_sum.at[:, width:], dot(grad_one, message_ref[...].reshape(count, width), TN)),
        (middle_sum, dot(act_one_ref[...], grad_two_ref[...], TN)),
        (last_sum, dot(act_two_ref[...], grad_ref[...].reshape(count, width), TN)),
    )

    @pl.when(step == 0)
    def _():
        for total, part in parts:
            total[...] = part

    @pl.when(step > 0)
    def _():
        for total, part in parts:
            total[...] += part

    @pl.when(step == pl.num_programs(0) - 1)
    def _():
        base = 0
        for total in (first_sum, middle_sum, last_sum):
            store_blocks(flat, base, total[...])
            base += total.shape[1] // LANES
        live = base * first_sum.shape[0]
        if flat.shape[0] > live:
            flat[live:] = jnp.zeros((flat.shape[0] - live, LANES), F32)
        here = place_ref[0]
        if not pieces:
            (out_ref,) = out_refs
            for owned in range(out_ref.shape[0]):
                out_ref[owned] = jnp.where(owned == here, flat[...], 0.0).astype(BF16)
        for shift, piece_ref in enumerate(out_refs if pieces else ()):
            rows_each = piece_ref.shape[0]
            target = lax.rem(here + shift, pieces)
            piece_ref[...] = flat[pl.ds(pl.multiple_of(target * rows_each, 16), rows_each), :].astype(BF16)


def weight_grad(place, hidden, message, grad, which, saved, shape, pieces=0):
    holders, _, rows, width = message.shape
    hidden_width = saved[0].shape[1]
    steps = 2
    sources = holders // steps

    def rows_of(values, kind):
        return pl.BlockSpec(
            (sources, 1) + values.shape[2:], lambda step, place: (step, kind, 0, 0)
        )

    saved_rows = pl.BlockSpec((saved[0].shape[0] // steps, hidden_width), lambda step, place: (step, 0))
    flat_rows = shape[-2] * max(pieces, 1)
    return pl.pallas_call(
        functools.partial(weight_grad_kernel, pieces),
        grid_spec=pltpu.PrefetchScalarGridSpec(
            num_scalar_prefetch=1,
            grid=(steps,),
            in_specs=[rows_of(hidden, 0), rows_of(message, 0), rows_of(grad, which)] + [saved_rows] * 4,
            out_specs=[whole(shape)] * max(pieces, 1),
            scratch_shapes=[
                pltpu.VMEM((hidden_width, cols), F32) for cols in (2 * width, hidden_width, width)
            ]
            + [pltpu.VMEM((flat_rows, LANES), F32)],
        ),
        out_shape=[shape_of(shape, BF16)] * max(pieces, 1),
        compiler_params=params(),
        cost_estimate=cost(1.4e9, 8e6),
        name="weight_grad",
    )(place, hidden, message, grad, *saved)


def newton_step(current, tall, centre, eye_ref):
    high = current.astype(BF16)
    rest = dot(high, high, TN if tall else NT)
    if centre:
        size = rest.shape[0]
        rest = rest - centre * eye_ref[:size, :size]
    rest_low = rest.astype(BF16)
    linear = NEWTON_B + 2.0 * NEWTON_C * centre
    poly = (linear * rest + NEWTON_C * dot(rest_low, rest_low, NN)).astype(BF16)
    step = dot(high, poly, NN) if tall else dot(poly, high, NN)
    return (NEWTON_A + NEWTON_B * centre + NEWTON_C * centre * centre) * current + step


def unit(moment):
    return moment / (jnp.sqrt(jnp.sum(moment * moment)) + 1e-07)


def native(values, which, fill=True):
    cols = values.shape[2 if which == 0 else 3]
    padded = LANES * (1 << (round_up(cols, LANES) // LANES - 1).bit_length())
    if padded > cols and fill:
        values = jnp.pad(values, ((0, 0), (0, 0), (0, 0), (0, padded - cols)))
    values = jnp.transpose(values, (0, 3, 1, 2) if which == 0 else (0, 2, 1, 3))
    if padded > cols and not fill:
        return values
    layers, rows, per_owner, _ = values.shape
    values = values.reshape(layers, rows, per_owner, padded // LANES, LANES)
    return jnp.transpose(values, (0, 1, 3, 2, 4)).reshape(layers, -1, LANES)


def from_native(values, which, per_owner, rows):
    if values.ndim == 3:
        layers = values.shape[0]
        values = values.reshape(layers, rows, -1, per_owner, LANES)
        values = jnp.transpose(values, (0, 1, 3, 2, 4)).reshape(layers, rows, per_owner, -1)
    return jnp.transpose(values, (0, 2, 3, 1) if which == 0 else (0, 2, 1, 3))


class Lying:
    def __init__(self, ref, rows, per_owner, blocks):
        self.ref, self.rows, self.per_owner, self.blocks = ref, rows, per_owner, blocks
        self.spread = ref.shape[1] // rows if len(ref.shape) == 3 else 0

    def place(self, block, owned):
        if self.spread:
            return (0, pl.ds(block * self.per_owner + owned, self.rows, stride=self.spread), slice(None))
        return (0, slice(None), owned, slice(block * LANES, block * LANES + self.lanes(block)))

    def lanes(self, block):
        return LANES if self.spread else min(LANES, self.ref.shape[3] - block * LANES)

    def read(self, block, owned):
        return self.ref[self.place(block, owned)]

    def write(self, block, owned, value):
        self.ref[self.place(block, owned)] = value[:, : self.lanes(block)]


def lying(refs, rows, per_owner):
    blocks = [ref.shape[1] // rows // per_owner for ref in refs]
    blocks[1] = round_up(rows, LANES) // LANES
    return [Lying(ref, rows, per_owner, count) for ref, count in zip(refs, blocks)]


def half_kernel(rows, per_owner, *refs):
    moms, flat_ref = lying(refs[:3], rows, per_owner), refs[3]
    padded = round_up(rows, LANES)
    base = 0
    for mom in moms:
        for block in range(mom.blocks):
            begin = base * padded
            for owned in range(per_owner):
                flat_ref[owned, begin : begin + padded] = jnp.zeros((padded, LANES), F32)
                flat_ref[owned, begin : begin + rows, : mom.lanes(block)] = MOMENTUM * mom.read(block, owned)
            base += 1


def half_moments(moms, rows, per_owner, flat_rows):
    layers = moms[0].shape[0]
    return pl.pallas_call(
        functools.partial(half_kernel, rows, per_owner),
        grid=(layers,),
        in_specs=[at_step(mom.shape, 0) for mom in moms],
        out_specs=pl.BlockSpec((per_owner, flat_rows, LANES), lambda step: (step, 0, 0)),
        out_shape=shape_of((layers * per_owner, flat_rows, LANES), F32),
        compiler_params=params(),
        cost_estimate=cost(4e6, 14e6),
        name="half_moments",
    )(*moms)


def cast_kernel(rows, per_owner, mine_ref, *refs):
    olds, lows, scratches = lying(refs[:3], rows, per_owner), refs[3:6], refs[6:]
    for old, low, scratch in zip(olds, lows, scratches):
        scratch[rows:] = jnp.zeros((scratch.shape[0] - rows, scratch.shape[1]), F32)
        for block in range(old.blocks):
            scratch[:rows, block * LANES : (block + 1) * LANES] = old.read(block, mine_ref[0])
        low[0] = scratch[...].astype(BF16)


def cast_weights(mine, weights, rows, per_owner, width):
    layers = weights[0].shape[0]
    padded = round_up(rows, LANES)
    shapes = [(padded, blocks * LANES) for blocks in flat_blocks(width, padded)]
    layer_spec = lambda shape: pl.BlockSpec(
        (1,) + shape[1:], lambda step, mine: (step,) + (0,) * (len(shape) - 1)
    )
    return pl.pallas_call(
        functools.partial(cast_kernel, rows, per_owner),
        grid_spec=pltpu.PrefetchScalarGridSpec(
            num_scalar_prefetch=1,
            grid=(layers,),
            in_specs=[layer_spec(w.shape) for w in weights],
            out_specs=[layer_spec((layers,) + shape) for shape in shapes],
            scratch_shapes=[pltpu.VMEM(shape, F32) for shape in shapes],
        ),
        out_shape=[shape_of((layers,) + shape, BF16) for shape in shapes],
        compiler_params=params(),
        cost_estimate=cost(4e6, 11e6),
        name="cast_weights",
    )(mine, *weights)


def sum_kernel(*refs):
    total = refs[0][...].astype(F32)
    for ref in refs[1:-1]:
        total = total + ref[...].astype(F32)
    total = total.astype(BF16)
    for copy in range(refs[-1].shape[0]):
        refs[-1][copy] = total


def sum_arrays(parts, copies=1):
    shape = parts[0].shape
    return pl.pallas_call(
        sum_kernel,
        grid=(1,),
        in_specs=[whole(shape)] * len(parts),
        out_specs=whole((copies,) + shape),
        out_shape=shape_of((copies,) + shape, BF16),
        compiler_params=params(),
        cost_estimate=cost(1e6, 2e6),
        name="sum_arrays",
    )(*parts)


def sum_first_kernel(parts_ref, total_ref):
    total = parts_ref[0].astype(F32)
    for part in range(1, parts_ref.shape[0]):
        total = total + parts_ref[part].astype(F32)
    total_ref[...] = total.astype(BF16)


def sum_first(parts):
    return pl.pallas_call(
        sum_first_kernel,
        grid=(1,),
        in_specs=[whole(parts.shape)],
        out_specs=whole(parts.shape[1:]),
        out_shape=shape_of(parts.shape[1:], BF16),
        compiler_params=params(),
        cost_estimate=cost(1e6, 1e6),
        name="sum_first",
    )(parts)


def join_kernel(slab_ref, *refs):
    *parts, whole_ref = refs
    rows = parts[0].shape[0]
    for shift, part in enumerate(parts):
        origin = lax.rem(slab_ref[0] - shift + len(parts), len(parts))
        whole_ref[pl.ds(pl.multiple_of(origin * rows, 16), rows), :] = part[...]


def join(slab, parts):
    rows, lanes = parts[0].shape
    shape = (rows * len(parts), lanes)
    return pl.pallas_call(
        join_kernel,
        grid_spec=pltpu.PrefetchScalarGridSpec(
            num_scalar_prefetch=1,
            grid=(1,),
            in_specs=[whole((rows, lanes))] * len(parts),
            out_specs=whole(shape),
        ),
        out_shape=shape_of(shape, BF16),
        compiler_params=params(),
        cost_estimate=cost(1e6, 2e6),
        name="join",
    )(slab, *parts)


def muon_kernel(rows, task_ref, half_ref, grad_ref, step_ref, eye_ref):
    padded = round_up(rows, LANES)
    eye_ref[...] = (iota(eye_ref.shape, 0) == iota(eye_ref.shape, 1)).astype(F32)
    base = 0
    values = []
    blocks = flat_blocks_of(half_ref.shape[1], padded)
    for count in blocks:
        parts = []
        for block in range(base, base + count):
            span = slice(block * padded, (block + 1) * padded)
            parts.append(half_ref[0, span] + grad_ref[span].astype(F32))
        base += count
        values.append(unit(jnp.concatenate(parts, axis=1)))
    for centre in NEWTON_CENTRES:
        values = [newton_step(value, which == 2, centre, eye_ref) for which, value in enumerate(values)]
    base = 0
    for count, value in zip(blocks, values):
        longest = rows if count == padded // LANES else max(count * LANES, rows)
        store_blocks(step_ref, base, value * (LEARNING_RATE * 0.2 * math.sqrt(longest)))
        base += count


def layer_of(values, layer):
    return pl.BlockSpec(
        (1,) + values.shape[1:], lambda step, *scalars: (layer,) + (0,) * (values.ndim - 1)
    )


def muon_step(task, grads, halves, rows):
    block = (1,) + halves.shape[1:]
    padded = round_up(rows, LANES)
    return pl.pallas_call(
        functools.partial(muon_kernel, rows),
        grid_spec=pltpu.PrefetchScalarGridSpec(
            num_scalar_prefetch=1,
            grid=(1,),
            in_specs=[pl.BlockSpec(block, lambda step, task: (task[0], 0, 0)), whole(grads.shape)],
            out_specs=whole(block[1:]),
            scratch_shapes=[pltpu.VMEM((padded, padded), F32)],
        ),
        out_shape=shape_of(block[1:], BF16),
        compiler_params=params(),
        cost_estimate=cost(7e9, 4e6),
        name="muon",
    )(task, halves, grads)


def apply_kernel(rows, per_owner, mine_ref, half_ref, *refs):
    steps, grads, weights = refs[:2], refs[2:4], lying(refs[4:7], rows, per_owner)
    new_moms, new_weights = lying(refs[-6:-3], rows, per_owner), lying(refs[-3:], rows, per_owner)
    mine = mine_ref[0]
    padded = round_up(rows, LANES)
    base = 0
    for weight, new_mom, new_weight in zip(weights, new_moms, new_weights):
        for block in range(weight.blocks):
            span = slice(base * padded, base * padded + rows)
            both_grads = [ref[span].astype(F32) for ref in grads]
            both_steps = [ref[span].astype(F32) for ref in steps]
            for owned in range(per_owner):
                grad = jnp.where(mine == owned, *both_grads)
                step = jnp.where(mine == owned, *both_steps)
                new_mom.write(block, owned, half_ref[owned, span] + grad)
                new_weight.write(block, owned, weight.read(block, owned) - step)
            base += 1


def apply_layer(mine, grads, steps, halves, weights, news, layer, rows, per_owner, partial=None):
    args = [mine, halves, *steps, *grads, *weights]
    in_specs = [pl.BlockSpec((per_owner,) + halves.shape[1:], lambda step, mine: (layer, 0, 0))]
    in_specs += [whole(value.shape) for value in (*steps, *grads)]
    in_specs += [layer_of(weight, layer) for weight in weights]
    aliases = {}
    if partial is not None:
        aliases = {len(args) + which: which for which in range(len(news))}
        args += list(partial)
        in_specs += [pl.BlockSpec(memory_space=pl.ANY)] * len(news)
    return pl.pallas_call(
        functools.partial(apply_kernel, rows, per_owner),
        grid_spec=pltpu.PrefetchScalarGridSpec(
            num_scalar_prefetch=1,
            grid=(1,),
            in_specs=in_specs,
            out_specs=[layer_of(new, layer) for new in news],
        ),
        out_shape=[shape_of(new.shape, F32) for new in news],
        input_output_aliases=aliases,
        compiler_params=params(),
        cost_estimate=cost(2e6, 18e6),
        name="apply_layer",
    )(*args)


def small_kernel(count_parts, *refs):
    parts, refs = refs[:count_parts], refs[count_parts:]
    radial_ref, radial_mom_ref, mixing_ref, mixing_mom_ref, *outs = refs
    new_radial_ref, new_radial_mom_ref, new_mixing_ref, new_mixing_mom_ref = outs
    layers, shells, width = radial_ref.shape
    channels = mixing_ref.shape[1]
    values = []
    total = parts[0][...].astype(F32)
    for part in parts[1:]:
        total = total + part[...].astype(F32)
    each = total.shape[0] // layers
    for layer in range(layers):
        total_here = total[layer * each : (layer + 1) * each]
        moment = MOMENTUM * radial_mom_ref[layer] + total_here[:shells]
        new_radial_mom_ref[layer] = moment
        values.append(unit(moment))
        moment = eight_rows(MOMENTUM * mixing_mom_ref[layer]) + total_here[shells:]
        new_mixing_mom_ref[layer] = moment[:channels]
        values.append(unit(moment))
    for _ in NEWTON_CENTRES:
        grams = [dot(value, value, NT, EXACT) for value in values]
        polys = [NEWTON_B * gram + NEWTON_C * dot(gram, gram, NN, EXACT) for gram in grams]
        values = [NEWTON_A * value + dot(poly, value, NN, EXACT) for value, poly in zip(values, polys)]
    for layer in range(layers):
        lift = LEARNING_RATE * 0.2 * math.sqrt(max(shells, width))
        new_radial_ref[layer] = radial_ref[layer] - lift * values[2 * layer]
        lift = LEARNING_RATE * 0.2 * math.sqrt(max(channels, width))
        new_mixing_ref[layer] = mixing_ref[layer] - lift * values[2 * layer + 1][:channels]


def small_step(parts, radial, radial_mom, mixing, mixing_mom):
    args = (*parts, radial, radial_mom, mixing, mixing_mom)
    outs = [radial, radial_mom, mixing, mixing_mom]
    return pl.pallas_call(
        functools.partial(small_kernel, len(parts)),
        grid=(1,),
        in_specs=[whole(arg.shape) for arg in args],
        out_specs=[whole(out.shape) for out in outs],
        out_shape=[shape_of(out.shape, F32) for out in outs],
        compiler_params=params(),
        cost_estimate=cost(1e8, 3e6),
        name="small_step",
    )(*args)


EVERY = ("slab", "pair", "elem")
HOLDERS = ("pair", "elem")


def swap(values):
    return lax.all_to_all(values, HOLDERS, split_axis=0, concat_axis=0, tiled=True)


def to_both_sides(to_left, to_right):
    count = lax.axis_size(EVERY)
    up = [(i, (i + 1) % count) for i in range(count)]
    down = [((i + 1) % count, i) for i in range(count)]
    return lax.ppermute(to_right, EVERY, up), lax.ppermute(to_left, EVERY, down)


def other_of_pair(values):
    return lax.ppermute(values, "pair", [(0, 1), (1, 0)])


def shifted(values, shift):
    count = lax.axis_size("slab")
    return lax.ppermute(values, "slab", [(i, (i + shift) % count) for i in range(count)])


def exchange(pieces):
    return [piece if shift == 0 else shifted(piece, shift) for shift, piece in enumerate(pieces)]


def to_all_slabs(piece):
    return exchange([piece] * lax.axis_size("slab"))


def on_device(
    features,
    charges,
    elements,
    neighbours,
    counts,
    distances,
    radial,
    radial_mom,
    mixing,
    mixing_mom,
    w_in,
    w_mid,
    w_out,
    mom_in,
    mom_mid,
    mom_out,
    cot_features,
    cot_charges,
):
    batches, atoms, width = features.shape
    per_owner, hidden_width = w_in.shape[1], w_in.shape[3]
    owners = lax.axis_size("elem")
    shells = radial.shape[1]
    holders = per_owner * owners
    cap = 2 * atoms // holders
    rim = atoms // 8
    sizes = (owners, per_owner, cap)
    by_rows = (holders, 1, batches * cap, width)
    by_atom = (holders, 1, batches, cap, width)
    barrier = lax.optimization_barrier
    mine = lax.axis_index("pair").astype(jnp.int32)[None]
    slab = lax.axis_index("slab").astype(jnp.int32)[None]
    slabs = lax.axis_size("slab")
    padded = round_up(hidden_width, LANES)
    flat_rows = sum(flat_blocks(width, padded)) * padded
    piece = round_up(-(-flat_rows // slabs), 16)

    place, place_t, packed, source, first, last = start(
        elements, features, charges, cot_features, cot_charges, mixing, rim, sizes
    )
    arrived = swap(packed).reshape(holders, 2, batches * cap, width)
    left, right = to_both_sides(first, last)
    band, band_t = make_bands(distances, neighbours, counts, shells, rim)
    old_weights = [native(w, which) for which, w in enumerate((w_in, w_mid, w_out))]
    old_moms = [native(m, which, False) for which, m in enumerate((mom_in, mom_mid, mom_out))]
    weights = cast_weights(mine, old_weights, hidden_width, per_owner, width)

    message = edge_forward(source, left, right, band, radial, 0, place, sizes)
    message, arrived = barrier((message, arrived))
    message = swap(message).reshape(by_rows)
    result, pre_one, pre_two = network_forward(arrived, message, weights, 0)
    back, halves = barrier(
        (swap(result).reshape(by_atom), half_moments(old_moms, hidden_width, per_owner, flat_rows))
    )
    hidden_one, charge_one, source_one, first, last = update_atoms(
        back, 0, place_t, features, charges, mixing, 1, rim
    )

    left_one, right_one = to_both_sides(first, last)
    message_one = edge_forward(source_one, left_one, right_one, band, radial, 1, place, sizes)
    message_one = swap(message_one).reshape(by_rows)
    result_one, rows_one, grad_hidden, grad_message, *saved = network_turn(
        arrived, result, message_one, weights, 1
    )
    grad_message = swap(grad_message).reshape(by_atom)
    pieces = weight_grad(slab, rows_one, message_one, arrived, 1, saved, (piece, LANES), slabs)
    grad_message, grad_hidden, pieces = barrier((grad_message, grad_hidden, pieces))
    grad_hidden = swap(grad_hidden).reshape(by_atom)
    pieces_one = exchange(pieces)
    inner, to_left, to_right, radial_grad = edge_backward(
        grad_message, place_t, source_one, left_one, right_one, band, band_t, radial, 1
    )
    to_left, to_right, pieces_one[1] = barrier((to_left, to_right, pieces_one[1]))
    from_left, from_right = to_both_sides(to_left, to_right)
    from_left, pieces_one[-1] = barrier((from_left, pieces_one[-1]))
    grad, grad_charge, small_one, packed = finish(
        inner, from_left, from_right, grad_hidden, place_t, cot_features, cot_charges, charge_one,
        mixing, 1, radial_grad, place,
    )

    grad_update = swap(packed).reshape(by_rows)
    grad_update, piece_one = barrier((grad_update, sum_arrays(pieces_one)[0]))
    totals_one = to_all_slabs(piece_one)
    grad_message, both, *saved = network_backward(grad_update, pre_one, pre_two, result_one, weights, 0)
    grad_message, totals_one[1] = barrier((grad_message, totals_one[1]))
    grad_message = swap(grad_message).reshape(by_atom)
    pieces = weight_grad(slab, arrived, message, grad_update, 0, saved, (piece, LANES), slabs)
    grad_message, both, pieces, totals_one = barrier((grad_message, both, pieces, totals_one))
    pieces_zero = exchange(pieces)
    both = swap(both).reshape(holders, 2, batches, cap, width)
    total_one, pieces_zero[1] = barrier((join(slab, totals_one), pieces_zero[1]))
    task = lambda layer: layer * per_owner + mine
    step_one = muon_step(task(1), total_one, halves, hidden_width)
    step_one, other_one = barrier((step_one, other_of_pair(total_one)))
    steps_one = (step_one, other_of_pair(step_one))
    pieces_zero, _ = barrier((pieces_zero, step_one))
    copies, grad_message = barrier((sum_arrays(pieces_zero, slabs), grad_message))
    total_zero = lax.all_to_all(copies, "slab", split_axis=0, concat_axis=0, tiled=True)
    total_zero = total_zero.reshape(slabs * piece, LANES)
    inner, to_left, to_right, radial_grad = edge_backward(
        grad_message, place_t, source, left, right, band, band_t, radial, 0
    )
    from_left, from_right = to_both_sides(to_left, to_right)
    from_left, steps_one = barrier((from_left, steps_one))
    grad_features, grad_charges, smalls, features_out, charges_out = finish(
        inner, from_left, from_right, both, place_t, grad, grad_charge, charges, mixing, 0, radial_grad,
        last=(small_one, hidden_one, charge_one),
    )
    total_zero, smalls = barrier((total_zero, smalls))
    step = muon_step(task(0), total_zero, halves, hidden_width)
    step, other, smalls = barrier((step, other_of_pair(total_zero), sum_first(swap(smalls))))
    steps = (step, other_of_pair(step))

    new_radial, new_radial_mom, new_mixing, new_mixing_mom = small_step(
        to_all_slabs(smalls), radial, radial_mom, mixing, mixing_mom
    )
    news = [native(jnp.zeros(m.shape, F32), which, False) for which, m in enumerate((mom_in, mom_mid, mom_out))]
    news = [shape_of(new.shape, F32) for new in news] * 2
    sizes = (hidden_width, per_owner)
    done = apply_layer(mine, (total_one, other_one), steps_one, halves, old_weights, news, 1, *sizes)
    done = apply_layer(mine, (total_zero, other), steps, halves, old_weights, news, 0, *sizes, done)
    news = [from_native(value, which % 3, per_owner, hidden_width) for which, value in enumerate(done)]
    return (
        features_out,
        charges_out,
        grad_features,
        grad_charges,
        *news[3:],
        *news[:3],
        new_radial,
        new_radial_mom,
        new_mixing,
        new_mixing_mom,
    )


def solution(mesh):
    in_specs = (
        P(None, EVERY, None),
        P(None, None, EVERY),
        P(None, EVERY),
        P(None, None, EVERY),
        P(None, EVERY),
        P(None, None, EVERY),
        P(),
        P(),
        P(),
        P(),
        P(None, "elem", None, None),
        P(None, "elem", None, None),
        P(None, "elem", None, None),
        P(None, "elem", None, None),
        P(None, "elem", None, None),
        P(None, "elem", None, None),
        P(None, EVERY, None),
        P(None, None, EVERY),
    )
    out_specs = (
        P(None, EVERY, None),
        P(None, None, EVERY),
        P(None, EVERY, None),
        P(None, None, EVERY),
        P(None, "elem", None, None),
        P(None, "elem", None, None),
        P(None, "elem", None, None),
        P(None, "elem", None, None),
        P(None, "elem", None, None),
        P(None, "elem", None, None),
        P(),
        P(),
        P(),
        P(),
    )
    devices = mesh.devices
    folded = jax.sharding.Mesh(devices.reshape(devices.shape[0] // 2, 2, devices.shape[1]), EVERY)
    return jax.shard_map(
        on_device, mesh=folded, in_specs=in_specs, out_specs=out_specs, check_vma=False
    )
```

```python
import functools
import math

import jax
import jax.numpy as jnp
from jax import lax
from jax.experimental import pallas as pl
from jax.experimental.pallas import tpu as pltpu
from jax.sharding import PartitionSpec as P

EXACT = lax.Precision.HIGHEST
SHELL_START = 0.8
SHELL_SPACING = 0.28
SHELL_SHARPNESS = 8.0
CUTOFF_RADIUS = 5.0
MOMENTUM = 0.5
LEARNING_RATE = 0.25
NEWTON_A = 3.4445
NEWTON_B = -4.775
NEWTON_C = 2.0315
NEWTON_CENTRES = (0.0, 0.0, 0.5, 1.0, 1.0)
QUARTERS = 4
GROUP = 8
SOURCES = 2
LANES = 128
FAR = 100.0
VMEM_BYTES = 60 * 1024 * 1024
F32 = jnp.float32
BF16 = jnp.bfloat16
NN = (((1,), (0,)), ((), ()))
NT = (((1,), (1,)), ((), ()))
TN = (((0,), (0,)), ((), ()))


def dot(left, right, dims, precision=None):
    return lax.dot_general(left, right, dims, precision=precision, preferred_element_type=F32)


def iota(shape, dim):
    return lax.broadcasted_iota(jnp.int32, shape, dim)


def round_up(size, multiple):
    return -(-size // multiple) * multiple


def params():
    return pltpu.CompilerParams(vmem_limit_bytes=VMEM_BYTES)


def cost(flops, read_bytes):
    return pl.CostEstimate(flops=int(flops), bytes_accessed=int(read_bytes), transcendentals=0)


def shape_of(shape, dtype):
    return jax.ShapeDtypeStruct(shape, dtype)


def at_step(shape, axis):
    block = tuple(1 if dim == axis else size for dim, size in enumerate(shape))
    return pl.BlockSpec(block, lambda step: tuple(step if dim == axis else 0 for dim in range(len(shape))))


def whole(shape):
    return pl.BlockSpec(shape, lambda *step: (0,) * len(shape))


def columns(rows):
    count, atoms = rows.shape
    return jnp.concatenate([rows, jnp.zeros((LANES - count, atoms), F32)], axis=0).T


def eight_rows(rows):
    return jnp.concatenate([rows, jnp.zeros((8 - rows.shape[0], rows.shape[1]), F32)], axis=0)


def add_columns(values, first):
    return jnp.concatenate([values[:, :LANES] + first, values[:, LANES:]], axis=1)


def source_of(hidden, charge_cols, mixing, channels):
    for channel in range(channels):
        hidden = hidden + charge_cols[:, channel : channel + 1] * mixing[channel : channel + 1, :]
    return hidden.astype(BF16)


def store_source(source, source_ref, first_ref, last_ref):
    rim = first_ref.shape[1]
    source_ref[0] = source
    first_ref[0] = source[:rim]
    last_ref[0] = source[source.shape[0] - rim :]


def atom_spec(values, which=0):
    holders, _, _, cap, width = values.shape
    return pl.BlockSpec((holders, 1, 1, cap, width), lambda step: (0, which, step, 0, 0))


def start_kernel(
    sizes, elem_ref, feat_ref, charge_ref, cotf_ref, cotc_ref, mixing_ref,
    place_ref, place_t_ref, packed_ref, source_ref, first_ref, last_ref,
):
    owners, per_owner, cap = sizes
    slots, atoms = place_ref.shape[1:]
    channels = charge_ref.shape[1]
    row = elem_ref[pl.ds(pl.program_id(0), 1), :]
    before = iota((atoms, atoms), 0)
    after = iota((atoms, atoms), 1)
    hot = (iota((LANES, atoms), 0) == row).astype(F32)
    rank = dot(hot.astype(BF16), (before < after).astype(F32).astype(BF16), NN)
    rank = jnp.sum(rank * hot, axis=0, keepdims=True)
    holder = lax.rem(row, per_owner) * owners + lax.div(row, per_owner)
    slot = holder.astype(F32) * cap + rank
    place = (iota((slots, atoms), 0) == slot.astype(jnp.int32)).astype(F32).astype(BF16)
    slot_t = jnp.broadcast_to(slot, (LANES, atoms)).T[:, :1].astype(jnp.int32)
    place_t = (iota((atoms, slots), 1) == slot_t).astype(F32).astype(BF16)
    place_ref[0] = place
    place_t_ref[0] = place_t
    features = feat_ref[0]
    grad = add_columns(cotf_ref[0].astype(F32), columns(cotc_ref[0])).astype(BF16)
    holders, _, _, _, width = packed_ref.shape
    for which, values in enumerate((features, grad)):
        packed = dot(place, values, NN).astype(BF16)
        packed_ref[:, which] = packed.reshape(holders, 1, cap, width)
    store_source(
        source_of(features.astype(F32), columns(charge_ref[0]), mixing_ref[0], channels),
        source_ref, first_ref, last_ref,
    )


def start(elements, features, charges, cot_features, cot_charges, mixing, rim, sizes):
    batches, atoms, width = features.shape
    owners, per_owner, cap = sizes
    holders = owners * per_owner
    packed_shape = (holders, 2, batches, cap, width)
    args = (elements, features, charges, cot_features, cot_charges, mixing)
    outs = (
        shape_of((batches, holders * cap, atoms), BF16),
        shape_of((batches, atoms, holders * cap), BF16),
        shape_of(packed_shape, BF16),
        shape_of((batches, atoms, width), BF16),
        shape_of((batches, rim, width), BF16),
        shape_of((batches, rim, width), BF16),
    )
    return pl.pallas_call(
        functools.partial(start_kernel, sizes),
        grid=(batches,),
        in_specs=[whole(elements.shape)]
        + [at_step(arg.shape, 0) for arg in args[1:-1]]
        + [whole(mixing.shape)],
        out_specs=[
            at_step(outs[0].shape, 0),
            at_step(outs[1].shape, 0),
            at_step(packed_shape, 2),
        ]
        + [at_step(out.shape, 0) for out in outs[3:]],
        out_shape=outs,
        compiler_params=params(),
        cost_estimate=cost(6e8, 8e6),
        name="start",
    )(*args)


def bands_kernel(shells, dist_ref, near_ref, band_ref, band_t_ref):
    groups, pairs = dist_ref.shape[1:]
    slots = pairs // GROUP
    per_quarter = groups // QUARTERS
    window = band_ref.shape[2]
    rows = shells * GROUP
    sub = iota((GROUP, pairs), 0)
    lane = iota((GROUP, pairs), 1)
    own = ((lane >= sub * slots) & (lane < (sub + 1) * slots)).astype(F32)
    centres = SHELL_START + SHELL_SPACING * iota((shells, 1), 0).astype(F32)
    target = iota((window, pairs), 0)
    distance_all = dist_ref[0]
    envelope_all = 0.5 * (jnp.cos(math.pi * distance_all / CUTOFF_RADIUS) + 1.0)
    for group in range(groups):
        distance = distance_all[group : group + 1]
        spread = distance - centres
        basis = jnp.exp(-SHELL_SHARPNESS * spread * spread) * envelope_all[group : group + 1]
        spaced = (basis[:, None, :] * own[None]).reshape(rows, pairs).astype(BF16)
        hot = (target == near_ref[0, group : group + 1, :]).astype(F32).astype(BF16)
        band_ref[0, group * rows : (group + 1) * rows, :] = dot(spaced, hot, NT).astype(BF16)
        quarter, inner = group // per_quarter, group % per_quarter
        band_t_ref[0, quarter, :, inner * rows : (inner + 1) * rows] = dot(hot, spaced, NT).astype(BF16)


def make_bands(distances, neighbours, counts, shells, rim):
    batches, slots, atoms = distances.shape
    groups = atoms // GROUP
    block = atoms // QUARTERS
    window = block + 2 * rim
    live = iota(distances.shape, 1) < counts[:, None, :]
    distance = jnp.where(live, distances, FAR)
    local = neighbours - (iota(neighbours.shape, 2) // block) * block

    def grouped(values):
        return jnp.transpose(values, (0, 2, 1)).reshape(batches, groups, GROUP * slots)

    args = (grouped(distance), grouped(local))
    rows = shells * GROUP
    outs = (
        shape_of((batches, groups * rows, window), BF16),
        shape_of((batches, QUARTERS, window, groups // QUARTERS * rows), BF16),
    )
    return pl.pallas_call(
        functools.partial(bands_kernel, shells),
        grid=(batches,),
        in_specs=[at_step(arg.shape, 0) for arg in args],
        out_specs=[at_step(out.shape, 0) for out in outs],
        out_shape=outs,
        compiler_params=params(),
        cost_estimate=cost(3e9, 8e6),
        name="bands",
    )(*args)


def edge_forward_kernel(source_ref, left_ref, right_ref, band_ref, radial_ref, place_ref, packed_ref):
    atoms, width = source_ref.shape[1:]
    shells = radial_ref.shape[1]
    rim = left_ref.shape[1]
    block = atoms // QUARTERS
    window = block + 2 * rim
    per_quarter = block // GROUP
    extended = jnp.concatenate([left_ref[0], source_ref[0], right_ref[0]], axis=0)
    radial = jnp.broadcast_to(radial_ref[0][:, None, :], (shells, GROUP, width))
    rows = block * shells
    pieces = []
    for quarter in range(QUARTERS):
        near = extended[quarter * block : quarter * block + window]
        sums = dot(band_ref[0, quarter * rows : (quarter + 1) * rows, :], near, NN)
        sums = sums.reshape(per_quarter, shells, GROUP, width) * radial[None]
        pieces.append(jnp.sum(sums, axis=1).reshape(block, width))
    message = jnp.concatenate(pieces, axis=0).astype(BF16)
    packed = dot(place_ref[0], message, NN).astype(BF16)
    packed_ref[...] = packed.reshape(packed_ref.shape)


def edge_forward(source, left, right, band, radial, layer, place, sizes):
    batches, atoms, width = source.shape
    owners, per_owner, cap = sizes
    packed_shape = (owners * per_owner, 1, batches, cap, width)
    return pl.pallas_call(
        edge_forward_kernel,
        grid=(batches,),
        in_specs=[at_step(arg.shape, 0) for arg in (source, left, right, band)]
        + [pl.BlockSpec((1,) + radial.shape[1:], lambda step: (layer, 0, 0)), at_step(place.shape, 0)],
        out_specs=at_step(packed_shape, 2),
        out_shape=shape_of(packed_shape, BF16),
        compiler_params=params(),
        cost_estimate=cost(1.2e9, 6e6),
        name="edge_forward",
    )(source, left, right, band, radial, place)


def edge_backward_kernel(
    grad_ref, place_t_ref, source_ref, left_ref, right_ref, band_ref, band_t_ref, radial_ref,
    inner_ref, to_left_ref, to_right_ref, radial_grad_ref, total,
):
    atoms, width = source_ref.shape[1:]
    shells = radial_ref.shape[1]
    rim = left_ref.shape[1]
    block = atoms // QUARTERS
    window = block + 2 * rim
    per_quarter = block // GROUP
    rows = block * shells
    step = pl.program_id(0)
    slots = place_t_ref.shape[2]
    grad = dot(place_t_ref[0], grad_ref[...].reshape(slots, width), NN)
    extended = jnp.concatenate([left_ref[0], source_ref[0], right_ref[0]], axis=0)
    radial = jnp.broadcast_to(radial_ref[0][:, None, :], (shells, GROUP, width))
    total[...] = jnp.zeros_like(total)
    radial_sum = jnp.zeros((shells, GROUP, width), F32)
    for quarter in range(QUARTERS):
        near = extended[quarter * block : quarter * block + window]
        sums = dot(band_ref[0, quarter * rows : (quarter + 1) * rows, :], near, NN)
        piece = grad[quarter * block : (quarter + 1) * block].reshape(per_quarter, 1, GROUP, width)
        radial_sum = radial_sum + jnp.sum(
            sums.reshape(per_quarter, shells, GROUP, width) * piece, axis=0
        )
        scaled = (radial[None] * piece).reshape(rows, width).astype(BF16)
        total[quarter * block : quarter * block + window] += dot(band_t_ref[0, quarter], scaled, NN)
    inner_ref[0] = total[rim : rim + atoms]
    to_left_ref[0] = total[:rim].astype(BF16)
    to_right_ref[0] = total[rim + atoms :].astype(BF16)
    radial_here = jnp.sum(radial_sum, axis=1)

    @pl.when(step == 0)
    def _():
        radial_grad_ref[...] = radial_here

    @pl.when(step > 0)
    def _():
        radial_grad_ref[...] += radial_here


def edge_backward(grad, place_t, source, left, right, band, band_t, radial, layer):
    batches, atoms, width = source.shape
    rim = left.shape[1]
    shells = radial.shape[1]
    outs = (
        shape_of((batches, atoms, width), F32),
        shape_of(left.shape, BF16),
        shape_of(left.shape, BF16),
        shape_of((shells, width), F32),
    )
    return pl.pallas_call(
        edge_backward_kernel,
        grid=(batches,),
        in_specs=[atom_spec(grad), at_step(place_t.shape, 0)]
        + [at_step(arg.shape, 0) for arg in (source, left, right, band, band_t)]
        + [pl.BlockSpec((1,) + radial.shape[1:], lambda step: (layer, 0, 0))],
        out_specs=[at_step(out.shape, 0) for out in outs[:3]] + [whole(outs[3].shape)],
        out_shape=outs,
        scratch_shapes=[pltpu.VMEM((atoms + 2 * rim, width), F32)],
        compiler_params=params(),
        cost_estimate=cost(2.5e9, 10e6),
        name="edge_backward",
    )(grad, place_t, source, left, right, band, band_t, radial)


def update_kernel(back_ref, place_t_ref, hidden_ref, charge_ref, *rest):
    mixing_ref, hidden_out_ref, charge_out_ref, *sources = rest if len(rest) > 2 else (None, *rest)
    slots, width = place_t_ref.shape[2], hidden_ref.shape[2]
    channels = charge_ref.shape[1]
    update = dot(place_t_ref[0], back_ref[...].reshape(slots, width), NN)
    hidden = hidden_ref[0].astype(F32) + update
    charge = charge_ref[0] + update[:, :LANES].T[:channels]
    hidden_out_ref[0] = hidden
    charge_out_ref[0] = charge
    if sources:
        store_source(source_of(hidden, columns(charge), mixing_ref[0], channels), *sources)


def update_atoms(back, which, place_t, hidden, charge, mixing=None, layer=0, rim=0):
    batches, atoms, width = hidden.shape
    outs = [shape_of((batches, atoms, width), F32), shape_of(charge.shape, F32)]
    args = [back, place_t, hidden, charge]
    specs = [atom_spec(back, which)] + [at_step(arg.shape, 0) for arg in args[1:]]
    if mixing is not None:
        args.append(mixing)
        specs.append(pl.BlockSpec((1,) + mixing.shape[1:], lambda step: (layer, 0, 0)))
        outs += [shape_of((batches, rows, width), BF16) for rows in (atoms, rim, rim)]
    return pl.pallas_call(
        update_kernel,
        grid=(batches,),
        in_specs=specs,
        out_specs=[at_step(out.shape, 0) for out in outs],
        out_shape=outs,
        compiler_params=params(),
        cost_estimate=cost(2e8, 4e6),
        name="update_atoms",
    )(*args)


def finish_kernel(
    repack, inner_ref, from_left_ref, from_right_ref, back_ref, place_t_ref, grad_ref, grad_charge_ref,
    charge_ref, mixing_ref, radial_grad_ref, *rest,
):
    if repack:
        place_ref, grad_out_ref, charge_out_ref, small_ref, packed_ref = rest
    else:
        earlier_ref, late_ref, hidden_ref, late_charge_ref, *rest = rest
        grad_out_ref, charge_out_ref, copies_ref, hidden_out_ref, late_charge_out_ref, small_ref = rest
    atoms, width = inner_ref.shape[1:]
    rim = from_left_ref.shape[1]
    channels = charge_ref.shape[1]
    slots = place_t_ref.shape[2]
    shells = radial_grad_ref.shape[0]
    step = pl.program_id(0)
    inner = inner_ref[0]
    source_grad = jnp.concatenate(
        [
            inner[:rim] + from_left_ref[0].astype(F32),
            inner[rim : atoms - rim],
            inner[atoms - rim :] + from_right_ref[0].astype(F32),
        ],
        axis=0,
    )
    mixing_grad = dot(eight_rows(charge_ref[0]), source_grad, NN, EXACT)
    charge_term = dot(eight_rows(mixing_ref[0]), source_grad, NT, EXACT)
    joined = dot(place_t_ref[0], back_ref[...].reshape(slots, width), NN)
    grad = grad_ref[0].astype(F32) + joined + source_grad
    grad_charge = grad_charge_ref[0] + charge_term[:channels]
    grad_out_ref[0] = grad
    charge_out_ref[0] = grad_charge

    @pl.when(step == 0)
    def _():
        small_ref[:shells] = radial_grad_ref[...]
        small_ref[shells:] = mixing_grad

    @pl.when(step > 0)
    def _():
        small_ref[shells:] += mixing_grad

    if not repack:
        update = dot(place_t_ref[0], late_ref[...].reshape(slots, width), NN)
        hidden_out_ref[0] = hidden_ref[0] + update
        late_charge_out_ref[0] = late_charge_ref[0] + update[:, :LANES].T[:channels]

        @pl.when(step == pl.num_programs(0) - 1)
        def _():
            joined = jnp.concatenate([small_ref[...], earlier_ref[...]], axis=0).astype(BF16)
            for copy in range(copies_ref.shape[0]):
                copies_ref[copy] = joined

    else:
        sent = add_columns(grad, columns(grad_charge)).astype(BF16)
        packed = dot(place_ref[0], sent, NN).astype(BF16)
        packed_ref[...] = packed.reshape(packed_ref.shape)


def finish(inner, from_left, from_right, back, place_t, grad, grad_charge, charge, mixing, layer, radial_grad, place=None, last=None):
    batches, atoms, width = inner.shape
    args = [inner, from_left, from_right, back, place_t, grad, grad_charge, charge, mixing, radial_grad]
    specs = [at_step(arg.shape, 0) for arg in args]
    specs[3] = atom_spec(back)
    specs[8] = pl.BlockSpec((1,) + mixing.shape[1:], lambda step: (layer, 0, 0))
    specs[9] = whole(radial_grad.shape)
    small = (radial_grad.shape[0] + 8, width)
    outs = [shape_of(inner.shape, F32), shape_of(charge.shape, F32), shape_of(small, F32)]
    out_specs = [at_step(outs[0].shape, 0), at_step(outs[1].shape, 0), whole(small)]
    scratch = []
    if place is None:
        earlier, hidden, late_charge = last
        args += [earlier, back, hidden, late_charge]
        specs += [whole(earlier.shape), atom_spec(back, 1), at_step(hidden.shape, 0), at_step(charge.shape, 0)]
        copies = (back.shape[0], small[0] + earlier.shape[0], width)
        outs[2], out_specs[2] = shape_of(copies, BF16), whole(copies)
        outs += outs[:2]
        out_specs += out_specs[:2]
        scratch.append(pltpu.VMEM(small, F32))
    else:
        args.append(place)
        specs.append(at_step(place.shape, 0))
        outs.append(shape_of(back.shape[:1] + (1,) + back.shape[2:], BF16))
        out_specs.append(atom_spec(back))
    return pl.pallas_call(
        functools.partial(finish_kernel, place is not None),
        grid=(batches,),
        in_specs=specs,
        out_specs=out_specs,
        out_shape=outs,
        scratch_shapes=scratch,
        compiler_params=params(),
        cost_estimate=cost(6e8, 6e6),
        name="finish",
    )(*args)


def gelu_parts(value):
    scale = math.sqrt(2.0 / math.pi)
    square = value * value
    bent = jnp.tanh(scale * (value + 0.044715 * value * square))
    half = 0.5 * (1.0 + bent)
    slope = half + 0.5 * value * (1.0 - bent * bent) * scale * (1.0 + 3.0 * 0.044715 * square)
    return value * half, slope


def rows_spec(values, which=0, sources=SOURCES):
    _, _, rows, width = values.shape
    return pl.BlockSpec((sources, 1, rows, width), lambda step: (step, which, 0, 0))


def saved_spec(shape, steps):
    return pl.BlockSpec((shape[0] // steps, shape[1]), lambda step: (step, 0))


def weight_specs(weights, layer):
    return [pl.BlockSpec((1,) + w.shape[1:], lambda step: (layer, 0, 0)) for w in weights]


def forward_through(hidden, message, first_ref, middle_ref, last_ref):
    width = hidden.shape[1]
    pre_one = dot(hidden, first_ref[0, :, :width], NT) + dot(message, first_ref[0, :, width:], NT)
    act_one = gelu_parts(pre_one)[0].astype(BF16)
    pre_two = dot(act_one, middle_ref[0], NN)
    act_two = gelu_parts(pre_two)[0].astype(BF16)
    return dot(act_two, last_ref[0], NN).astype(BF16), pre_one, pre_two


def back_through(grad, pre_one, pre_two, first_ref, middle_ref, last_ref, span, outs):
    width = grad.shape[1]
    act_one_ref, act_two_ref, grad_one_ref, grad_two_ref = outs
    act_one, slope_one = gelu_parts(pre_one)
    act_two, slope_two = gelu_parts(pre_two)
    act_one_ref[span] = act_one.astype(BF16)
    act_two_ref[span] = act_two.astype(BF16)
    grad_two = (slope_two * dot(grad, last_ref[0], NT)).astype(BF16)
    grad_two_ref[span] = grad_two
    grad_one = (slope_one * dot(grad_two, middle_ref[0], NT)).astype(BF16)
    grad_one_ref[span] = grad_one
    return (
        dot(grad_one, first_ref[0, :, :width], NN).astype(BF16),
        dot(grad_one, first_ref[0, :, width:], NN).astype(BF16),
    )


def network_forward_kernel(
    feat_ref, message_ref, first_ref, middle_ref, last_ref, result_ref, pre_one_ref, pre_two_ref
):
    sources, _, rows, _ = feat_ref.shape
    for source in range(sources):
        span = slice(source * rows, (source + 1) * rows)
        result_ref[source, 0], pre_one_ref[span], pre_two_ref[span] = forward_through(
            feat_ref[source, 0], message_ref[source, 0], first_ref, middle_ref, last_ref
        )


def network_forward(arrived, message, weights, layer):
    holders, _, rows, width = message.shape
    steps = holders // SOURCES
    saved = (holders * rows, weights[1].shape[1])
    return pl.pallas_call(
        network_forward_kernel,
        grid=(steps,),
        in_specs=[rows_spec(arrived), rows_spec(message)] + weight_specs(weights, layer),
        out_specs=[rows_spec(message)] + [saved_spec(saved, steps)] * 2,
        out_shape=(shape_of(message.shape, BF16), shape_of(saved, F32), shape_of(saved, F32)),
        compiler_params=params(),
        cost_estimate=cost(1.4e9, 8e6),
        name="network_forward",
    )(arrived, message, *weights)


def network_turn_kernel(
    feat_ref, result_ref, message_ref, grad_ref, first_ref, middle_ref, last_ref,
    result_out_ref, rows_ref, grad_hidden_ref, grad_message_ref, *saved,
):
    sources, _, rows, _ = feat_ref.shape
    for source in range(sources):
        span = slice(source * rows, (source + 1) * rows)
        hidden = feat_ref[source, 0].astype(F32) + result_ref[source, 0].astype(F32)
        hidden = hidden.astype(BF16)
        rows_ref[source, 0] = hidden
        result_out_ref[source, 0], pre_one, pre_two = forward_through(
            hidden, message_ref[source, 0], first_ref, middle_ref, last_ref
        )
        grad_hidden_ref[source, 0], grad_message_ref[source, 0] = back_through(
            grad_ref[source, 0], pre_one, pre_two, first_ref, middle_ref, last_ref, span, saved
        )


def network_turn(arrived, result, message, weights, layer):
    holders, _, rows, width = message.shape
    steps = holders // SOURCES
    saved = (holders * rows, weights[1].shape[1])
    spec = rows_spec(message)
    return pl.pallas_call(
        network_turn_kernel,
        grid=(steps,),
        in_specs=[rows_spec(arrived), spec, spec, rows_spec(arrived, 1)] + weight_specs(weights, layer),
        out_specs=[spec] * 4 + [saved_spec(saved, steps)] * 4,
        out_shape=[shape_of(message.shape, BF16)] * 4 + [shape_of(saved, BF16)] * 4,
        compiler_params=params(),
        cost_estimate=cost(2.8e9, 12e6),
        name="network_turn",
    )(arrived, result, message, arrived, *weights)


def network_backward_kernel(
    grad_ref, pre_one_ref, pre_two_ref, late_ref, first_ref, middle_ref, last_ref,
    grad_message_ref, both_ref, *saved,
):
    sources, _, rows, _ = grad_ref.shape
    both_ref[:, 1] = late_ref[:, 0]
    for source in range(sources):
        span = slice(source * rows, (source + 1) * rows)
        both_ref[source, 0], grad_message_ref[source, 0] = back_through(
            grad_ref[source, 0], pre_one_ref[span], pre_two_ref[span],
            first_ref, middle_ref, last_ref, span, saved,
        )


def network_backward(grad, pre_one, pre_two, late, weights, layer):
    holders, _, rows, width = grad.shape
    steps = holders // SOURCES
    saved = pre_one.shape
    spec = rows_spec(grad)
    both = pl.BlockSpec((SOURCES, 2, rows, width), lambda step: (step, 0, 0, 0))
    return pl.pallas_call(
        network_backward_kernel,
        grid=(steps,),
        in_specs=[spec] + [saved_spec(saved, steps)] * 2 + [spec] + weight_specs(weights, layer),
        out_specs=[spec, both] + [saved_spec(saved, steps)] * 4,
        out_shape=[shape_of(grad.shape, BF16), shape_of((holders, 2, rows, width), BF16)]
        + [shape_of(saved, BF16)] * 4,
        compiler_params=params(),
        cost_estimate=cost(1.4e9, 12e6),
        name="network_backward",
    )(grad, pre_one, pre_two, late, *weights)


def flat_blocks(width, hidden_width):
    return 2 * width // LANES, hidden_width // LANES, width // LANES


def flat_blocks_of(flat_rows, padded):
    width_blocks = (flat_rows // padded - padded // LANES) // 3
    return 2 * width_blocks, padded // LANES, width_blocks


def store_blocks(ref, base, values):
    rows = values.shape[0]
    for block in range(values.shape[1] // LANES):
        ref[(base + block) * rows : (base + block + 1) * rows, :] = values[
            :, block * LANES : (block + 1) * LANES
        ].astype(ref.dtype)


def weight_grad_kernel(
    pieces, place_ref, hidden_ref, message_ref, grad_ref, act_one_ref, act_two_ref, grad_one_ref, grad_two_ref, *rest
):
    *out_refs, first_sum, middle_sum, last_sum, flat = rest
    sources, _, rows, width = hidden_ref.shape
    count = sources * rows
    step = pl.program_id(0)
    grad_one = grad_one_ref[...]
    parts = (
        (first_sum.at[:, :width], dot(grad_one, hidden_ref[...].reshape(count, width), TN)),
        (first_sum.at[:, width:], dot(grad_one, message_ref[...].reshape(count, width), TN)),
        (middle_sum, dot(act_one_ref[...], grad_two_ref[...], TN)),
        (last_sum, dot(act_two_ref[...], grad_ref[...].reshape(count, width), TN)),
    )

    @pl.when(step == 0)
    def _():
        for total, part in parts:
            total[...] = part

    @pl.when(step > 0)
    def _():
        for total, part in parts:
            total[...] += part

    @pl.when(step == pl.num_programs(0) - 1)
    def _():
        base = 0
        for total in (first_sum, middle_sum, last_sum):
            store_blocks(flat, base, total[...])
            base += total.shape[1] // LANES
        live = base * first_sum.shape[0]
        if flat.shape[0] > live:
            flat[live:] = jnp.zeros((flat.shape[0] - live, LANES), F32)
        here = place_ref[0]
        if not pieces:
            (out_ref,) = out_refs
            for owned in range(out_ref.shape[0]):
                out_ref[owned] = jnp.where(owned == here, flat[...], 0.0).astype(BF16)
        for shift, piece_ref in enumerate(out_refs if pieces else ()):
            rows_each = piece_ref.shape[0]
            target = lax.rem(here + shift, pieces)
            piece_ref[...] = flat[pl.ds(pl.multiple_of(target * rows_each, 16), rows_each), :].astype(BF16)


def weight_grad(place, hidden, message, grad, which, saved, shape, pieces=0):
    holders, _, rows, width = message.shape
    hidden_width = saved[0].shape[1]
    steps = 2
    sources = holders // steps

    def rows_of(values, kind):
        return pl.BlockSpec(
            (sources, 1) + values.shape[2:], lambda step, place: (step, kind, 0, 0)
        )

    saved_rows = pl.BlockSpec((saved[0].shape[0] // steps, hidden_width), lambda step, place: (step, 0))
    flat_rows = shape[-2] * max(pieces, 1)
    return pl.pallas_call(
        functools.partial(weight_grad_kernel, pieces),
        grid_spec=pltpu.PrefetchScalarGridSpec(
            num_scalar_prefetch=1,
            grid=(steps,),
            in_specs=[rows_of(hidden, 0), rows_of(message, 0), rows_of(grad, which)] + [saved_rows] * 4,
            out_specs=[whole(shape)] * max(pieces, 1),
            scratch_shapes=[
                pltpu.VMEM((hidden_width, cols), F32) for cols in (2 * width, hidden_width, width)
            ]
            + [pltpu.VMEM((flat_rows, LANES), F32)],
        ),
        out_shape=[shape_of(shape, BF16)] * max(pieces, 1),
        compiler_params=params(),
        cost_estimate=cost(1.4e9, 8e6),
        name="weight_grad",
    )(place, hidden, message, grad, *saved)


def newton_step(current, tall, centre, eye_ref):
    high = current.astype(BF16)
    rest = dot(high, high, TN if tall else NT)
    if centre:
        size = rest.shape[0]
        rest = rest - centre * eye_ref[:size, :size]
    rest_low = rest.astype(BF16)
    linear = NEWTON_B + 2.0 * NEWTON_C * centre
    poly = (linear * rest + NEWTON_C * dot(rest_low, rest_low, NN)).astype(BF16)
    step = dot(high, poly, NN) if tall else dot(poly, high, NN)
    return (NEWTON_A + NEWTON_B * centre + NEWTON_C * centre * centre) * current + step


def unit(moment):
    return moment / (jnp.sqrt(jnp.sum(moment * moment)) + 1e-07)


def native(values, which, fill=True):
    cols = values.shape[2 if which == 0 else 3]
    padded = LANES * (1 << (round_up(cols, LANES) // LANES - 1).bit_length())
    if padded > cols and fill:
        values = jnp.pad(values, ((0, 0), (0, 0), (0, 0), (0, padded - cols)))
    values = jnp.transpose(values, (0, 3, 1, 2) if which == 0 else (0, 2, 1, 3))
    if padded > cols and not fill:
        return values
    layers, rows, per_owner, _ = values.shape
    values = values.reshape(layers, rows, per_owner, padded // LANES, LANES)
    return jnp.transpose(values, (0, 1, 3, 2, 4)).reshape(layers, -1, LANES)


def from_native(values, which, per_owner, rows):
    if values.ndim == 3:
        layers = values.shape[0]
        values = values.reshape(layers, rows, -1, per_owner, LANES)
        values = jnp.transpose(values, (0, 1, 3, 2, 4)).reshape(layers, rows, per_owner, -1)
    return jnp.transpose(values, (0, 2, 3, 1) if which == 0 else (0, 2, 1, 3))


class Lying:
    def __init__(self, ref, rows, per_owner, blocks):
        self.ref, self.rows, self.per_owner, self.blocks = ref, rows, per_owner, blocks
        self.spread = ref.shape[1] // rows if len(ref.shape) == 3 else 0

    def place(self, block, owned):
        if self.spread:
            return (0, pl.ds(block * self.per_owner + owned, self.rows, stride=self.spread), slice(None))
        return (0, slice(None), owned, slice(block * LANES, block * LANES + self.lanes(block)))

    def lanes(self, block):
        return LANES if self.spread else min(LANES, self.ref.shape[3] - block * LANES)

    def read(self, block, owned):
        return self.ref[self.place(block, owned)]

    def write(self, block, owned, value):
        self.ref[self.place(block, owned)] = value[:, : self.lanes(block)]


def lying(refs, rows, per_owner):
    blocks = [ref.shape[1] // rows // per_owner for ref in refs]
    blocks[1] = round_up(rows, LANES) // LANES
    return [Lying(ref, rows, per_owner, count) for ref, count in zip(refs, blocks)]


def half_kernel(rows, per_owner, *refs):
    moms, flat_ref = lying(refs[:3], rows, per_owner), refs[3]
    padded = round_up(rows, LANES)
    base = 0
    for mom in moms:
        for block in range(mom.blocks):
            begin = base * padded
            for owned in range(per_owner):
                flat_ref[owned, begin : begin + padded] = jnp.zeros((padded, LANES), F32)
                flat_ref[owned, begin : begin + rows, : mom.lanes(block)] = MOMENTUM * mom.read(block, owned)
            base += 1


def half_moments(moms, rows, per_owner, flat_rows):
    layers = moms[0].shape[0]
    return pl.pallas_call(
        functools.partial(half_kernel, rows, per_owner),
        grid=(layers,),
        in_specs=[at_step(mom.shape, 0) for mom in moms],
        out_specs=pl.BlockSpec((per_owner, flat_rows, LANES), lambda step: (step, 0, 0)),
        out_shape=shape_of((layers * per_owner, flat_rows, LANES), F32),
        compiler_params=params(),
        cost_estimate=cost(4e6, 14e6),
        name="half_moments",
    )(*moms)


def cast_kernel(rows, per_owner, mine_ref, *refs):
    olds, lows, scratches = lying(refs[:3], rows, per_owner), refs[3:6], refs[6:]
    for old, low, scratch in zip(olds, lows, scratches):
        scratch[rows:] = jnp.zeros((scratch.shape[0] - rows, scratch.shape[1]), F32)
        for block in range(old.blocks):
            scratch[:rows, block * LANES : (block + 1) * LANES] = old.read(block, mine_ref[0])
        low[0] = scratch[...].astype(BF16)


def cast_weights(mine, weights, rows, per_owner, width):
    layers = weights[0].shape[0]
    padded = round_up(rows, LANES)
    shapes = [(padded, blocks * LANES) for blocks in flat_blocks(width, padded)]
    layer_spec = lambda shape: pl.BlockSpec(
        (1,) + shape[1:], lambda step, mine: (step,) + (0,) * (len(shape) - 1)
    )
    return pl.pallas_call(
        functools.partial(cast_kernel, rows, per_owner),
        grid_spec=pltpu.PrefetchScalarGridSpec(
            num_scalar_prefetch=1,
            grid=(layers,),
            in_specs=[layer_spec(w.shape) for w in weights],
            out_specs=[layer_spec((layers,) + shape) for shape in shapes],
            scratch_shapes=[pltpu.VMEM(shape, F32) for shape in shapes],
        ),
        out_shape=[shape_of((layers,) + shape, BF16) for shape in shapes],
        compiler_params=params(),
        cost_estimate=cost(4e6, 11e6),
        name="cast_weights",
    )(mine, *weights)


def sum_kernel(*refs):
    total = refs[0][...].astype(F32)
    for ref in refs[1:-1]:
        total = total + ref[...].astype(F32)
    total = total.astype(BF16)
    for copy in range(refs[-1].shape[0]):
        refs[-1][copy] = total


def sum_arrays(parts, copies=1):
    shape = parts[0].shape
    return pl.pallas_call(
        sum_kernel,
        grid=(1,),
        in_specs=[whole(shape)] * len(parts),
        out_specs=whole((copies,) + shape),
        out_shape=shape_of((copies,) + shape, BF16),
        compiler_params=params(),
        cost_estimate=cost(1e6, 2e6),
        name="sum_arrays",
    )(*parts)


def sum_first_kernel(parts_ref, total_ref):
    total = parts_ref[0].astype(F32)
    for part in range(1, parts_ref.shape[0]):
        total = total + parts_ref[part].astype(F32)
    total_ref[...] = total.astype(BF16)


def sum_first(parts):
    return pl.pallas_call(
        sum_first_kernel,
        grid=(1,),
        in_specs=[whole(parts.shape)],
        out_specs=whole(parts.shape[1:]),
        out_shape=shape_of(parts.shape[1:], BF16),
        compiler_params=params(),
        cost_estimate=cost(1e6, 1e6),
        name="sum_first",
    )(parts)


def join_kernel(slab_ref, *refs):
    *parts, whole_ref = refs
    rows = parts[0].shape[0]
    for shift, part in enumerate(parts):
        origin = lax.rem(slab_ref[0] - shift + len(parts), len(parts))
        whole_ref[pl.ds(pl.multiple_of(origin * rows, 16), rows), :] = part[...]


def join(slab, parts):
    rows, lanes = parts[0].shape
    shape = (rows * len(parts), lanes)
    return pl.pallas_call(
        join_kernel,
        grid_spec=pltpu.PrefetchScalarGridSpec(
            num_scalar_prefetch=1,
            grid=(1,),
            in_specs=[whole((rows, lanes))] * len(parts),
            out_specs=whole(shape),
        ),
        out_shape=shape_of(shape, BF16),
        compiler_params=params(),
        cost_estimate=cost(1e6, 2e6),
        name="join",
    )(slab, *parts)


def muon_kernel(rows, task_ref, half_ref, grad_ref, step_ref, eye_ref):
    padded = round_up(rows, LANES)
    eye_ref[...] = (iota(eye_ref.shape, 0) == iota(eye_ref.shape, 1)).astype(F32)
    base = 0
    values = []
    blocks = flat_blocks_of(half_ref.shape[1], padded)
    for count in blocks:
        parts = []
        for block in range(base, base + count):
            span = slice(block * padded, (block + 1) * padded)
            parts.append(half_ref[0, span] + grad_ref[span].astype(F32))
        base += count
        values.append(unit(jnp.concatenate(parts, axis=1)))
    for centre in NEWTON_CENTRES:
        values = [newton_step(value, which == 2, centre, eye_ref) for which, value in enumerate(values)]
    base = 0
    for count, value in zip(blocks, values):
        longest = rows if count == padded // LANES else max(count * LANES, rows)
        store_blocks(step_ref, base, value * (LEARNING_RATE * 0.2 * math.sqrt(longest)))
        base += count


def layer_of(values, layer):
    return pl.BlockSpec(
        (1,) + values.shape[1:], lambda step, *scalars: (layer,) + (0,) * (values.ndim - 1)
    )


def muon_step(task, grads, halves, rows):
    block = (1,) + halves.shape[1:]
    padded = round_up(rows, LANES)
    return pl.pallas_call(
        functools.partial(muon_kernel, rows),
        grid_spec=pltpu.PrefetchScalarGridSpec(
            num_scalar_prefetch=1,
            grid=(1,),
            in_specs=[pl.BlockSpec(block, lambda step, task: (task[0], 0, 0)), whole(grads.shape)],
            out_specs=whole(block[1:]),
            scratch_shapes=[pltpu.VMEM((padded, padded), F32)],
        ),
        out_shape=shape_of(block[1:], BF16),
        compiler_params=params(),
        cost_estimate=cost(7e9, 4e6),
        name="muon",
    )(task, halves, grads)


def apply_kernel(rows, per_owner, mine_ref, half_ref, *refs):
    steps, grads, weights = refs[:2], refs[2:4], lying(refs[4:7], rows, per_owner)
    new_moms, new_weights = lying(refs[-6:-3], rows, per_owner), lying(refs[-3:], rows, per_owner)
    mine = mine_ref[0]
    padded = round_up(rows, LANES)
    base = 0
    for weight, new_mom, new_weight in zip(weights, new_moms, new_weights):
        for block in range(weight.blocks):
            span = slice(base * padded, base * padded + rows)
            both_grads = [ref[span].astype(F32) for ref in grads]
            both_steps = [ref[span].astype(F32) for ref in steps]
            for owned in range(per_owner):
                grad = jnp.where(mine == owned, *both_grads)
                step = jnp.where(mine == owned, *both_steps)
                new_mom.write(block, owned, half_ref[owned, span] + grad)
                new_weight.write(block, owned, weight.read(block, owned) - step)
            base += 1


def apply_layer(mine, grads, steps, halves, weights, news, layer, rows, per_owner, partial=None):
    args = [mine, halves, *steps, *grads, *weights]
    in_specs = [pl.BlockSpec((per_owner,) + halves.shape[1:], lambda step, mine: (layer, 0, 0))]
    in_specs += [whole(value.shape) for value in (*steps, *grads)]
    in_specs += [layer_of(weight, layer) for weight in weights]
    aliases = {}
    if partial is not None:
        aliases = {len(args) + which: which for which in range(len(news))}
        args += list(partial)
        in_specs += [pl.BlockSpec(memory_space=pl.ANY)] * len(news)
    return pl.pallas_call(
        functools.partial(apply_kernel, rows, per_owner),
        grid_spec=pltpu.PrefetchScalarGridSpec(
            num_scalar_prefetch=1,
            grid=(1,),
            in_specs=in_specs,
            out_specs=[layer_of(new, layer) for new in news],
        ),
        out_shape=[shape_of(new.shape, F32) for new in news],
        input_output_aliases=aliases,
        compiler_params=params(),
        cost_estimate=cost(2e6, 18e6),
        name="apply_layer",
    )(*args)


def small_kernel(count_parts, *refs):
    parts, refs = refs[:count_parts], refs[count_parts:]
    radial_ref, radial_mom_ref, mixing_ref, mixing_mom_ref, *outs = refs
    new_radial_ref, new_radial_mom_ref, new_mixing_ref, new_mixing_mom_ref = outs
    layers, shells, width = radial_ref.shape
    channels = mixing_ref.shape[1]
    values = []
    total = parts[0][...].astype(F32)
    for part in parts[1:]:
        total = total + part[...].astype(F32)
    each = total.shape[0] // layers
    for layer in range(layers):
        total_here = total[layer * each : (layer + 1) * each]
        moment = MOMENTUM * radial_mom_ref[layer] + total_here[:shells]
        new_radial_mom_ref[layer] = moment
        values.append(unit(moment))
        moment = eight_rows(MOMENTUM * mixing_mom_ref[layer]) + total_here[shells:]
        new_mixing_mom_ref[layer] = moment[:channels]
        values.append(unit(moment))
    for _ in NEWTON_CENTRES:
        grams = [dot(value, value, NT, EXACT) for value in values]
        polys = [NEWTON_B * gram + NEWTON_C * dot(gram, gram, NN, EXACT) for gram in grams]
        values = [NEWTON_A * value + dot(poly, value, NN, EXACT) for value, poly in zip(values, polys)]
    for layer in range(layers):
        lift = LEARNING_RATE * 0.2 * math.sqrt(max(shells, width))
        new_radial_ref[layer] = radial_ref[layer] - lift * values[2 * layer]
        lift = LEARNING_RATE * 0.2 * math.sqrt(max(channels, width))
        new_mixing_ref[layer] = mixing_ref[layer] - lift * values[2 * layer + 1][:channels]


def small_step(parts, radial, radial_mom, mixing, mixing_mom):
    args = (*parts, radial, radial_mom, mixing, mixing_mom)
    outs = [radial, radial_mom, mixing, mixing_mom]
    return pl.pallas_call(
        functools.partial(small_kernel, len(parts)),
        grid=(1,),
        in_specs=[whole(arg.shape) for arg in args],
        out_specs=[whole(out.shape) for out in outs],
        out_shape=[shape_of(out.shape, F32) for out in outs],
        compiler_params=params(),
        cost_estimate=cost(1e8, 3e6),
        name="small_step",
    )(*args)


EVERY = ("slab", "pair", "elem")
HOLDERS = ("pair", "elem")


def swap(values):
    return lax.all_to_all(values, HOLDERS, split_axis=0, concat_axis=0, tiled=True)


def to_both_sides(to_left, to_right):
    count = lax.axis_size(EVERY)
    up = [(i, (i + 1) % count) for i in range(count)]
    down = [((i + 1) % count, i) for i in range(count)]
    return lax.ppermute(to_right, EVERY, up), lax.ppermute(to_left, EVERY, down)


def other_of_pair(values):
    return lax.ppermute(values, "pair", [(0, 1), (1, 0)])


def shifted(values, shift):
    count = lax.axis_size("slab")
    return lax.ppermute(values, "slab", [(i, (i + shift) % count) for i in range(count)])


def exchange(pieces):
    return [piece if shift == 0 else shifted(piece, shift) for shift, piece in enumerate(pieces)]


def to_all_slabs(piece):
    return exchange([piece] * lax.axis_size("slab"))


def on_device(
    features,
    charges,
    elements,
    neighbours,
    counts,
    distances,
    radial,
    radial_mom,
    mixing,
    mixing_mom,
    w_in,
    w_mid,
    w_out,
    mom_in,
    mom_mid,
    mom_out,
    cot_features,
    cot_charges,
):
    batches, atoms, width = features.shape
    per_owner, hidden_width = w_in.shape[1], w_in.shape[3]
    owners = lax.axis_size("elem")
    shells = radial.shape[1]
    holders = per_owner * owners
    cap = 2 * atoms // holders
    rim = atoms // 8
    sizes = (owners, per_owner, cap)
    by_rows = (holders, 1, batches * cap, width)
    by_atom = (holders, 1, batches, cap, width)
    barrier = lax.optimization_barrier
    mine = lax.axis_index("pair").astype(jnp.int32)[None]
    slab = lax.axis_index("slab").astype(jnp.int32)[None]
    slabs = lax.axis_size("slab")
    padded = round_up(hidden_width, LANES)
    flat_rows = sum(flat_blocks(width, padded)) * padded
    piece = round_up(-(-flat_rows // slabs), 16)

    place, place_t, packed, source, first, last = start(
        elements, features, charges, cot_features, cot_charges, mixing, rim, sizes
    )
    arrived = swap(packed).reshape(holders, 2, batches * cap, width)
    left, right = to_both_sides(first, last)
    band, band_t = make_bands(distances, neighbours, counts, shells, rim)
    old_weights = [native(w, which) for which, w in enumerate((w_in, w_mid, w_out))]
    old_moms = [native(m, which, False) for which, m in enumerate((mom_in, mom_mid, mom_out))]
    weights = cast_weights(mine, old_weights, hidden_width, per_owner, width)

    message = edge_forward(source, left, right, band, radial, 0, place, sizes)
    message, arrived = barrier((message, arrived))
    message = swap(message).reshape(by_rows)
    result, pre_one, pre_two = network_forward(arrived, message, weights, 0)
    back, halves = barrier(
        (swap(result).reshape(by_atom), half_moments(old_moms, hidden_width, per_owner, flat_rows))
    )
    hidden_one, charge_one, source_one, first, last = update_atoms(
        back, 0, place_t, features, charges, mixing, 1, rim
    )

    left_one, right_one = to_both_sides(first, last)
    message_one = edge_forward(source_one, left_one, right_one, band, radial, 1, place, sizes)
    message_one = swap(message_one).reshape(by_rows)
    result_one, rows_one, grad_hidden, grad_message, *saved = network_turn(
        arrived, result, message_one, weights, 1
    )
    grad_message = swap(grad_message).reshape(by_atom)
    pieces = weight_grad(slab, rows_one, message_one, arrived, 1, saved, (piece, LANES), slabs)
    grad_message, grad_hidden, pieces = barrier((grad_message, grad_hidden, pieces))
    grad_hidden = swap(grad_hidden).reshape(by_atom)
    pieces_one = exchange(pieces)
    inner, to_left, to_right, radial_grad = edge_backward(
        grad_message, place_t, source_one, left_one, right_one, band, band_t, radial, 1
    )
    to_left, to_right, pieces_one[1] = barrier((to_left, to_right, pieces_one[1]))
    from_left, from_right = to_both_sides(to_left, to_right)
    from_left, pieces_one[-1] = barrier((from_left, pieces_one[-1]))
    grad, grad_charge, small_one, packed = finish(
        inner, from_left, from_right, grad_hidden, place_t, cot_features, cot_charges, charge_one,
        mixing, 1, radial_grad, place,
    )

    grad_update = swap(packed).reshape(by_rows)
    grad_update, piece_one = barrier((grad_update, sum_arrays(pieces_one)[0]))
    totals_one = to_all_slabs(piece_one)
    grad_message, both, *saved = network_backward(grad_update, pre_one, pre_two, result_one, weights, 0)
    grad_message, totals_one[1] = barrier((grad_message, totals_one[1]))
    grad_message = swap(grad_message).reshape(by_atom)
    pieces = weight_grad(slab, arrived, message, grad_update, 0, saved, (piece, LANES), slabs)
    grad_message, both, pieces, totals_one = barrier((grad_message, both, pieces, totals_one))
    pieces_zero = exchange(pieces)
    both = swap(both).reshape(holders, 2, batches, cap, width)
    inner, to_left, to_right, radial_grad = edge_backward(
        grad_message, place_t, source, left, right, band, band_t, radial, 0
    )
    total_one, pieces_zero[1], inner = barrier((join(slab, totals_one), pieces_zero[1], inner))
    task = lambda layer: layer * per_owner + mine
    step = muon_step(task(1), total_one, halves, hidden_width)
    pieces_zero, _ = barrier((pieces_zero, step))
    step, other_one = barrier((step, other_of_pair(total_one)))
    steps_one = (step, other_of_pair(step))
    copies = sum_arrays(pieces_zero, slabs)
    total_zero = lax.all_to_all(copies, "slab", split_axis=0, concat_axis=0, tiled=True)
    total_zero = total_zero.reshape(slabs * piece, LANES)
    from_left, from_right = to_both_sides(to_left, to_right)
    grad_features, grad_charges, smalls, features_out, charges_out = finish(
        inner, from_left, from_right, both, place_t, grad, grad_charge, charges, mixing, 0, radial_grad,
        last=(small_one, hidden_one, charge_one),
    )
    total_zero, smalls, steps_one = barrier((total_zero, smalls, steps_one))
    step = muon_step(task(0), total_zero, halves, hidden_width)
    step, other = barrier((step, other_of_pair(total_zero)))
    steps = (step, other_of_pair(step))
    steps_one, smalls = barrier((steps_one, sum_first(swap(smalls))))

    new_radial, new_radial_mom, new_mixing, new_mixing_mom = small_step(
        to_all_slabs(smalls), radial, radial_mom, mixing, mixing_mom
    )
    news = [native(jnp.zeros(m.shape, F32), which, False) for which, m in enumerate((mom_in, mom_mid, mom_out))]
    news = [shape_of(new.shape, F32) for new in news] * 2
    sizes = (hidden_width, per_owner)
    done = apply_layer(mine, (total_one, other_one), steps_one, halves, old_weights, news, 1, *sizes)
    done = apply_layer(mine, (total_zero, other), steps, halves, old_weights, news, 0, *sizes, done)
    news = [from_native(value, which % 3, per_owner, hidden_width) for which, value in enumerate(done)]
    return (
        features_out,
        charges_out,
        grad_features,
        grad_charges,
        *news[3:],
        *news[:3],
        new_radial,
        new_radial_mom,
        new_mixing,
        new_mixing_mom,
    )


def solution(mesh):
    in_specs = (
        P(None, EVERY, None),
        P(None, None, EVERY),
        P(None, EVERY),
        P(None, None, EVERY),
        P(None, EVERY),
        P(None, None, EVERY),
        P(),
        P(),
        P(),
        P(),
        P(None, "elem", None, None),
        P(None, "elem", None, None),
        P(None, "elem", None, None),
        P(None, "elem", None, None),
        P(None, "elem", None, None),
        P(None, "elem", None, None),
        P(None, EVERY, None),
        P(None, None, EVERY),
    )
    out_specs = (
        P(None, EVERY, None),
        P(None, None, EVERY),
        P(None, EVERY, None),
        P(None, None, EVERY),
        P(None, "elem", None, None),
        P(None, "elem", None, None),
        P(None, "elem", None, None),
        P(None, "elem", None, None),
        P(None, "elem", None, None),
        P(None, "elem", None, None),
        P(),
        P(),
        P(),
        P(),
    )
    devices = mesh.devices
    folded = jax.sharding.Mesh(devices.reshape(devices.shape[0] // 2, 2, devices.shape[1]), EVERY)
    return jax.shard_map(
        on_device, mesh=folded, in_specs=in_specs, out_specs=out_specs, check_vma=False
    )
```

```python
import functools
import math

import jax
import jax.numpy as jnp
from jax import lax
from jax.experimental import pallas as pl
from jax.experimental.pallas import tpu as pltpu
from jax.sharding import PartitionSpec as P

EXACT = lax.Precision.HIGHEST
SHELL_START = 0.8
SHELL_SPACING = 0.28
SHELL_SHARPNESS = 8.0
CUTOFF_RADIUS = 5.0
MOMENTUM = 0.5
LEARNING_RATE = 0.25
NEWTON_A = 3.4445
NEWTON_B = -4.775
NEWTON_C = 2.0315
NEWTON_CENTRES = (0.0, 0.0, 0.5, 1.0, 1.0)
QUARTERS = 4
GROUP = 8
SOURCES = 2
LANES = 128
FAR = 100.0
VMEM_BYTES = 60 * 1024 * 1024
F32 = jnp.float32
BF16 = jnp.bfloat16
NN = (((1,), (0,)), ((), ()))
NT = (((1,), (1,)), ((), ()))
TN = (((0,), (0,)), ((), ()))


def dot(left, right, dims, precision=None):
    return lax.dot_general(left, right, dims, precision=precision, preferred_element_type=F32)


def iota(shape, dim):
    return lax.broadcasted_iota(jnp.int32, shape, dim)


def round_up(size, multiple):
    return -(-size // multiple) * multiple


def params():
    return pltpu.CompilerParams(vmem_limit_bytes=VMEM_BYTES)


def cost(flops, read_bytes):
    return pl.CostEstimate(flops=int(flops), bytes_accessed=int(read_bytes), transcendentals=0)


def shape_of(shape, dtype):
    return jax.ShapeDtypeStruct(shape, dtype)


def at_step(shape, axis):
    block = tuple(1 if dim == axis else size for dim, size in enumerate(shape))
    return pl.BlockSpec(block, lambda step: tuple(step if dim == axis else 0 for dim in range(len(shape))))


def whole(shape):
    return pl.BlockSpec(shape, lambda *step: (0,) * len(shape))


def columns(rows):
    count, atoms = rows.shape
    return jnp.concatenate([rows, jnp.zeros((LANES - count, atoms), F32)], axis=0).T


def eight_rows(rows):
    return jnp.concatenate([rows, jnp.zeros((8 - rows.shape[0], rows.shape[1]), F32)], axis=0)


def add_columns(values, first):
    return jnp.concatenate([values[:, :LANES] + first, values[:, LANES:]], axis=1)


def source_of(hidden, charge_cols, mixing, channels):
    for channel in range(channels):
        hidden = hidden + charge_cols[:, channel : channel + 1] * mixing[channel : channel + 1, :]
    return hidden.astype(BF16)


def store_source(source, source_ref, first_ref, last_ref):
    rim = first_ref.shape[1]
    source_ref[0] = source
    first_ref[0] = source[:rim]
    last_ref[0] = source[source.shape[0] - rim :]


def atom_spec(values, which=0):
    holders, _, _, cap, width = values.shape
    return pl.BlockSpec((holders, 1, 1, cap, width), lambda step: (0, which, step, 0, 0))


def start_kernel(
    sizes, elem_ref, feat_ref, charge_ref, cotf_ref, cotc_ref, mixing_ref,
    place_ref, place_t_ref, packed_ref, source_ref, first_ref, last_ref,
):
    owners, per_owner, cap = sizes
    slots, atoms = place_ref.shape[1:]
    channels = charge_ref.shape[1]
    row = elem_ref[pl.ds(pl.program_id(0), 1), :]
    before = iota((atoms, atoms), 0)
    after = iota((atoms, atoms), 1)
    hot = (iota((LANES, atoms), 0) == row).astype(F32)
    rank = dot(hot.astype(BF16), (before < after).astype(F32).astype(BF16), NN)
    rank = jnp.sum(rank * hot, axis=0, keepdims=True)
    holder = lax.rem(row, per_owner) * owners + lax.div(row, per_owner)
    slot = holder.astype(F32) * cap + rank
    place = (iota((slots, atoms), 0) == slot.astype(jnp.int32)).astype(F32).astype(BF16)
    slot_t = jnp.broadcast_to(slot, (LANES, atoms)).T[:, :1].astype(jnp.int32)
    place_t = (iota((atoms, slots), 1) == slot_t).astype(F32).astype(BF16)
    place_ref[0] = place
    place_t_ref[0] = place_t
    features = feat_ref[0]
    grad = add_columns(cotf_ref[0].astype(F32), columns(cotc_ref[0])).astype(BF16)
    holders, _, _, _, width = packed_ref.shape
    for which, values in enumerate((features, grad)):
        packed = dot(place, values, NN).astype(BF16)
        packed_ref[:, which] = packed.reshape(holders, 1, cap, width)
    store_source(
        source_of(features.astype(F32), columns(charge_ref[0]), mixing_ref[0], channels),
        source_ref, first_ref, last_ref,
    )


def start(elements, features, charges, cot_features, cot_charges, mixing, rim, sizes):
    batches, atoms, width = features.shape
    owners, per_owner, cap = sizes
    holders = owners * per_owner
    packed_shape = (holders, 2, batches, cap, width)
    args = (elements, features, charges, cot_features, cot_charges, mixing)
    outs = (
        shape_of((batches, holders * cap, atoms), BF16),
        shape_of((batches, atoms, holders * cap), BF16),
        shape_of(packed_shape, BF16),
        shape_of((batches, atoms, width), BF16),
        shape_of((batches, rim, width), BF16),
        shape_of((batches, rim, width), BF16),
    )
    return pl.pallas_call(
        functools.partial(start_kernel, sizes),
        grid=(batches,),
        in_specs=[whole(elements.shape)]
        + [at_step(arg.shape, 0) for arg in args[1:-1]]
        + [whole(mixing.shape)],
        out_specs=[
            at_step(outs[0].shape, 0),
            at_step(outs[1].shape, 0),
            at_step(packed_shape, 2),
        ]
        + [at_step(out.shape, 0) for out in outs[3:]],
        out_shape=outs,
        compiler_params=params(),
        cost_estimate=cost(6e8, 8e6),
        name="start",
    )(*args)


def bands_kernel(shells, dist_ref, near_ref, band_ref, band_t_ref):
    groups, pairs = dist_ref.shape[1:]
    slots = pairs // GROUP
    per_quarter = groups // QUARTERS
    window = band_ref.shape[2]
    rows = shells * GROUP
    sub = iota((GROUP, pairs), 0)
    lane = iota((GROUP, pairs), 1)
    own = ((lane >= sub * slots) & (lane < (sub + 1) * slots)).astype(F32)
    centres = SHELL_START + SHELL_SPACING * iota((shells, 1), 0).astype(F32)
    target = iota((window, pairs), 0)
    distance_all = dist_ref[0]
    envelope_all = 0.5 * (jnp.cos(math.pi * distance_all / CUTOFF_RADIUS) + 1.0)
    for group in range(groups):
        distance = distance_all[group : group + 1]
        spread = distance - centres
        basis = jnp.exp(-SHELL_SHARPNESS * spread * spread) * envelope_all[group : group + 1]
        spaced = (basis[:, None, :] * own[None]).reshape(rows, pairs).astype(BF16)
        hot = (target == near_ref[0, group : group + 1, :]).astype(F32).astype(BF16)
        band_ref[0, group * rows : (group + 1) * rows, :] = dot(spaced, hot, NT).astype(BF16)
        quarter, inner = group // per_quarter, group % per_quarter
        band_t_ref[0, quarter, :, inner * rows : (inner + 1) * rows] = dot(hot, spaced, NT).astype(BF16)


def make_bands(distances, neighbours, counts, shells, rim):
    batches, slots, atoms = distances.shape
    groups = atoms // GROUP
    block = atoms // QUARTERS
    window = block + 2 * rim
    live = iota(distances.shape, 1) < counts[:, None, :]
    distance = jnp.where(live, distances, FAR)
    local = neighbours - (iota(neighbours.shape, 2) // block) * block

    def grouped(values):
        return jnp.transpose(values, (0, 2, 1)).reshape(batches, groups, GROUP * slots)

    args = (grouped(distance), grouped(local))
    rows = shells * GROUP
    outs = (
        shape_of((batches, groups * rows, window), BF16),
        shape_of((batches, QUARTERS, window, groups // QUARTERS * rows), BF16),
    )
    return pl.pallas_call(
        functools.partial(bands_kernel, shells),
        grid=(batches,),
        in_specs=[at_step(arg.shape, 0) for arg in args],
        out_specs=[at_step(out.shape, 0) for out in outs],
        out_shape=outs,
        compiler_params=params(),
        cost_estimate=cost(3e9, 8e6),
        name="bands",
    )(*args)


def edge_forward_kernel(source_ref, left_ref, right_ref, band_ref, radial_ref, place_ref, packed_ref):
    atoms, width = source_ref.shape[1:]
    shells = radial_ref.shape[1]
    rim = left_ref.shape[1]
    block = atoms // QUARTERS
    window = block + 2 * rim
    per_quarter = block // GROUP
    extended = jnp.concatenate([left_ref[0], source_ref[0], right_ref[0]], axis=0)
    radial = jnp.broadcast_to(radial_ref[0][:, None, :], (shells, GROUP, width))
    rows = block * shells
    pieces = []
    for quarter in range(QUARTERS):
        near = extended[quarter * block : quarter * block + window]
        sums = dot(band_ref[0, quarter * rows : (quarter + 1) * rows, :], near, NN)
        sums = sums.reshape(per_quarter, shells, GROUP, width) * radial[None]
        pieces.append(jnp.sum(sums, axis=1).reshape(block, width))
    message = jnp.concatenate(pieces, axis=0).astype(BF16)
    packed = dot(place_ref[0], message, NN).astype(BF16)
    packed_ref[...] = packed.reshape(packed_ref.shape)


def edge_forward(source, left, right, band, radial, layer, place, sizes):
    batches, atoms, width = source.shape
    owners, per_owner, cap = sizes
    packed_shape = (owners * per_owner, 1, batches, cap, width)
    return pl.pallas_call(
        edge_forward_kernel,
        grid=(batches,),
        in_specs=[at_step(arg.shape, 0) for arg in (source, left, right, band)]
        + [pl.BlockSpec((1,) + radial.shape[1:], lambda step: (layer, 0, 0)), at_step(place.shape, 0)],
        out_specs=at_step(packed_shape, 2),
        out_shape=shape_of(packed_shape, BF16),
        compiler_params=params(),
        cost_estimate=cost(1.2e9, 6e6),
        name="edge_forward",
    )(source, left, right, band, radial, place)


def edge_backward_kernel(
    grad_ref, place_t_ref, source_ref, left_ref, right_ref, band_ref, band_t_ref, radial_ref,
    inner_ref, to_left_ref, to_right_ref, radial_grad_ref, total,
):
    atoms, width = source_ref.shape[1:]
    shells = radial_ref.shape[1]
    rim = left_ref.shape[1]
    block = atoms // QUARTERS
    window = block + 2 * rim
    per_quarter = block // GROUP
    rows = block * shells
    step = pl.program_id(0)
    slots = place_t_ref.shape[2]
    grad = dot(place_t_ref[0], grad_ref[...].reshape(slots, width), NN)
    extended = jnp.concatenate([left_ref[0], source_ref[0], right_ref[0]], axis=0)
    radial = jnp.broadcast_to(radial_ref[0][:, None, :], (shells, GROUP, width))
    total[...] = jnp.zeros_like(total)
    radial_sum = jnp.zeros((shells, GROUP, width), F32)
    for quarter in range(QUARTERS):
        near = extended[quarter * block : quarter * block + window]
        sums = dot(band_ref[0, quarter * rows : (quarter + 1) * rows, :], near, NN)
        piece = grad[quarter * block : (quarter + 1) * block].reshape(per_quarter, 1, GROUP, width)
        radial_sum = radial_sum + jnp.sum(
            sums.reshape(per_quarter, shells, GROUP, width) * piece, axis=0
        )
        scaled = (radial[None] * piece).reshape(rows, width).astype(BF16)
        total[quarter * block : quarter * block + window] += dot(band_t_ref[0, quarter], scaled, NN)
    inner_ref[0] = total[rim : rim + atoms]
    to_left_ref[0] = total[:rim].astype(BF16)
    to_right_ref[0] = total[rim + atoms :].astype(BF16)
    radial_here = jnp.sum(radial_sum, axis=1)

    @pl.when(step == 0)
    def _():
        radial_grad_ref[...] = radial_here

    @pl.when(step > 0)
    def _():
        radial_grad_ref[...] += radial_here


def edge_backward(grad, place_t, source, left, right, band, band_t, radial, layer):
    batches, atoms, width = source.shape
    rim = left.shape[1]
    shells = radial.shape[1]
    outs = (
        shape_of((batches, atoms, width), F32),
        shape_of(left.shape, BF16),
        shape_of(left.shape, BF16),
        shape_of((shells, width), F32),
    )
    return pl.pallas_call(
        edge_backward_kernel,
        grid=(batches,),
        in_specs=[atom_spec(grad), at_step(place_t.shape, 0)]
        + [at_step(arg.shape, 0) for arg in (source, left, right, band, band_t)]
        + [pl.BlockSpec((1,) + radial.shape[1:], lambda step: (layer, 0, 0))],
        out_specs=[at_step(out.shape, 0) for out in outs[:3]] + [whole(outs[3].shape)],
        out_shape=outs,
        scratch_shapes=[pltpu.VMEM((atoms + 2 * rim, width), F32)],
        compiler_params=params(),
        cost_estimate=cost(2.5e9, 10e6),
        name="edge_backward",
    )(grad, place_t, source, left, right, band, band_t, radial)


def update_kernel(back_ref, place_t_ref, hidden_ref, charge_ref, *rest):
    mixing_ref, hidden_out_ref, charge_out_ref, *sources = rest if len(rest) > 2 else (None, *rest)
    slots, width = place_t_ref.shape[2], hidden_ref.shape[2]
    channels = charge_ref.shape[1]
    update = dot(place_t_ref[0], back_ref[...].reshape(slots, width), NN)
    hidden = hidden_ref[0].astype(F32) + update
    charge = charge_ref[0] + update[:, :LANES].T[:channels]
    hidden_out_ref[0] = hidden
    charge_out_ref[0] = charge
    if sources:
        store_source(source_of(hidden, columns(charge), mixing_ref[0], channels), *sources)


def update_atoms(back, which, place_t, hidden, charge, mixing=None, layer=0, rim=0):
    batches, atoms, width = hidden.shape
    outs = [shape_of((batches, atoms, width), F32), shape_of(charge.shape, F32)]
    args = [back, place_t, hidden, charge]
    specs = [atom_spec(back, which)] + [at_step(arg.shape, 0) for arg in args[1:]]
    if mixing is not None:
        args.append(mixing)
        specs.append(pl.BlockSpec((1,) + mixing.shape[1:], lambda step: (layer, 0, 0)))
        outs += [shape_of((batches, rows, width), BF16) for rows in (atoms, rim, rim)]
    return pl.pallas_call(
        update_kernel,
        grid=(batches,),
        in_specs=specs,
        out_specs=[at_step(out.shape, 0) for out in outs],
        out_shape=outs,
        compiler_params=params(),
        cost_estimate=cost(2e8, 4e6),
        name="update_atoms",
    )(*args)


def finish_kernel(
    repack, inner_ref, from_left_ref, from_right_ref, back_ref, place_t_ref, grad_ref, grad_charge_ref,
    charge_ref, mixing_ref, radial_grad_ref, *rest,
):
    if repack:
        place_ref, grad_out_ref, charge_out_ref, small_ref, packed_ref = rest
    else:
        earlier_ref, late_ref, hidden_ref, late_charge_ref, *rest = rest
        grad_out_ref, charge_out_ref, joined_ref, hidden_out_ref, late_charge_out_ref, small_ref = rest
    atoms, width = inner_ref.shape[1:]
    rim = from_left_ref.shape[1]
    channels = charge_ref.shape[1]
    slots = place_t_ref.shape[2]
    shells = radial_grad_ref.shape[0]
    step = pl.program_id(0)
    inner = inner_ref[0]
    source_grad = jnp.concatenate(
        [
            inner[:rim] + from_left_ref[0].astype(F32),
            inner[rim : atoms - rim],
            inner[atoms - rim :] + from_right_ref[0].astype(F32),
        ],
        axis=0,
    )
    mixing_grad = dot(eight_rows(charge_ref[0]), source_grad, NN, EXACT)
    charge_term = dot(eight_rows(mixing_ref[0]), source_grad, NT, EXACT)
    joined = dot(place_t_ref[0], back_ref[...].reshape(slots, width), NN)
    grad = grad_ref[0].astype(F32) + joined + source_grad
    grad_charge = grad_charge_ref[0] + charge_term[:channels]
    grad_out_ref[0] = grad
    charge_out_ref[0] = grad_charge

    @pl.when(step == 0)
    def _():
        small_ref[:shells] = radial_grad_ref[...]
        small_ref[shells:] = mixing_grad

    @pl.when(step > 0)
    def _():
        small_ref[shells:] += mixing_grad

    if not repack:
        update = dot(place_t_ref[0], late_ref[...].reshape(slots, width), NN)
        hidden_out_ref[0] = hidden_ref[0] + update
        late_charge_out_ref[0] = late_charge_ref[0] + update[:, :LANES].T[:channels]

        @pl.when(step == pl.num_programs(0) - 1)
        def _():
            joined_ref[...] = jnp.concatenate([small_ref[...], earlier_ref[...]], axis=0).astype(BF16)

    else:
        sent = add_columns(grad, columns(grad_charge)).astype(BF16)
        packed = dot(place_ref[0], sent, NN).astype(BF16)
        packed_ref[...] = packed.reshape(packed_ref.shape)


def finish(inner, from_left, from_right, back, place_t, grad, grad_charge, charge, mixing, layer, radial_grad, place=None, last=None):
    batches, atoms, width = inner.shape
    args = [inner, from_left, from_right, back, place_t, grad, grad_charge, charge, mixing, radial_grad]
    specs = [at_step(arg.shape, 0) for arg in args]
    specs[3] = atom_spec(back)
    specs[8] = pl.BlockSpec((1,) + mixing.shape[1:], lambda step: (layer, 0, 0))
    specs[9] = whole(radial_grad.shape)
    small = (radial_grad.shape[0] + 8, width)
    outs = [shape_of(inner.shape, F32), shape_of(charge.shape, F32), shape_of(small, F32)]
    out_specs = [at_step(outs[0].shape, 0), at_step(outs[1].shape, 0), whole(small)]
    scratch = []
    if place is None:
        earlier, hidden, late_charge = last
        args += [earlier, back, hidden, late_charge]
        specs += [whole(earlier.shape), atom_spec(back, 1), at_step(hidden.shape, 0), at_step(charge.shape, 0)]
        joined = (small[0] + earlier.shape[0], width)
        outs[2], out_specs[2] = shape_of(joined, BF16), whole(joined)
        outs += outs[:2]
        out_specs += out_specs[:2]
        scratch.append(pltpu.VMEM(small, F32))
    else:
        args.append(place)
        specs.append(at_step(place.shape, 0))
        outs.append(shape_of(back.shape[:1] + (1,) + back.shape[2:], BF16))
        out_specs.append(atom_spec(back))
    return pl.pallas_call(
        functools.partial(finish_kernel, place is not None),
        grid=(batches,),
        in_specs=specs,
        out_specs=out_specs,
        out_shape=outs,
        scratch_shapes=scratch,
        compiler_params=params(),
        cost_estimate=cost(6e8, 6e6),
        name="finish",
    )(*args)


def gelu_parts(value):
    scale = math.sqrt(2.0 / math.pi)
    square = value * value
    bent = jnp.tanh(scale * (value + 0.044715 * value * square))
    half = 0.5 * (1.0 + bent)
    slope = half + 0.5 * value * (1.0 - bent * bent) * scale * (1.0 + 3.0 * 0.044715 * square)
    return value * half, slope


def rows_spec(values, which=0, sources=SOURCES):
    _, _, rows, width = values.shape
    return pl.BlockSpec((sources, 1, rows, width), lambda step: (step, which, 0, 0))


def saved_spec(shape, steps):
    return pl.BlockSpec((shape[0] // steps, shape[1]), lambda step: (step, 0))


def weight_specs(weights, layer):
    return [pl.BlockSpec((1,) + w.shape[1:], lambda step: (layer, 0, 0)) for w in weights]


def forward_through(hidden, message, first_ref, middle_ref, last_ref):
    width = hidden.shape[1]
    pre_one = dot(hidden, first_ref[0, :, :width], NT) + dot(message, first_ref[0, :, width:], NT)
    act_one = gelu_parts(pre_one)[0].astype(BF16)
    pre_two = dot(act_one, middle_ref[0], NN)
    act_two = gelu_parts(pre_two)[0].astype(BF16)
    return dot(act_two, last_ref[0], NN).astype(BF16), pre_one, pre_two


def back_through(grad, pre_one, pre_two, first_ref, middle_ref, last_ref, span, outs):
    width = grad.shape[1]
    act_one_ref, act_two_ref, grad_one_ref, grad_two_ref = outs
    act_one, slope_one = gelu_parts(pre_one)
    act_two, slope_two = gelu_parts(pre_two)
    act_one_ref[span] = act_one.astype(BF16)
    act_two_ref[span] = act_two.astype(BF16)
    grad_two = (slope_two * dot(grad, last_ref[0], NT)).astype(BF16)
    grad_two_ref[span] = grad_two
    grad_one = (slope_one * dot(grad_two, middle_ref[0], NT)).astype(BF16)
    grad_one_ref[span] = grad_one
    return (
        dot(grad_one, first_ref[0, :, :width], NN).astype(BF16),
        dot(grad_one, first_ref[0, :, width:], NN).astype(BF16),
    )


def network_forward_kernel(
    feat_ref, message_ref, first_ref, middle_ref, last_ref, result_ref, pre_one_ref, pre_two_ref
):
    sources, _, rows, _ = feat_ref.shape
    for source in range(sources):
        span = slice(source * rows, (source + 1) * rows)
        result_ref[source, 0], pre_one_ref[span], pre_two_ref[span] = forward_through(
            feat_ref[source, 0], message_ref[source, 0], first_ref, middle_ref, last_ref
        )


def network_forward(arrived, message, weights, layer):
    holders, _, rows, width = message.shape
    steps = holders // SOURCES
    saved = (holders * rows, weights[1].shape[1])
    return pl.pallas_call(
        network_forward_kernel,
        grid=(steps,),
        in_specs=[rows_spec(arrived), rows_spec(message)] + weight_specs(weights, layer),
        out_specs=[rows_spec(message)] + [saved_spec(saved, steps)] * 2,
        out_shape=(shape_of(message.shape, BF16), shape_of(saved, F32), shape_of(saved, F32)),
        compiler_params=params(),
        cost_estimate=cost(1.4e9, 8e6),
        name="network_forward",
    )(arrived, message, *weights)


def network_turn_kernel(
    feat_ref, result_ref, message_ref, grad_ref, first_ref, middle_ref, last_ref,
    result_out_ref, rows_ref, grad_hidden_ref, grad_message_ref, *saved,
):
    sources, _, rows, _ = feat_ref.shape
    for source in range(sources):
        span = slice(source * rows, (source + 1) * rows)
        hidden = feat_ref[source, 0].astype(F32) + result_ref[source, 0].astype(F32)
        hidden = hidden.astype(BF16)
        rows_ref[source, 0] = hidden
        result_out_ref[source, 0], pre_one, pre_two = forward_through(
            hidden, message_ref[source, 0], first_ref, middle_ref, last_ref
        )
        grad_hidden_ref[source, 0], grad_message_ref[source, 0] = back_through(
            grad_ref[source, 0], pre_one, pre_two, first_ref, middle_ref, last_ref, span, saved
        )


def network_turn(arrived, result, message, weights, layer):
    holders, _, rows, width = message.shape
    steps = holders // SOURCES
    saved = (holders * rows, weights[1].shape[1])
    spec = rows_spec(message)
    return pl.pallas_call(
        network_turn_kernel,
        grid=(steps,),
        in_specs=[rows_spec(arrived), spec, spec, rows_spec(arrived, 1)] + weight_specs(weights, layer),
        out_specs=[spec] * 4 + [saved_spec(saved, steps)] * 4,
        out_shape=[shape_of(message.shape, BF16)] * 4 + [shape_of(saved, BF16)] * 4,
        compiler_params=params(),
        cost_estimate=cost(2.8e9, 12e6),
        name="network_turn",
    )(arrived, result, message, arrived, *weights)


def network_backward_kernel(
    grad_ref, pre_one_ref, pre_two_ref, late_ref, first_ref, middle_ref, last_ref,
    grad_message_ref, both_ref, *saved,
):
    sources, _, rows, _ = grad_ref.shape
    both_ref[:, 1] = late_ref[:, 0]
    for source in range(sources):
        span = slice(source * rows, (source + 1) * rows)
        both_ref[source, 0], grad_message_ref[source, 0] = back_through(
            grad_ref[source, 0], pre_one_ref[span], pre_two_ref[span],
            first_ref, middle_ref, last_ref, span, saved,
        )


def network_backward(grad, pre_one, pre_two, late, weights, layer):
    holders, _, rows, width = grad.shape
    steps = holders // SOURCES
    saved = pre_one.shape
    spec = rows_spec(grad)
    both = pl.BlockSpec((SOURCES, 2, rows, width), lambda step: (step, 0, 0, 0))
    return pl.pallas_call(
        network_backward_kernel,
        grid=(steps,),
        in_specs=[spec] + [saved_spec(saved, steps)] * 2 + [spec] + weight_specs(weights, layer),
        out_specs=[spec, both] + [saved_spec(saved, steps)] * 4,
        out_shape=[shape_of(grad.shape, BF16), shape_of((holders, 2, rows, width), BF16)]
        + [shape_of(saved, BF16)] * 4,
        compiler_params=params(),
        cost_estimate=cost(1.4e9, 12e6),
        name="network_backward",
    )(grad, pre_one, pre_two, late, *weights)


def flat_blocks(width, hidden_width):
    return 2 * width // LANES, hidden_width // LANES, width // LANES


def flat_blocks_of(flat_rows, padded):
    width_blocks = (flat_rows // padded - padded // LANES) // 3
    return 2 * width_blocks, padded // LANES, width_blocks


def store_blocks(ref, base, values):
    rows = values.shape[0]
    for block in range(values.shape[1] // LANES):
        ref[(base + block) * rows : (base + block + 1) * rows, :] = values[
            :, block * LANES : (block + 1) * LANES
        ].astype(ref.dtype)


def weight_grad_kernel(
    pieces, place_ref, hidden_ref, message_ref, grad_ref, act_one_ref, act_two_ref, grad_one_ref, grad_two_ref, *rest
):
    *out_refs, first_sum, middle_sum, last_sum, flat = rest
    sources, _, rows, width = hidden_ref.shape
    count = sources * rows
    step = pl.program_id(0)
    grad_one = grad_one_ref[...]
    parts = (
        (first_sum.at[:, :width], dot(grad_one, hidden_ref[...].reshape(count, width), TN)),
        (first_sum.at[:, width:], dot(grad_one, message_ref[...].reshape(count, width), TN)),
        (middle_sum, dot(act_one_ref[...], grad_two_ref[...], TN)),
        (last_sum, dot(act_two_ref[...], grad_ref[...].reshape(count, width), TN)),
    )

    @pl.when(step == 0)
    def _():
        for total, part in parts:
            total[...] = part

    @pl.when(step > 0)
    def _():
        for total, part in parts:
            total[...] += part

    @pl.when(step == pl.num_programs(0) - 1)
    def _():
        base = 0
        for total in (first_sum, middle_sum, last_sum):
            store_blocks(flat, base, total[...])
            base += total.shape[1] // LANES
        live = base * first_sum.shape[0]
        if flat.shape[0] > live:
            flat[live:] = jnp.zeros((flat.shape[0] - live, LANES), F32)
        here = place_ref[0]
        if not pieces:
            (out_ref,) = out_refs
            for owned in range(out_ref.shape[0]):
                out_ref[owned] = jnp.where(owned == here, flat[...], 0.0).astype(BF16)
        for shift, piece_ref in enumerate(out_refs if pieces else ()):
            rows_each = piece_ref.shape[0]
            target = lax.rem(here + shift, pieces)
            piece_ref[...] = flat[pl.ds(pl.multiple_of(target * rows_each, 16), rows_each), :].astype(BF16)


def weight_grad(place, hidden, message, grad, which, saved, shape, pieces=0):
    holders, _, rows, width = message.shape
    hidden_width = saved[0].shape[1]
    steps = 2
    sources = holders // steps

    def rows_of(values, kind):
        return pl.BlockSpec(
            (sources, 1) + values.shape[2:], lambda step, place: (step, kind, 0, 0)
        )

    saved_rows = pl.BlockSpec((saved[0].shape[0] // steps, hidden_width), lambda step, place: (step, 0))
    flat_rows = shape[-2] * max(pieces, 1)
    return pl.pallas_call(
        functools.partial(weight_grad_kernel, pieces),
        grid_spec=pltpu.PrefetchScalarGridSpec(
            num_scalar_prefetch=1,
            grid=(steps,),
            in_specs=[rows_of(hidden, 0), rows_of(message, 0), rows_of(grad, which)] + [saved_rows] * 4,
            out_specs=[whole(shape)] * max(pieces, 1),
            scratch_shapes=[
                pltpu.VMEM((hidden_width, cols), F32) for cols in (2 * width, hidden_width, width)
            ]
            + [pltpu.VMEM((flat_rows, LANES), F32)],
        ),
        out_shape=[shape_of(shape, BF16)] * max(pieces, 1),
        compiler_params=params(),
        cost_estimate=cost(1.4e9, 8e6),
        name="weight_grad",
    )(place, hidden, message, grad, *saved)


def newton_step(current, tall, centre, eye_ref):
    high = current.astype(BF16)
    rest = dot(high, high, TN if tall else NT)
    if centre:
        size = rest.shape[0]
        rest = rest - centre * eye_ref[:size, :size]
    rest_low = rest.astype(BF16)
    linear = NEWTON_B + 2.0 * NEWTON_C * centre
    poly = (linear * rest + NEWTON_C * dot(rest_low, rest_low, NN)).astype(BF16)
    step = dot(high, poly, NN) if tall else dot(poly, high, NN)
    return (NEWTON_A + NEWTON_B * centre + NEWTON_C * centre * centre) * current + step


def unit(moment):
    return moment / (jnp.sqrt(jnp.sum(moment * moment)) + 1e-07)


def native(values, which, fill=True):
    cols = values.shape[2 if which == 0 else 3]
    padded = LANES * (1 << (round_up(cols, LANES) // LANES - 1).bit_length())
    if padded > cols and fill:
        values = jnp.pad(values, ((0, 0), (0, 0), (0, 0), (0, padded - cols)))
    values = jnp.transpose(values, (0, 3, 1, 2) if which == 0 else (0, 2, 1, 3))
    if padded > cols and not fill:
        return values
    layers, rows, per_owner, _ = values.shape
    values = values.reshape(layers, rows, per_owner, padded // LANES, LANES)
    return jnp.transpose(values, (0, 1, 3, 2, 4)).reshape(layers, -1, LANES)


def from_native(values, which, per_owner, rows):
    if values.ndim == 3:
        layers = values.shape[0]
        values = values.reshape(layers, rows, -1, per_owner, LANES)
        values = jnp.transpose(values, (0, 1, 3, 2, 4)).reshape(layers, rows, per_owner, -1)
    return jnp.transpose(values, (0, 2, 3, 1) if which == 0 else (0, 2, 1, 3))


class Lying:
    def __init__(self, ref, rows, per_owner, blocks):
        self.ref, self.rows, self.per_owner, self.blocks = ref, rows, per_owner, blocks
        self.spread = ref.shape[1] // rows if len(ref.shape) == 3 else 0

    def place(self, block, owned):
        if self.spread:
            return (0, pl.ds(block * self.per_owner + owned, self.rows, stride=self.spread), slice(None))
        return (0, slice(None), owned, slice(block * LANES, block * LANES + self.lanes(block)))

    def lanes(self, block):
        return LANES if self.spread else min(LANES, self.ref.shape[3] - block * LANES)

    def read(self, block, owned):
        return self.ref[self.place(block, owned)]

    def write(self, block, owned, value):
        self.ref[self.place(block, owned)] = value[:, : self.lanes(block)]


def lying(refs, rows, per_owner):
    blocks = [ref.shape[1] // rows // per_owner for ref in refs]
    blocks[1] = round_up(rows, LANES) // LANES
    return [Lying(ref, rows, per_owner, count) for ref, count in zip(refs, blocks)]


def half_kernel(rows, per_owner, *refs):
    moms, flat_ref = lying(refs[:3], rows, per_owner), refs[3]
    padded = round_up(rows, LANES)
    base = 0
    for mom in moms:
        for block in range(mom.blocks):
            begin = base * padded
            for owned in range(per_owner):
                flat_ref[owned, begin : begin + padded] = jnp.zeros((padded, LANES), F32)
                flat_ref[owned, begin : begin + rows, : mom.lanes(block)] = MOMENTUM * mom.read(block, owned)
            base += 1


def half_moments(moms, rows, per_owner, flat_rows):
    layers = moms[0].shape[0]
    return pl.pallas_call(
        functools.partial(half_kernel, rows, per_owner),
        grid=(layers,),
        in_specs=[at_step(mom.shape, 0) for mom in moms],
        out_specs=pl.BlockSpec((per_owner, flat_rows, LANES), lambda step: (step, 0, 0)),
        out_shape=shape_of((layers * per_owner, flat_rows, LANES), F32),
        compiler_params=params(),
        cost_estimate=cost(4e6, 14e6),
        name="half_moments",
    )(*moms)


def cast_kernel(rows, per_owner, mine_ref, *refs):
    olds, lows, scratches = lying(refs[:3], rows, per_owner), refs[3:6], refs[6:]
    for old, low, scratch in zip(olds, lows, scratches):
        scratch[rows:] = jnp.zeros((scratch.shape[0] - rows, scratch.shape[1]), F32)
        for block in range(old.blocks):
            scratch[:rows, block * LANES : (block + 1) * LANES] = old.read(block, mine_ref[0])
        low[0] = scratch[...].astype(BF16)


def cast_weights(mine, weights, rows, per_owner, width):
    layers = weights[0].shape[0]
    padded = round_up(rows, LANES)
    shapes = [(padded, blocks * LANES) for blocks in flat_blocks(width, padded)]
    layer_spec = lambda shape: pl.BlockSpec(
        (1,) + shape[1:], lambda step, mine: (step,) + (0,) * (len(shape) - 1)
    )
    return pl.pallas_call(
        functools.partial(cast_kernel, rows, per_owner),
        grid_spec=pltpu.PrefetchScalarGridSpec(
            num_scalar_prefetch=1,
            grid=(layers,),
            in_specs=[layer_spec(w.shape) for w in weights],
            out_specs=[layer_spec((layers,) + shape) for shape in shapes],
            scratch_shapes=[pltpu.VMEM(shape, F32) for shape in shapes],
        ),
        out_shape=[shape_of((layers,) + shape, BF16) for shape in shapes],
        compiler_params=params(),
        cost_estimate=cost(4e6, 11e6),
        name="cast_weights",
    )(mine, *weights)


def sum_kernel(*refs):
    total = refs[0][...].astype(F32)
    for ref in refs[1:-1]:
        total = total + ref[...].astype(F32)
    total = total.astype(BF16)
    for copy in range(refs[-1].shape[0]):
        refs[-1][copy] = total


def sum_arrays(parts, copies=1):
    shape = parts[0].shape
    return pl.pallas_call(
        sum_kernel,
        grid=(1,),
        in_specs=[whole(shape)] * len(parts),
        out_specs=whole((copies,) + shape),
        out_shape=shape_of((copies,) + shape, BF16),
        compiler_params=params(),
        cost_estimate=cost(1e6, 2e6),
        name="sum_arrays",
    )(*parts)


def join_kernel(slab_ref, *refs):
    *parts, whole_ref = refs
    rows = parts[0].shape[0]
    for shift, part in enumerate(parts):
        origin = lax.rem(slab_ref[0] - shift + len(parts), len(parts))
        whole_ref[pl.ds(pl.multiple_of(origin * rows, 16), rows), :] = part[...]


def join(slab, parts):
    rows, lanes = parts[0].shape
    shape = (rows * len(parts), lanes)
    return pl.pallas_call(
        join_kernel,
        grid_spec=pltpu.PrefetchScalarGridSpec(
            num_scalar_prefetch=1,
            grid=(1,),
            in_specs=[whole((rows, lanes))] * len(parts),
            out_specs=whole(shape),
        ),
        out_shape=shape_of(shape, BF16),
        compiler_params=params(),
        cost_estimate=cost(1e6, 2e6),
        name="join",
    )(slab, *parts)


def muon_kernel(rows, task_ref, half_ref, grad_ref, step_ref, eye_ref):
    padded = round_up(rows, LANES)
    eye_ref[...] = (iota(eye_ref.shape, 0) == iota(eye_ref.shape, 1)).astype(F32)
    base = 0
    values = []
    blocks = flat_blocks_of(half_ref.shape[1], padded)
    for count in blocks:
        parts = []
        for block in range(base, base + count):
            span = slice(block * padded, (block + 1) * padded)
            parts.append(half_ref[0, span] + grad_ref[span].astype(F32))
        base += count
        values.append(unit(jnp.concatenate(parts, axis=1)))
    for centre in NEWTON_CENTRES:
        values = [newton_step(value, which == 2, centre, eye_ref) for which, value in enumerate(values)]
    base = 0
    for count, value in zip(blocks, values):
        longest = rows if count == padded // LANES else max(count * LANES, rows)
        store_blocks(step_ref, base, value * (LEARNING_RATE * 0.2 * math.sqrt(longest)))
        base += count


def layer_of(values, layer):
    return pl.BlockSpec(
        (1,) + values.shape[1:], lambda step, *scalars: (layer,) + (0,) * (values.ndim - 1)
    )


def muon_step(task, grads, halves, rows):
    block = (1,) + halves.shape[1:]
    padded = round_up(rows, LANES)
    return pl.pallas_call(
        functools.partial(muon_kernel, rows),
        grid_spec=pltpu.PrefetchScalarGridSpec(
            num_scalar_prefetch=1,
            grid=(1,),
            in_specs=[pl.BlockSpec(block, lambda step, task: (task[0], 0, 0)), whole(grads.shape)],
            out_specs=whole(block[1:]),
            scratch_shapes=[pltpu.VMEM((padded, padded), F32)],
        ),
        out_shape=shape_of(block[1:], BF16),
        compiler_params=params(),
        cost_estimate=cost(7e9, 4e6),
        name="muon",
    )(task, halves, grads)


def apply_kernel(rows, per_owner, mine_ref, half_ref, *refs):
    steps, grads, weights = refs[:2], refs[2:4], lying(refs[4:7], rows, per_owner)
    new_moms, new_weights = lying(refs[-6:-3], rows, per_owner), lying(refs[-3:], rows, per_owner)
    mine = mine_ref[0]
    padded = round_up(rows, LANES)
    base = 0
    for weight, new_mom, new_weight in zip(weights, new_moms, new_weights):
        for block in range(weight.blocks):
            span = slice(base * padded, base * padded + rows)
            both_grads = [ref[span].astype(F32) for ref in grads]
            both_steps = [ref[span].astype(F32) for ref in steps]
            for owned in range(per_owner):
                grad = jnp.where(mine == owned, *both_grads)
                step = jnp.where(mine == owned, *both_steps)
                new_mom.write(block, owned, half_ref[owned, span] + grad)
                new_weight.write(block, owned, weight.read(block, owned) - step)
            base += 1


def apply_layer(mine, grads, steps, halves, weights, news, layer, rows, per_owner, partial=None):
    args = [mine, halves, *steps, *grads, *weights]
    in_specs = [pl.BlockSpec((per_owner,) + halves.shape[1:], lambda step, mine: (layer, 0, 0))]
    in_specs += [whole(value.shape) for value in (*steps, *grads)]
    in_specs += [layer_of(weight, layer) for weight in weights]
    aliases = {}
    if partial is not None:
        aliases = {len(args) + which: which for which in range(len(news))}
        args += list(partial)
        in_specs += [pl.BlockSpec(memory_space=pl.ANY)] * len(news)
    return pl.pallas_call(
        functools.partial(apply_kernel, rows, per_owner),
        grid_spec=pltpu.PrefetchScalarGridSpec(
            num_scalar_prefetch=1,
            grid=(1,),
            in_specs=in_specs,
            out_specs=[layer_of(new, layer) for new in news],
        ),
        out_shape=[shape_of(new.shape, F32) for new in news],
        input_output_aliases=aliases,
        compiler_params=params(),
        cost_estimate=cost(2e6, 18e6),
        name="apply_layer",
    )(*args)


def small_kernel(count_parts, *refs):
    parts, refs = refs[:count_parts], refs[count_parts:]
    radial_ref, radial_mom_ref, mixing_ref, mixing_mom_ref, *outs = refs
    new_radial_ref, new_radial_mom_ref, new_mixing_ref, new_mixing_mom_ref = outs
    layers, shells, width = radial_ref.shape
    channels = mixing_ref.shape[1]
    values = []
    total = parts[0][...].astype(F32)
    for part in parts[1:]:
        total = total + part[...].astype(F32)
    each = total.shape[0] // layers
    for layer in range(layers):
        total_here = total[layer * each : (layer + 1) * each]
        moment = MOMENTUM * radial_mom_ref[layer] + total_here[:shells]
        new_radial_mom_ref[layer] = moment
        values.append(unit(moment))
        moment = eight_rows(MOMENTUM * mixing_mom_ref[layer]) + total_here[shells:]
        new_mixing_mom_ref[layer] = moment[:channels]
        values.append(unit(moment))
    for _ in NEWTON_CENTRES:
        grams = [dot(value, value, NT, EXACT) for value in values]
        polys = [NEWTON_B * gram + NEWTON_C * dot(gram, gram, NN, EXACT) for gram in grams]
        values = [NEWTON_A * value + dot(poly, value, NN, EXACT) for value, poly in zip(values, polys)]
    for layer in range(layers):
        lift = LEARNING_RATE * 0.2 * math.sqrt(max(shells, width))
        new_radial_ref[layer] = radial_ref[layer] - lift * values[2 * layer]
        lift = LEARNING_RATE * 0.2 * math.sqrt(max(channels, width))
        new_mixing_ref[layer] = mixing_ref[layer] - lift * values[2 * layer + 1][:channels]


def small_step(parts, radial, radial_mom, mixing, mixing_mom):
    args = (*parts, radial, radial_mom, mixing, mixing_mom)
    outs = [radial, radial_mom, mixing, mixing_mom]
    return pl.pallas_call(
        functools.partial(small_kernel, len(parts)),
        grid=(1,),
        in_specs=[whole(arg.shape) for arg in args],
        out_specs=[whole(out.shape) for out in outs],
        out_shape=[shape_of(out.shape, F32) for out in outs],
        compiler_params=params(),
        cost_estimate=cost(1e8, 3e6),
        name="small_step",
    )(*args)


EVERY = ("slab", "pair", "elem")
HOLDERS = ("pair", "elem")


def swap(values):
    return lax.all_to_all(values, HOLDERS, split_axis=0, concat_axis=0, tiled=True)


def to_both_sides(to_left, to_right):
    count = lax.axis_size(EVERY)
    up = [(i, (i + 1) % count) for i in range(count)]
    down = [((i + 1) % count, i) for i in range(count)]
    return lax.ppermute(to_right, EVERY, up), lax.ppermute(to_left, EVERY, down)


def other_of_pair(values):
    return lax.ppermute(values, "pair", [(0, 1), (1, 0)])


def shifted(values, shift, axis):
    count = lax.axis_size(axis)
    return lax.ppermute(values, axis, [(i, (i + shift) % count) for i in range(count)])


def exchange(pieces, axis="slab"):
    return [piece if shift == 0 else shifted(piece, shift, axis) for shift, piece in enumerate(pieces)]


def to_all(piece, axis="slab"):
    return exchange([piece] * lax.axis_size(axis), axis)


def on_device(
    features,
    charges,
    elements,
    neighbours,
    counts,
    distances,
    radial,
    radial_mom,
    mixing,
    mixing_mom,
    w_in,
    w_mid,
    w_out,
    mom_in,
    mom_mid,
    mom_out,
    cot_features,
    cot_charges,
):
    batches, atoms, width = features.shape
    per_owner, hidden_width = w_in.shape[1], w_in.shape[3]
    owners = lax.axis_size("elem")
    shells = radial.shape[1]
    holders = per_owner * owners
    cap = 2 * atoms // holders
    rim = atoms // 8
    sizes = (owners, per_owner, cap)
    by_rows = (holders, 1, batches * cap, width)
    by_atom = (holders, 1, batches, cap, width)
    barrier = lax.optimization_barrier
    mine = lax.axis_index("pair").astype(jnp.int32)[None]
    slab = lax.axis_index("slab").astype(jnp.int32)[None]
    slabs = lax.axis_size("slab")
    padded = round_up(hidden_width, LANES)
    flat_rows = sum(flat_blocks(width, padded)) * padded
    piece = round_up(-(-flat_rows // slabs), 16)

    place, place_t, packed, source, first, last = start(
        elements, features, charges, cot_features, cot_charges, mixing, rim, sizes
    )
    arrived = swap(packed).reshape(holders, 2, batches * cap, width)
    left, right = to_both_sides(first, last)
    band, band_t = make_bands(distances, neighbours, counts, shells, rim)
    old_weights = [native(w, which) for which, w in enumerate((w_in, w_mid, w_out))]
    old_moms = [native(m, which, False) for which, m in enumerate((mom_in, mom_mid, mom_out))]
    weights = cast_weights(mine, old_weights, hidden_width, per_owner, width)

    message = edge_forward(source, left, right, band, radial, 0, place, sizes)
    message, arrived = barrier((message, arrived))
    message = swap(message).reshape(by_rows)
    result, pre_one, pre_two = network_forward(arrived, message, weights, 0)
    back, halves = barrier(
        (swap(result).reshape(by_atom), half_moments(old_moms, hidden_width, per_owner, flat_rows))
    )
    hidden_one, charge_one, source_one, first, last = update_atoms(
        back, 0, place_t, features, charges, mixing, 1, rim
    )

    left_one, right_one = to_both_sides(first, last)
    message_one = edge_forward(source_one, left_one, right_one, band, radial, 1, place, sizes)
    message_one = swap(message_one).reshape(by_rows)
    result_one, rows_one, grad_hidden, grad_message, *saved = network_turn(
        arrived, result, message_one, weights, 1
    )
    grad_message = swap(grad_message).reshape(by_atom)
    pieces = weight_grad(slab, rows_one, message_one, arrived, 1, saved, (piece, LANES), slabs)
    grad_message, grad_hidden, pieces = barrier((grad_message, grad_hidden, pieces))
    grad_hidden = swap(grad_hidden).reshape(by_atom)
    pieces_one = exchange(pieces)
    inner, to_left, to_right, radial_grad = edge_backward(
        grad_message, place_t, source_one, left_one, right_one, band, band_t, radial, 1
    )
    to_left, to_right, pieces_one[1] = barrier((to_left, to_right, pieces_one[1]))
    from_left, from_right = to_both_sides(to_left, to_right)
    from_left, pieces_one[-1] = barrier((from_left, pieces_one[-1]))
    grad, grad_charge, small_one, packed = finish(
        inner, from_left, from_right, grad_hidden, place_t, cot_features, cot_charges, charge_one,
        mixing, 1, radial_grad, place,
    )

    grad_update = swap(packed).reshape(by_rows)
    grad_update, piece_one = barrier((grad_update, sum_arrays(pieces_one)[0]))
    totals_one = to_all(piece_one)
    grad_message, both, *saved = network_backward(grad_update, pre_one, pre_two, result_one, weights, 0)
    grad_message, totals_one[1] = barrier((grad_message, totals_one[1]))
    grad_message = swap(grad_message).reshape(by_atom)
    pieces = weight_grad(slab, arrived, message, grad_update, 0, saved, (piece, LANES), slabs)
    grad_message, both, pieces, totals_one = barrier((grad_message, both, pieces, totals_one))
    pieces_zero = exchange(pieces)
    both = swap(both).reshape(holders, 2, batches, cap, width)
    inner, to_left, to_right, radial_grad = edge_backward(
        grad_message, place_t, source, left, right, band, band_t, radial, 0
    )
    total_one, pieces_zero[1], inner = barrier((join(slab, totals_one), pieces_zero[1], inner))
    from_left, from_right = to_both_sides(to_left, to_right)
    task = lambda layer: layer * per_owner + mine
    step = muon_step(task(1), total_one, halves, hidden_width)
    pieces_zero, from_left, from_right, _ = barrier((pieces_zero, from_left, from_right, step))
    step, other_one = barrier((step, other_of_pair(total_one)))
    steps_one = (step, other_of_pair(step))
    copies, from_left = barrier((sum_arrays(pieces_zero, slabs), from_left))
    total_zero = lax.all_to_all(copies, "slab", split_axis=0, concat_axis=0, tiled=True)
    total_zero = total_zero.reshape(slabs * piece, LANES)
    grad_features, grad_charges, smalls, features_out, charges_out = finish(
        inner, from_left, from_right, both, place_t, grad, grad_charge, charges, mixing, 0, radial_grad,
        last=(small_one, hidden_one, charge_one),
    )
    (smalls,) = sum_arrays(to_all(smalls, "elem"))
    total_zero, steps_one, smalls = barrier((total_zero, steps_one, smalls))
    news = [native(jnp.zeros(m.shape, F32), which, False) for which, m in enumerate((mom_in, mom_mid, mom_out))]
    news = [shape_of(new.shape, F32) for new in news] * 2
    sizes = (hidden_width, per_owner)
    done = apply_layer(mine, (total_one, other_one), steps_one, halves, old_weights, news, 1, *sizes)
    step = muon_step(task(0), total_zero, halves, hidden_width)
    step, other, smalls, done = barrier((step, other_of_pair(total_zero), to_all(smalls), done))
    steps = (step, other_of_pair(step))
    (smalls,) = sum_arrays(smalls)
    new_radial, new_radial_mom, new_mixing, new_mixing_mom = small_step(
        (smalls, other_of_pair(smalls)), radial, radial_mom, mixing, mixing_mom
    )
    done = apply_layer(mine, (total_zero, other), steps, halves, old_weights, news, 0, *sizes, done)
    news = [from_native(value, which % 3, per_owner, hidden_width) for which, value in enumerate(done)]
    return (
        features_out,
        charges_out,
        grad_features,
        grad_charges,
        *news[3:],
        *news[:3],
        new_radial,
        new_radial_mom,
        new_mixing,
        new_mixing_mom,
    )


def solution(mesh):
    in_specs = (
        P(None, EVERY, None),
        P(None, None, EVERY),
        P(None, EVERY),
        P(None, None, EVERY),
        P(None, EVERY),
        P(None, None, EVERY),
        P(),
        P(),
        P(),
        P(),
        P(None, "elem", None, None),
        P(None, "elem", None, None),
        P(None, "elem", None, None),
        P(None, "elem", None, None),
        P(None, "elem", None, None),
        P(None, "elem", None, None),
        P(None, EVERY, None),
        P(None, None, EVERY),
    )
    out_specs = (
        P(None, EVERY, None),
        P(None, None, EVERY),
        P(None, EVERY, None),
        P(None, None, EVERY),
        P(None, "elem", None, None),
        P(None, "elem", None, None),
        P(None, "elem", None, None),
        P(None, "elem", None, None),
        P(None, "elem", None, None),
        P(None, "elem", None, None),
        P(),
        P(),
        P(),
        P(),
    )
    devices = mesh.devices
    folded = jax.sharding.Mesh(devices.reshape(devices.shape[0] // 2, 2, devices.shape[1]), EVERY)
    return jax.shard_map(
        on_device, mesh=folded, in_specs=in_specs, out_specs=out_specs, check_vma=False
    )
```

```python
import functools
import math

import jax
import jax.numpy as jnp
from jax import lax
from jax.experimental import pallas as pl
from jax.experimental.pallas import tpu as pltpu
from jax.sharding import PartitionSpec as P

EXACT = lax.Precision.HIGHEST
SHELL_START = 0.8
SHELL_SPACING = 0.28
SHELL_SHARPNESS = 8.0
CUTOFF_RADIUS = 5.0
MOMENTUM = 0.5
LEARNING_RATE = 0.25
NEWTON_A = 3.4445
NEWTON_B = -4.775
NEWTON_C = 2.0315
NEWTON_CENTRES = (0.0, 0.0, 0.5, 1.0, 1.0)
QUARTERS = 4
GROUP = 8
SOURCES = 2
LANES = 128
FAR = 100.0
VMEM_BYTES = 60 * 1024 * 1024
F32 = jnp.float32
BF16 = jnp.bfloat16
NN = (((1,), (0,)), ((), ()))
NT = (((1,), (1,)), ((), ()))
TN = (((0,), (0,)), ((), ()))


def dot(left, right, dims, precision=None):
    return lax.dot_general(left, right, dims, precision=precision, preferred_element_type=F32)


def iota(shape, dim):
    return lax.broadcasted_iota(jnp.int32, shape, dim)


def round_up(size, multiple):
    return -(-size // multiple) * multiple


def params():
    return pltpu.CompilerParams(vmem_limit_bytes=VMEM_BYTES)


def cost(flops, read_bytes):
    return pl.CostEstimate(flops=int(flops), bytes_accessed=int(read_bytes), transcendentals=0)


def shape_of(shape, dtype):
    return jax.ShapeDtypeStruct(shape, dtype)


def at_step(shape, axis):
    block = tuple(1 if dim == axis else size for dim, size in enumerate(shape))
    return pl.BlockSpec(block, lambda step: tuple(step if dim == axis else 0 for dim in range(len(shape))))


def whole(shape):
    return pl.BlockSpec(shape, lambda *step: (0,) * len(shape))


def columns(rows):
    count, atoms = rows.shape
    return jnp.concatenate([rows, jnp.zeros((LANES - count, atoms), F32)], axis=0).T


def eight_rows(rows):
    return jnp.concatenate([rows, jnp.zeros((8 - rows.shape[0], rows.shape[1]), F32)], axis=0)


def add_columns(values, first):
    return jnp.concatenate([values[:, :LANES] + first, values[:, LANES:]], axis=1)


def source_of(hidden, charge_cols, mixing, channels):
    for channel in range(channels):
        hidden = hidden + charge_cols[:, channel : channel + 1] * mixing[channel : channel + 1, :]
    return hidden.astype(BF16)


def store_source(source, source_ref, first_ref, last_ref):
    rim = first_ref.shape[1]
    source_ref[0] = source
    first_ref[0] = source[:rim]
    last_ref[0] = source[source.shape[0] - rim :]


def atom_spec(values, which=0):
    holders, _, _, cap, width = values.shape
    return pl.BlockSpec((holders, 1, 1, cap, width), lambda step: (0, which, step, 0, 0))


def start_kernel(
    sizes, elem_ref, feat_ref, charge_ref, cotf_ref, cotc_ref, mixing_ref,
    place_ref, place_t_ref, packed_ref, source_ref, first_ref, last_ref,
):
    owners, per_owner, cap = sizes
    slots, atoms = place_ref.shape[1:]
    channels = charge_ref.shape[1]
    row = elem_ref[pl.ds(pl.program_id(0), 1), :]
    before = iota((atoms, atoms), 0)
    after = iota((atoms, atoms), 1)
    hot = (iota((LANES, atoms), 0) == row).astype(F32)
    rank = dot(hot.astype(BF16), (before < after).astype(F32).astype(BF16), NN)
    rank = jnp.sum(rank * hot, axis=0, keepdims=True)
    holder = lax.rem(row, per_owner) * owners + lax.div(row, per_owner)
    slot = holder.astype(F32) * cap + rank
    place = (iota((slots, atoms), 0) == slot.astype(jnp.int32)).astype(F32).astype(BF16)
    slot_t = jnp.broadcast_to(slot, (LANES, atoms)).T[:, :1].astype(jnp.int32)
    place_t = (iota((atoms, slots), 1) == slot_t).astype(F32).astype(BF16)
    place_ref[0] = place
    place_t_ref[0] = place_t
    features = feat_ref[0]
    grad = add_columns(cotf_ref[0].astype(F32), columns(cotc_ref[0])).astype(BF16)
    holders, _, _, _, width = packed_ref.shape
    for which, values in enumerate((features, grad)):
        packed = dot(place, values, NN).astype(BF16)
        packed_ref[:, which] = packed.reshape(holders, 1, cap, width)
    store_source(
        source_of(features.astype(F32), columns(charge_ref[0]), mixing_ref[0], channels),
        source_ref, first_ref, last_ref,
    )


def start(elements, features, charges, cot_features, cot_charges, mixing, rim, sizes):
    batches, atoms, width = features.shape
    owners, per_owner, cap = sizes
    holders = owners * per_owner
    packed_shape = (holders, 2, batches, cap, width)
    args = (elements, features, charges, cot_features, cot_charges, mixing)
    outs = (
        shape_of((batches, holders * cap, atoms), BF16),
        shape_of((batches, atoms, holders * cap), BF16),
        shape_of(packed_shape, BF16),
        shape_of((batches, atoms, width), BF16),
        shape_of((batches, rim, width), BF16),
        shape_of((batches, rim, width), BF16),
    )
    return pl.pallas_call(
        functools.partial(start_kernel, sizes),
        grid=(batches,),
        in_specs=[whole(elements.shape)]
        + [at_step(arg.shape, 0) for arg in args[1:-1]]
        + [whole(mixing.shape)],
        out_specs=[
            at_step(outs[0].shape, 0),
            at_step(outs[1].shape, 0),
            at_step(packed_shape, 2),
        ]
        + [at_step(out.shape, 0) for out in outs[3:]],
        out_shape=outs,
        compiler_params=params(),
        cost_estimate=cost(6e8, 8e6),
        name="start",
    )(*args)


def bands_kernel(shells, dist_ref, near_ref, band_ref, band_t_ref):
    groups, pairs = dist_ref.shape[1:]
    slots = pairs // GROUP
    per_quarter = groups // QUARTERS
    window = band_ref.shape[2]
    rows = shells * GROUP
    sub = iota((GROUP, pairs), 0)
    lane = iota((GROUP, pairs), 1)
    own = ((lane >= sub * slots) & (lane < (sub + 1) * slots)).astype(F32)
    centres = SHELL_START + SHELL_SPACING * iota((shells, 1), 0).astype(F32)
    target = iota((window, pairs), 0)
    distance_all = dist_ref[0]
    envelope_all = 0.5 * (jnp.cos(math.pi * distance_all / CUTOFF_RADIUS) + 1.0)
    for group in range(groups):
        distance = distance_all[group : group + 1]
        spread = distance - centres
        basis = jnp.exp(-SHELL_SHARPNESS * spread * spread) * envelope_all[group : group + 1]
        spaced = (basis[:, None, :] * own[None]).reshape(rows, pairs).astype(BF16)
        hot = (target == near_ref[0, group : group + 1, :]).astype(F32).astype(BF16)
        band_ref[0, group * rows : (group + 1) * rows, :] = dot(spaced, hot, NT).astype(BF16)
        quarter, inner = group // per_quarter, group % per_quarter
        band_t_ref[0, quarter, :, inner * rows : (inner + 1) * rows] = dot(hot, spaced, NT).astype(BF16)


def make_bands(distances, neighbours, counts, shells, rim):
    batches, slots, atoms = distances.shape
    groups = atoms // GROUP
    block = atoms // QUARTERS
    window = block + 2 * rim
    live = iota(distances.shape, 1) < counts[:, None, :]
    distance = jnp.where(live, distances, FAR)
    local = neighbours - (iota(neighbours.shape, 2) // block) * block

    def grouped(values):
        return jnp.transpose(values, (0, 2, 1)).reshape(batches, groups, GROUP * slots)

    args = (grouped(distance), grouped(local))
    rows = shells * GROUP
    outs = (
        shape_of((batches, groups * rows, window), BF16),
        shape_of((batches, QUARTERS, window, groups // QUARTERS * rows), BF16),
    )
    return pl.pallas_call(
        functools.partial(bands_kernel, shells),
        grid=(batches,),
        in_specs=[at_step(arg.shape, 0) for arg in args],
        out_specs=[at_step(out.shape, 0) for out in outs],
        out_shape=outs,
        compiler_params=params(),
        cost_estimate=cost(3e9, 8e6),
        name="bands",
    )(*args)


def edge_forward_kernel(source_ref, left_ref, right_ref, band_ref, radial_ref, place_ref, packed_ref):
    atoms, width = source_ref.shape[1:]
    shells = radial_ref.shape[1]
    rim = left_ref.shape[1]
    block = atoms // QUARTERS
    window = block + 2 * rim
    per_quarter = block // GROUP
    extended = jnp.concatenate([left_ref[0], source_ref[0], right_ref[0]], axis=0)
    radial = jnp.broadcast_to(radial_ref[0][:, None, :], (shells, GROUP, width))
    rows = block * shells
    pieces = []
    for quarter in range(QUARTERS):
        near = extended[quarter * block : quarter * block + window]
        sums = dot(band_ref[0, quarter * rows : (quarter + 1) * rows, :], near, NN)
        sums = sums.reshape(per_quarter, shells, GROUP, width) * radial[None]
        pieces.append(jnp.sum(sums, axis=1).reshape(block, width))
    message = jnp.concatenate(pieces, axis=0).astype(BF16)
    packed = dot(place_ref[0], message, NN).astype(BF16)
    packed_ref[...] = packed.reshape(packed_ref.shape)


def edge_forward(source, left, right, band, radial, layer, place, sizes):
    batches, atoms, width = source.shape
    owners, per_owner, cap = sizes
    packed_shape = (owners * per_owner, 1, batches, cap, width)
    return pl.pallas_call(
        edge_forward_kernel,
        grid=(batches,),
        in_specs=[at_step(arg.shape, 0) for arg in (source, left, right, band)]
        + [pl.BlockSpec((1,) + radial.shape[1:], lambda step: (layer, 0, 0)), at_step(place.shape, 0)],
        out_specs=at_step(packed_shape, 2),
        out_shape=shape_of(packed_shape, BF16),
        compiler_params=params(),
        cost_estimate=cost(1.2e9, 6e6),
        name="edge_forward",
    )(source, left, right, band, radial, place)


def edge_backward_kernel(
    grad_ref, place_t_ref, source_ref, left_ref, right_ref, band_ref, band_t_ref, radial_ref,
    inner_ref, to_left_ref, to_right_ref, radial_grad_ref, total,
):
    atoms, width = source_ref.shape[1:]
    shells = radial_ref.shape[1]
    rim = left_ref.shape[1]
    block = atoms // QUARTERS
    window = block + 2 * rim
    per_quarter = block // GROUP
    rows = block * shells
    step = pl.program_id(0)
    slots = place_t_ref.shape[2]
    grad = dot(place_t_ref[0], grad_ref[...].reshape(slots, width), NN)
    extended = jnp.concatenate([left_ref[0], source_ref[0], right_ref[0]], axis=0)
    radial = jnp.broadcast_to(radial_ref[0][:, None, :], (shells, GROUP, width))
    total[...] = jnp.zeros_like(total)
    radial_sum = jnp.zeros((shells, GROUP, width), F32)
    for quarter in range(QUARTERS):
        near = extended[quarter * block : quarter * block + window]
        sums = dot(band_ref[0, quarter * rows : (quarter + 1) * rows, :], near, NN)
        piece = grad[quarter * block : (quarter + 1) * block].reshape(per_quarter, 1, GROUP, width)
        radial_sum = radial_sum + jnp.sum(
            sums.reshape(per_quarter, shells, GROUP, width) * piece, axis=0
        )
        scaled = (radial[None] * piece).reshape(rows, width).astype(BF16)
        total[quarter * block : quarter * block + window] += dot(band_t_ref[0, quarter], scaled, NN)
    inner_ref[0] = total[rim : rim + atoms]
    to_left_ref[0] = total[:rim].astype(BF16)
    to_right_ref[0] = total[rim + atoms :].astype(BF16)
    radial_here = jnp.sum(radial_sum, axis=1)

    @pl.when(step == 0)
    def _():
        radial_grad_ref[...] = radial_here

    @pl.when(step > 0)
    def _():
        radial_grad_ref[...] += radial_here


def edge_backward(grad, place_t, source, left, right, band, band_t, radial, layer):
    batches, atoms, width = source.shape
    rim = left.shape[1]
    shells = radial.shape[1]
    outs = (
        shape_of((batches, atoms, width), F32),
        shape_of(left.shape, BF16),
        shape_of(left.shape, BF16),
        shape_of((shells, width), F32),
    )
    return pl.pallas_call(
        edge_backward_kernel,
        grid=(batches,),
        in_specs=[atom_spec(grad), at_step(place_t.shape, 0)]
        + [at_step(arg.shape, 0) for arg in (source, left, right, band, band_t)]
        + [pl.BlockSpec((1,) + radial.shape[1:], lambda step: (layer, 0, 0))],
        out_specs=[at_step(out.shape, 0) for out in outs[:3]] + [whole(outs[3].shape)],
        out_shape=outs,
        scratch_shapes=[pltpu.VMEM((atoms + 2 * rim, width), F32)],
        compiler_params=params(),
        cost_estimate=cost(2.5e9, 10e6),
        name="edge_backward",
    )(grad, place_t, source, left, right, band, band_t, radial)


def update_kernel(back_ref, place_t_ref, hidden_ref, charge_ref, *rest):
    mixing_ref, hidden_out_ref, charge_out_ref, *sources = rest if len(rest) > 2 else (None, *rest)
    slots, width = place_t_ref.shape[2], hidden_ref.shape[2]
    channels = charge_ref.shape[1]
    update = dot(place_t_ref[0], back_ref[...].reshape(slots, width), NN)
    hidden = hidden_ref[0].astype(F32) + update
    charge = charge_ref[0] + update[:, :LANES].T[:channels]
    hidden_out_ref[0] = hidden
    charge_out_ref[0] = charge
    if sources:
        store_source(source_of(hidden, columns(charge), mixing_ref[0], channels), *sources)


def update_atoms(back, which, place_t, hidden, charge, mixing=None, layer=0, rim=0):
    batches, atoms, width = hidden.shape
    outs = [shape_of((batches, atoms, width), F32), shape_of(charge.shape, F32)]
    args = [back, place_t, hidden, charge]
    specs = [atom_spec(back, which)] + [at_step(arg.shape, 0) for arg in args[1:]]
    if mixing is not None:
        args.append(mixing)
        specs.append(pl.BlockSpec((1,) + mixing.shape[1:], lambda step: (layer, 0, 0)))
        outs += [shape_of((batches, rows, width), BF16) for rows in (atoms, rim, rim)]
    return pl.pallas_call(
        update_kernel,
        grid=(batches,),
        in_specs=specs,
        out_specs=[at_step(out.shape, 0) for out in outs],
        out_shape=outs,
        compiler_params=params(),
        cost_estimate=cost(2e8, 4e6),
        name="update_atoms",
    )(*args)


def finish_kernel(
    repack, inner_ref, from_left_ref, from_right_ref, back_ref, place_t_ref, grad_ref, grad_charge_ref,
    charge_ref, mixing_ref, radial_grad_ref, *rest,
):
    if repack:
        place_ref, grad_out_ref, charge_out_ref, small_ref, packed_ref = rest
    else:
        earlier_ref, late_ref, hidden_ref, late_charge_ref, *rest = rest
        grad_out_ref, charge_out_ref, joined_ref, hidden_out_ref, late_charge_out_ref, small_ref = rest
    atoms, width = inner_ref.shape[1:]
    rim = from_left_ref.shape[1]
    channels = charge_ref.shape[1]
    slots = place_t_ref.shape[2]
    shells = radial_grad_ref.shape[0]
    step = pl.program_id(0)
    inner = inner_ref[0]
    source_grad = jnp.concatenate(
        [
            inner[:rim] + from_left_ref[0].astype(F32),
            inner[rim : atoms - rim],
            inner[atoms - rim :] + from_right_ref[0].astype(F32),
        ],
        axis=0,
    )
    mixing_grad = dot(eight_rows(charge_ref[0]), source_grad, NN, EXACT)
    charge_term = dot(eight_rows(mixing_ref[0]), source_grad, NT, EXACT)
    joined = dot(place_t_ref[0], back_ref[...].reshape(slots, width), NN)
    grad = grad_ref[0].astype(F32) + joined + source_grad
    grad_charge = grad_charge_ref[0] + charge_term[:channels]
    grad_out_ref[0] = grad
    charge_out_ref[0] = grad_charge

    @pl.when(step == 0)
    def _():
        small_ref[:shells] = radial_grad_ref[...]
        small_ref[shells:] = mixing_grad

    @pl.when(step > 0)
    def _():
        small_ref[shells:] += mixing_grad

    if not repack:
        update = dot(place_t_ref[0], late_ref[...].reshape(slots, width), NN)
        hidden_out_ref[0] = hidden_ref[0] + update
        late_charge_out_ref[0] = late_charge_ref[0] + update[:, :LANES].T[:channels]

        @pl.when(step == pl.num_programs(0) - 1)
        def _():
            joined_ref[...] = jnp.concatenate([small_ref[...], earlier_ref[...]], axis=0).astype(BF16)

    else:
        sent = add_columns(grad, columns(grad_charge)).astype(BF16)
        packed = dot(place_ref[0], sent, NN).astype(BF16)
        packed_ref[...] = packed.reshape(packed_ref.shape)


def finish(inner, from_left, from_right, back, place_t, grad, grad_charge, charge, mixing, layer, radial_grad, place=None, last=None):
    batches, atoms, width = inner.shape
    args = [inner, from_left, from_right, back, place_t, grad, grad_charge, charge, mixing, radial_grad]
    specs = [at_step(arg.shape, 0) for arg in args]
    specs[3] = atom_spec(back)
    specs[8] = pl.BlockSpec((1,) + mixing.shape[1:], lambda step: (layer, 0, 0))
    specs[9] = whole(radial_grad.shape)
    small = (radial_grad.shape[0] + 8, width)
    outs = [shape_of(inner.shape, F32), shape_of(charge.shape, F32), shape_of(small, F32)]
    out_specs = [at_step(outs[0].shape, 0), at_step(outs[1].shape, 0), whole(small)]
    scratch = []
    if place is None:
        earlier, hidden, late_charge = last
        args += [earlier, back, hidden, late_charge]
        specs += [whole(earlier.shape), atom_spec(back, 1), at_step(hidden.shape, 0), at_step(charge.shape, 0)]
        joined = (small[0] + earlier.shape[0], width)
        outs[2], out_specs[2] = shape_of(joined, BF16), whole(joined)
        outs += outs[:2]
        out_specs += out_specs[:2]
        scratch.append(pltpu.VMEM(small, F32))
    else:
        args.append(place)
        specs.append(at_step(place.shape, 0))
        outs.append(shape_of(back.shape[:1] + (1,) + back.shape[2:], BF16))
        out_specs.append(atom_spec(back))
    return pl.pallas_call(
        functools.partial(finish_kernel, place is not None),
        grid=(batches,),
        in_specs=specs,
        out_specs=out_specs,
        out_shape=outs,
        scratch_shapes=scratch,
        compiler_params=params(),
        cost_estimate=cost(6e8, 6e6),
        name="finish",
    )(*args)


def gelu_parts(value):
    scale = math.sqrt(2.0 / math.pi)
    square = value * value
    bent = jnp.tanh(scale * (value + 0.044715 * value * square))
    half = 0.5 * (1.0 + bent)
    slope = half + 0.5 * value * (1.0 - bent * bent) * scale * (1.0 + 3.0 * 0.044715 * square)
    return value * half, slope


def rows_spec(values, which=0, sources=SOURCES):
    _, _, rows, width = values.shape
    return pl.BlockSpec((sources, 1, rows, width), lambda step: (step, which, 0, 0))


def saved_spec(shape, steps):
    return pl.BlockSpec((shape[0] // steps, shape[1]), lambda step: (step, 0))


def weight_specs(weights, layer):
    return [pl.BlockSpec((1,) + w.shape[1:], lambda step: (layer, 0, 0)) for w in weights]


def forward_through(hidden, message, first_ref, middle_ref, last_ref):
    width = hidden.shape[1]
    pre_one = dot(hidden, first_ref[0, :, :width], NT) + dot(message, first_ref[0, :, width:], NT)
    act_one = gelu_parts(pre_one)[0].astype(BF16)
    pre_two = dot(act_one, middle_ref[0], NN)
    act_two = gelu_parts(pre_two)[0].astype(BF16)
    return dot(act_two, last_ref[0], NN).astype(BF16), pre_one, pre_two


def back_through(grad, pre_one, pre_two, first_ref, middle_ref, last_ref, span, outs):
    width = grad.shape[1]
    act_one_ref, act_two_ref, grad_one_ref, grad_two_ref = outs
    act_one, slope_one = gelu_parts(pre_one)
    act_two, slope_two = gelu_parts(pre_two)
    act_one_ref[span] = act_one.astype(BF16)
    act_two_ref[span] = act_two.astype(BF16)
    grad_two = (slope_two * dot(grad, last_ref[0], NT)).astype(BF16)
    grad_two_ref[span] = grad_two
    grad_one = (slope_one * dot(grad_two, middle_ref[0], NT)).astype(BF16)
    grad_one_ref[span] = grad_one
    return (
        dot(grad_one, first_ref[0, :, :width], NN).astype(BF16),
        dot(grad_one, first_ref[0, :, width:], NN).astype(BF16),
    )


def network_forward_kernel(
    feat_ref, message_ref, first_ref, middle_ref, last_ref, result_ref, pre_one_ref, pre_two_ref
):
    sources, _, rows, _ = feat_ref.shape
    for source in range(sources):
        span = slice(source * rows, (source + 1) * rows)
        result_ref[source, 0], pre_one_ref[span], pre_two_ref[span] = forward_through(
            feat_ref[source, 0], message_ref[source, 0], first_ref, middle_ref, last_ref
        )


def network_forward(arrived, message, weights, layer):
    holders, _, rows, width = message.shape
    steps = holders // SOURCES
    saved = (holders * rows, weights[1].shape[1])
    return pl.pallas_call(
        network_forward_kernel,
        grid=(steps,),
        in_specs=[rows_spec(arrived), rows_spec(message)] + weight_specs(weights, layer),
        out_specs=[rows_spec(message)] + [saved_spec(saved, steps)] * 2,
        out_shape=(shape_of(message.shape, BF16), shape_of(saved, F32), shape_of(saved, F32)),
        compiler_params=params(),
        cost_estimate=cost(1.4e9, 8e6),
        name="network_forward",
    )(arrived, message, *weights)


def network_turn_kernel(
    feat_ref, result_ref, message_ref, grad_ref, first_ref, middle_ref, last_ref,
    result_out_ref, rows_ref, grad_hidden_ref, grad_message_ref, *saved,
):
    sources, _, rows, _ = feat_ref.shape
    for source in range(sources):
        span = slice(source * rows, (source + 1) * rows)
        hidden = feat_ref[source, 0].astype(F32) + result_ref[source, 0].astype(F32)
        hidden = hidden.astype(BF16)
        rows_ref[source, 0] = hidden
        result_out_ref[source, 0], pre_one, pre_two = forward_through(
            hidden, message_ref[source, 0], first_ref, middle_ref, last_ref
        )
        grad_hidden_ref[source, 0], grad_message_ref[source, 0] = back_through(
            grad_ref[source, 0], pre_one, pre_two, first_ref, middle_ref, last_ref, span, saved
        )


def network_turn(arrived, result, message, weights, layer):
    holders, _, rows, width = message.shape
    steps = holders // SOURCES
    saved = (holders * rows, weights[1].shape[1])
    spec = rows_spec(message)
    return pl.pallas_call(
        network_turn_kernel,
        grid=(steps,),
        in_specs=[rows_spec(arrived), spec, spec, rows_spec(arrived, 1)] + weight_specs(weights, layer),
        out_specs=[spec] * 4 + [saved_spec(saved, steps)] * 4,
        out_shape=[shape_of(message.shape, BF16)] * 4 + [shape_of(saved, BF16)] * 4,
        compiler_params=params(),
        cost_estimate=cost(2.8e9, 12e6),
        name="network_turn",
    )(arrived, result, message, arrived, *weights)


def network_backward_kernel(
    grad_ref, pre_one_ref, pre_two_ref, late_ref, first_ref, middle_ref, last_ref,
    grad_message_ref, both_ref, *saved,
):
    sources, _, rows, _ = grad_ref.shape
    both_ref[:, 1] = late_ref[:, 0]
    for source in range(sources):
        span = slice(source * rows, (source + 1) * rows)
        both_ref[source, 0], grad_message_ref[source, 0] = back_through(
            grad_ref[source, 0], pre_one_ref[span], pre_two_ref[span],
            first_ref, middle_ref, last_ref, span, saved,
        )


def network_backward(grad, pre_one, pre_two, late, weights, layer):
    holders, _, rows, width = grad.shape
    steps = holders // SOURCES
    saved = pre_one.shape
    spec = rows_spec(grad)
    both = pl.BlockSpec((SOURCES, 2, rows, width), lambda step: (step, 0, 0, 0))
    return pl.pallas_call(
        network_backward_kernel,
        grid=(steps,),
        in_specs=[spec] + [saved_spec(saved, steps)] * 2 + [spec] + weight_specs(weights, layer),
        out_specs=[spec, both] + [saved_spec(saved, steps)] * 4,
        out_shape=[shape_of(grad.shape, BF16), shape_of((holders, 2, rows, width), BF16)]
        + [shape_of(saved, BF16)] * 4,
        compiler_params=params(),
        cost_estimate=cost(1.4e9, 12e6),
        name="network_backward",
    )(grad, pre_one, pre_two, late, *weights)


def flat_blocks(width, hidden_width):
    return 2 * width // LANES, hidden_width // LANES, width // LANES


def flat_blocks_of(flat_rows, padded):
    width_blocks = (flat_rows // padded - padded // LANES) // 3
    return 2 * width_blocks, padded // LANES, width_blocks


def store_blocks(ref, base, values):
    rows = values.shape[0]
    for block in range(values.shape[1] // LANES):
        ref[(base + block) * rows : (base + block + 1) * rows, :] = values[
            :, block * LANES : (block + 1) * LANES
        ].astype(ref.dtype)


def weight_grad_kernel(
    pieces, place_ref, hidden_ref, message_ref, grad_ref, act_one_ref, act_two_ref, grad_one_ref, grad_two_ref, *rest
):
    *out_refs, first_sum, middle_sum, last_sum, flat = rest
    sources, _, rows, width = hidden_ref.shape
    count = sources * rows
    step = pl.program_id(0)
    grad_one = grad_one_ref[...]
    parts = (
        (first_sum.at[:, :width], dot(grad_one, hidden_ref[...].reshape(count, width), TN)),
        (first_sum.at[:, width:], dot(grad_one, message_ref[...].reshape(count, width), TN)),
        (middle_sum, dot(act_one_ref[...], grad_two_ref[...], TN)),
        (last_sum, dot(act_two_ref[...], grad_ref[...].reshape(count, width), TN)),
    )

    @pl.when(step == 0)
    def _():
        for total, part in parts:
            total[...] = part

    @pl.when(step > 0)
    def _():
        for total, part in parts:
            total[...] += part

    @pl.when(step == pl.num_programs(0) - 1)
    def _():
        base = 0
        for total in (first_sum, middle_sum, last_sum):
            store_blocks(flat, base, total[...])
            base += total.shape[1] // LANES
        live = base * first_sum.shape[0]
        if flat.shape[0] > live:
            flat[live:] = jnp.zeros((flat.shape[0] - live, LANES), F32)
        here = place_ref[0]
        if not pieces:
            (out_ref,) = out_refs
            for owned in range(out_ref.shape[0]):
                out_ref[owned] = jnp.where(owned == here, flat[...], 0.0).astype(BF16)
        for shift, piece_ref in enumerate(out_refs if pieces else ()):
            rows_each = piece_ref.shape[0]
            target = lax.rem(here + shift, pieces)
            piece_ref[...] = flat[pl.ds(pl.multiple_of(target * rows_each, 16), rows_each), :].astype(BF16)


def weight_grad(place, hidden, message, grad, which, saved, shape, pieces=0):
    holders, _, rows, width = message.shape
    hidden_width = saved[0].shape[1]
    steps = 2
    sources = holders // steps

    def rows_of(values, kind):
        return pl.BlockSpec(
            (sources, 1) + values.shape[2:], lambda step, place: (step, kind, 0, 0)
        )

    saved_rows = pl.BlockSpec((saved[0].shape[0] // steps, hidden_width), lambda step, place: (step, 0))
    flat_rows = shape[-2] * max(pieces, 1)
    return pl.pallas_call(
        functools.partial(weight_grad_kernel, pieces),
        grid_spec=pltpu.PrefetchScalarGridSpec(
            num_scalar_prefetch=1,
            grid=(steps,),
            in_specs=[rows_of(hidden, 0), rows_of(message, 0), rows_of(grad, which)] + [saved_rows] * 4,
            out_specs=[whole(shape)] * max(pieces, 1),
            scratch_shapes=[
                pltpu.VMEM((hidden_width, cols), F32) for cols in (2 * width, hidden_width, width)
            ]
            + [pltpu.VMEM((flat_rows, LANES), F32)],
        ),
        out_shape=[shape_of(shape, BF16)] * max(pieces, 1),
        compiler_params=params(),
        cost_estimate=cost(1.4e9, 8e6),
        name="weight_grad",
    )(place, hidden, message, grad, *saved)


def newton_step(current, tall, centre, eye_ref):
    high = current.astype(BF16)
    rest = dot(high, high, TN if tall else NT)
    if centre:
        size = rest.shape[0]
        rest = rest - centre * eye_ref[:size, :size]
    rest_low = rest.astype(BF16)
    linear = NEWTON_B + 2.0 * NEWTON_C * centre
    poly = (linear * rest + NEWTON_C * dot(rest_low, rest_low, NN)).astype(BF16)
    step = dot(high, poly, NN) if tall else dot(poly, high, NN)
    return (NEWTON_A + NEWTON_B * centre + NEWTON_C * centre * centre) * current + step


def unit(moment):
    return moment / (jnp.sqrt(jnp.sum(moment * moment)) + 1e-07)


def native(values, which, fill=True):
    cols = values.shape[2 if which == 0 else 3]
    padded = LANES * (1 << (round_up(cols, LANES) // LANES - 1).bit_length())
    if padded > cols and fill:
        values = jnp.pad(values, ((0, 0), (0, 0), (0, 0), (0, padded - cols)))
    values = jnp.transpose(values, (0, 3, 1, 2) if which == 0 else (0, 2, 1, 3))
    if padded > cols and not fill:
        return values
    layers, rows, per_owner, _ = values.shape
    values = values.reshape(layers, rows, per_owner, padded // LANES, LANES)
    return jnp.transpose(values, (0, 1, 3, 2, 4)).reshape(layers, -1, LANES)


def from_native(values, which, per_owner, rows):
    if values.ndim == 3:
        layers = values.shape[0]
        values = values.reshape(layers, rows, -1, per_owner, LANES)
        values = jnp.transpose(values, (0, 1, 3, 2, 4)).reshape(layers, rows, per_owner, -1)
    return jnp.transpose(values, (0, 2, 3, 1) if which == 0 else (0, 2, 1, 3))


class Lying:
    def __init__(self, ref, rows, per_owner, blocks):
        self.ref, self.rows, self.per_owner, self.blocks = ref, rows, per_owner, blocks
        self.spread = ref.shape[1] // rows if len(ref.shape) == 3 else 0

    def place(self, block, owned):
        if self.spread:
            return (0, pl.ds(block * self.per_owner + owned, self.rows, stride=self.spread), slice(None))
        return (0, slice(None), owned, slice(block * LANES, block * LANES + self.lanes(block)))

    def lanes(self, block):
        return LANES if self.spread else min(LANES, self.ref.shape[3] - block * LANES)

    def read(self, block, owned):
        return self.ref[self.place(block, owned)]

    def write(self, block, owned, value):
        self.ref[self.place(block, owned)] = value[:, : self.lanes(block)]


def lying(refs, rows, per_owner):
    blocks = [ref.shape[1] // rows // per_owner for ref in refs]
    blocks[1] = round_up(rows, LANES) // LANES
    return [Lying(ref, rows, per_owner, count) for ref, count in zip(refs, blocks)]


def half_kernel(rows, per_owner, *refs):
    moms, flat_ref = lying(refs[:3], rows, per_owner), refs[3]
    padded = round_up(rows, LANES)
    base = 0
    for mom in moms:
        for block in range(mom.blocks):
            begin = base * padded
            for owned in range(per_owner):
                flat_ref[owned, begin : begin + padded] = jnp.zeros((padded, LANES), F32)
                flat_ref[owned, begin : begin + rows, : mom.lanes(block)] = MOMENTUM * mom.read(block, owned)
            base += 1


def half_moments(moms, rows, per_owner, flat_rows):
    layers = moms[0].shape[0]
    return pl.pallas_call(
        functools.partial(half_kernel, rows, per_owner),
        grid=(layers,),
        in_specs=[at_step(mom.shape, 0) for mom in moms],
        out_specs=pl.BlockSpec((per_owner, flat_rows, LANES), lambda step: (step, 0, 0)),
        out_shape=shape_of((layers * per_owner, flat_rows, LANES), F32),
        compiler_params=params(),
        cost_estimate=cost(4e6, 14e6),
        name="half_moments",
    )(*moms)


def cast_kernel(rows, per_owner, mine_ref, *refs):
    olds, lows, scratches = lying(refs[:3], rows, per_owner), refs[3:6], refs[6:]
    for old, low, scratch in zip(olds, lows, scratches):
        scratch[rows:] = jnp.zeros((scratch.shape[0] - rows, scratch.shape[1]), F32)
        for block in range(old.blocks):
            scratch[:rows, block * LANES : (block + 1) * LANES] = old.read(block, mine_ref[0])
        low[0] = scratch[...].astype(BF16)


def cast_weights(mine, weights, rows, per_owner, width):
    layers = weights[0].shape[0]
    padded = round_up(rows, LANES)
    shapes = [(padded, blocks * LANES) for blocks in flat_blocks(width, padded)]
    layer_spec = lambda shape: pl.BlockSpec(
        (1,) + shape[1:], lambda step, mine: (step,) + (0,) * (len(shape) - 1)
    )
    return pl.pallas_call(
        functools.partial(cast_kernel, rows, per_owner),
        grid_spec=pltpu.PrefetchScalarGridSpec(
            num_scalar_prefetch=1,
            grid=(layers,),
            in_specs=[layer_spec(w.shape) for w in weights],
            out_specs=[layer_spec((layers,) + shape) for shape in shapes],
            scratch_shapes=[pltpu.VMEM(shape, F32) for shape in shapes],
        ),
        out_shape=[shape_of((layers,) + shape, BF16) for shape in shapes],
        compiler_params=params(),
        cost_estimate=cost(4e6, 11e6),
        name="cast_weights",
    )(mine, *weights)


def sum_kernel(*refs):
    total = refs[0][...].astype(F32)
    for ref in refs[1:-1]:
        total = total + ref[...].astype(F32)
    total = total.astype(BF16)
    for copy in range(refs[-1].shape[0]):
        refs[-1][copy] = total


def sum_arrays(parts, copies=1):
    shape = parts[0].shape
    return pl.pallas_call(
        sum_kernel,
        grid=(1,),
        in_specs=[whole(shape)] * len(parts),
        out_specs=whole((copies,) + shape),
        out_shape=shape_of((copies,) + shape, BF16),
        compiler_params=params(),
        cost_estimate=cost(1e6, 2e6),
        name="sum_arrays",
    )(*parts)


def join_kernel(slab_ref, *refs):
    *parts, whole_ref = refs
    rows = parts[0].shape[0]
    for shift, part in enumerate(parts):
        origin = lax.rem(slab_ref[0] - shift + len(parts), len(parts))
        whole_ref[pl.ds(pl.multiple_of(origin * rows, 16), rows), :] = part[...]


def join(slab, parts):
    rows, lanes = parts[0].shape
    shape = (rows * len(parts), lanes)
    return pl.pallas_call(
        join_kernel,
        grid_spec=pltpu.PrefetchScalarGridSpec(
            num_scalar_prefetch=1,
            grid=(1,),
            in_specs=[whole((rows, lanes))] * len(parts),
            out_specs=whole(shape),
        ),
        out_shape=shape_of(shape, BF16),
        compiler_params=params(),
        cost_estimate=cost(1e6, 2e6),
        name="join",
    )(slab, *parts)


def muon_kernel(rows, task_ref, half_ref, grad_ref, step_ref, eye_ref):
    padded = round_up(rows, LANES)
    eye_ref[...] = (iota(eye_ref.shape, 0) == iota(eye_ref.shape, 1)).astype(F32)
    base = 0
    values = []
    blocks = flat_blocks_of(half_ref.shape[1], padded)
    for count in blocks:
        parts = []
        for block in range(base, base + count):
            span = slice(block * padded, (block + 1) * padded)
            parts.append(half_ref[0, span] + grad_ref[span].astype(F32))
        base += count
        values.append(unit(jnp.concatenate(parts, axis=1)))
    for centre in NEWTON_CENTRES:
        values = [newton_step(value, which == 2, centre, eye_ref) for which, value in enumerate(values)]
    base = 0
    for count, value in zip(blocks, values):
        longest = rows if count == padded // LANES else max(count * LANES, rows)
        store_blocks(step_ref, base, value * (LEARNING_RATE * 0.2 * math.sqrt(longest)))
        base += count


def layer_of(values, layer):
    return pl.BlockSpec(
        (1,) + values.shape[1:], lambda step, *scalars: (layer,) + (0,) * (values.ndim - 1)
    )


def muon_step(task, grads, halves, rows):
    block = (1,) + halves.shape[1:]
    padded = round_up(rows, LANES)
    return pl.pallas_call(
        functools.partial(muon_kernel, rows),
        grid_spec=pltpu.PrefetchScalarGridSpec(
            num_scalar_prefetch=1,
            grid=(1,),
            in_specs=[pl.BlockSpec(block, lambda step, task: (task[0], 0, 0)), whole(grads.shape)],
            out_specs=whole(block[1:]),
            scratch_shapes=[pltpu.VMEM((padded, padded), F32)],
        ),
        out_shape=shape_of(block[1:], BF16),
        compiler_params=params(),
        cost_estimate=cost(7e9, 4e6),
        name="muon",
    )(task, halves, grads)


def apply_kernel(rows, per_owner, mine_ref, half_ref, *refs):
    steps, grads, weights = refs[:2], refs[2:4], lying(refs[4:7], rows, per_owner)
    new_moms, new_weights = lying(refs[-6:-3], rows, per_owner), lying(refs[-3:], rows, per_owner)
    mine = mine_ref[0]
    padded = round_up(rows, LANES)
    base = 0
    for weight, new_mom, new_weight in zip(weights, new_moms, new_weights):
        for block in range(weight.blocks):
            span = slice(base * padded, base * padded + rows)
            both_grads = [ref[span].astype(F32) for ref in grads]
            both_steps = [ref[span].astype(F32) for ref in steps]
            for owned in range(per_owner):
                grad = jnp.where(mine == owned, *both_grads)
                step = jnp.where(mine == owned, *both_steps)
                new_mom.write(block, owned, half_ref[owned, span] + grad)
                new_weight.write(block, owned, weight.read(block, owned) - step)
            base += 1


def apply_layer(mine, grads, steps, halves, weights, news, layer, rows, per_owner, partial=None):
    args = [mine, halves, *steps, *grads, *weights]
    in_specs = [pl.BlockSpec((per_owner,) + halves.shape[1:], lambda step, mine: (layer, 0, 0))]
    in_specs += [whole(value.shape) for value in (*steps, *grads)]
    in_specs += [layer_of(weight, layer) for weight in weights]
    aliases = {}
    if partial is not None:
        aliases = {len(args) + which: which for which in range(len(news))}
        args += list(partial)
        in_specs += [pl.BlockSpec(memory_space=pl.ANY)] * len(news)
    return pl.pallas_call(
        functools.partial(apply_kernel, rows, per_owner),
        grid_spec=pltpu.PrefetchScalarGridSpec(
            num_scalar_prefetch=1,
            grid=(1,),
            in_specs=in_specs,
            out_specs=[layer_of(new, layer) for new in news],
        ),
        out_shape=[shape_of(new.shape, F32) for new in news],
        input_output_aliases=aliases,
        compiler_params=params(),
        cost_estimate=cost(2e6, 18e6),
        name="apply_layer",
    )(*args)


def small_kernel(count_parts, *refs):
    parts, refs = refs[:count_parts], refs[count_parts:]
    radial_ref, radial_mom_ref, mixing_ref, mixing_mom_ref, *outs = refs
    new_radial_ref, new_radial_mom_ref, new_mixing_ref, new_mixing_mom_ref = outs
    layers, shells, width = radial_ref.shape
    channels = mixing_ref.shape[1]
    values = []
    total = parts[0][...].astype(F32)
    for part in parts[1:]:
        total = total + part[...].astype(F32)
    each = total.shape[0] // layers
    for layer in range(layers):
        total_here = total[layer * each : (layer + 1) * each]
        moment = MOMENTUM * radial_mom_ref[layer] + total_here[:shells]
        new_radial_mom_ref[layer] = moment
        values.append(unit(moment))
        moment = eight_rows(MOMENTUM * mixing_mom_ref[layer]) + total_here[shells:]
        new_mixing_mom_ref[layer] = moment[:channels]
        values.append(unit(moment))
    for _ in NEWTON_CENTRES:
        grams = [dot(value, value, NT, EXACT) for value in values]
        polys = [NEWTON_B * gram + NEWTON_C * dot(gram, gram, NN, EXACT) for gram in grams]
        values = [NEWTON_A * value + dot(poly, value, NN, EXACT) for value, poly in zip(values, polys)]
    for layer in range(layers):
        lift = LEARNING_RATE * 0.2 * math.sqrt(max(shells, width))
        new_radial_ref[layer] = radial_ref[layer] - lift * values[2 * layer]
        lift = LEARNING_RATE * 0.2 * math.sqrt(max(channels, width))
        new_mixing_ref[layer] = mixing_ref[layer] - lift * values[2 * layer + 1][:channels]


def small_step(parts, radial, radial_mom, mixing, mixing_mom):
    args = (*parts, radial, radial_mom, mixing, mixing_mom)
    outs = [radial, radial_mom, mixing, mixing_mom]
    return pl.pallas_call(
        functools.partial(small_kernel, len(parts)),
        grid=(1,),
        in_specs=[whole(arg.shape) for arg in args],
        out_specs=[whole(out.shape) for out in outs],
        out_shape=[shape_of(out.shape, F32) for out in outs],
        compiler_params=params(),
        cost_estimate=cost(1e8, 3e6),
        name="small_step",
    )(*args)


EVERY = ("slab", "pair", "elem")
HOLDERS = ("pair", "elem")


def swap(values):
    return lax.all_to_all(values, HOLDERS, split_axis=0, concat_axis=0, tiled=True)


def to_both_sides(to_left, to_right):
    count = lax.axis_size(EVERY)
    up = [(i, (i + 1) % count) for i in range(count)]
    down = [((i + 1) % count, i) for i in range(count)]
    return lax.ppermute(to_right, EVERY, up), lax.ppermute(to_left, EVERY, down)


def other_of_pair(values):
    return lax.ppermute(values, "pair", [(0, 1), (1, 0)])


def shifted(values, shift, axis):
    count = lax.axis_size(axis)
    return lax.ppermute(values, axis, [(i, (i + shift) % count) for i in range(count)])


def exchange(pieces, axis="slab"):
    return [piece if shift == 0 else shifted(piece, shift, axis) for shift, piece in enumerate(pieces)]


def to_all(piece, axis="slab"):
    return exchange([piece] * lax.axis_size(axis), axis)


def on_device(
    features,
    charges,
    elements,
    neighbours,
    counts,
    distances,
    radial,
    radial_mom,
    mixing,
    mixing_mom,
    w_in,
    w_mid,
    w_out,
    mom_in,
    mom_mid,
    mom_out,
    cot_features,
    cot_charges,
):
    batches, atoms, width = features.shape
    per_owner, hidden_width = w_in.shape[1], w_in.shape[3]
    owners = lax.axis_size("elem")
    shells = radial.shape[1]
    holders = per_owner * owners
    cap = 2 * atoms // holders
    rim = atoms // 8
    sizes = (owners, per_owner, cap)
    by_rows = (holders, 1, batches * cap, width)
    by_atom = (holders, 1, batches, cap, width)
    barrier = lax.optimization_barrier
    mine = lax.axis_index("pair").astype(jnp.int32)[None]
    slab = lax.axis_index("slab").astype(jnp.int32)[None]
    slabs = lax.axis_size("slab")
    padded = round_up(hidden_width, LANES)
    flat_rows = sum(flat_blocks(width, padded)) * padded
    piece = round_up(-(-flat_rows // slabs), 16)

    place, place_t, packed, source, first, last = start(
        elements, features, charges, cot_features, cot_charges, mixing, rim, sizes
    )
    arrived = swap(packed).reshape(holders, 2, batches * cap, width)
    left, right = to_both_sides(first, last)
    band, band_t = make_bands(distances, neighbours, counts, shells, rim)
    old_weights = [native(w, which) for which, w in enumerate((w_in, w_mid, w_out))]
    old_moms = [native(m, which, False) for which, m in enumerate((mom_in, mom_mid, mom_out))]
    weights = cast_weights(mine, old_weights, hidden_width, per_owner, width)

    message = edge_forward(source, left, right, band, radial, 0, place, sizes)
    message, arrived = barrier((message, arrived))
    message = swap(message).reshape(by_rows)
    result, pre_one, pre_two = network_forward(arrived, message, weights, 0)
    back, halves = barrier(
        (swap(result).reshape(by_atom), half_moments(old_moms, hidden_width, per_owner, flat_rows))
    )
    hidden_one, charge_one, source_one, first, last = update_atoms(
        back, 0, place_t, features, charges, mixing, 1, rim
    )

    left_one, right_one = to_both_sides(first, last)
    message_one = edge_forward(source_one, left_one, right_one, band, radial, 1, place, sizes)
    message_one = swap(message_one).reshape(by_rows)
    result_one, rows_one, grad_hidden, grad_message, *saved = network_turn(
        arrived, result, message_one, weights, 1
    )
    grad_message = swap(grad_message).reshape(by_atom)
    pieces = weight_grad(slab, rows_one, message_one, arrived, 1, saved, (piece, LANES), slabs)
    grad_message, grad_hidden, pieces = barrier((grad_message, grad_hidden, pieces))
    grad_hidden = swap(grad_hidden).reshape(by_atom)
    pieces_one = exchange(pieces)
    inner, to_left, to_right, radial_grad = edge_backward(
        grad_message, place_t, source_one, left_one, right_one, band, band_t, radial, 1
    )
    to_left, to_right, pieces_one[1] = barrier((to_left, to_right, pieces_one[1]))
    from_left, from_right = to_both_sides(to_left, to_right)
    from_left, pieces_one[-1] = barrier((from_left, pieces_one[-1]))
    grad, grad_charge, small_one, packed = finish(
        inner, from_left, from_right, grad_hidden, place_t, cot_features, cot_charges, charge_one,
        mixing, 1, radial_grad, place,
    )

    grad_update = swap(packed).reshape(by_rows)
    grad_update, piece_one = barrier((grad_update, sum_arrays(pieces_one)[0]))
    totals_one = to_all(piece_one)
    grad_message, both, *saved = network_backward(grad_update, pre_one, pre_two, result_one, weights, 0)
    grad_message, totals_one[1] = barrier((grad_message, totals_one[1]))
    grad_message = swap(grad_message).reshape(by_atom)
    pieces = weight_grad(slab, arrived, message, grad_update, 0, saved, (piece, LANES), slabs)
    grad_message, both, pieces, totals_one = barrier((grad_message, both, pieces, totals_one))
    pieces_zero = exchange(pieces)
    both = swap(both).reshape(holders, 2, batches, cap, width)
    inner, to_left, to_right, radial_grad = edge_backward(
        grad_message, place_t, source, left, right, band, band_t, radial, 0
    )
    total_one, pieces_zero[1], inner = barrier((join(slab, totals_one), pieces_zero[1], inner))
    from_left, from_right = to_both_sides(to_left, to_right)
    task = lambda layer: layer * per_owner + mine
    step = muon_step(task(1), total_one, halves, hidden_width)
    pieces_zero, from_left, from_right, _ = barrier((pieces_zero, from_left, from_right, step))
    step, other_one = barrier((step, other_of_pair(total_one)))
    steps_one = (step, other_of_pair(step))
    copies, from_left = barrier((sum_arrays(pieces_zero, slabs), from_left))
    total_zero = lax.all_to_all(copies, "slab", split_axis=0, concat_axis=0, tiled=True)
    total_zero = total_zero.reshape(slabs * piece, LANES)
    grad_features, grad_charges, smalls, features_out, charges_out = finish(
        inner, from_left, from_right, both, place_t, grad, grad_charge, charges, mixing, 0, radial_grad,
        last=(small_one, hidden_one, charge_one),
    )
    (smalls,) = sum_arrays(to_all(smalls, "elem"))
    total_zero, steps_one, smalls = barrier((total_zero, steps_one, smalls))
    news = [native(jnp.zeros(m.shape, F32), which, False) for which, m in enumerate((mom_in, mom_mid, mom_out))]
    news = [shape_of(new.shape, F32) for new in news] * 2
    sizes = (hidden_width, per_owner)
    done = apply_layer(mine, (total_one, other_one), steps_one, halves, old_weights, news, 1, *sizes)
    step = muon_step(task(0), total_zero, halves, hidden_width)
    step, other, smalls = barrier((step, other_of_pair(total_zero), to_all(smalls)))
    steps = (step, other_of_pair(step))
    (smalls,) = sum_arrays(smalls)
    new_radial, new_radial_mom, new_mixing, new_mixing_mom = small_step(
        (smalls, other_of_pair(smalls)), radial, radial_mom, mixing, mixing_mom
    )
    done = apply_layer(mine, (total_zero, other), steps, halves, old_weights, news, 0, *sizes, done)
    news = [from_native(value, which % 3, per_owner, hidden_width) for which, value in enumerate(done)]
    return (
        features_out,
        charges_out,
        grad_features,
        grad_charges,
        *news[3:],
        *news[:3],
        new_radial,
        new_radial_mom,
        new_mixing,
        new_mixing_mom,
    )


def solution(mesh):
    in_specs = (
        P(None, EVERY, None),
        P(None, None, EVERY),
        P(None, EVERY),
        P(None, None, EVERY),
        P(None, EVERY),
        P(None, None, EVERY),
        P(),
        P(),
        P(),
        P(),
        P(None, "elem", None, None),
        P(None, "elem", None, None),
        P(None, "elem", None, None),
        P(None, "elem", None, None),
        P(None, "elem", None, None),
        P(None, "elem", None, None),
        P(None, EVERY, None),
        P(None, None, EVERY),
    )
    out_specs = (
        P(None, EVERY, None),
        P(None, None, EVERY),
        P(None, EVERY, None),
        P(None, None, EVERY),
        P(None, "elem", None, None),
        P(None, "elem", None, None),
        P(None, "elem", None, None),
        P(None, "elem", None, None),
        P(None, "elem", None, None),
        P(None, "elem", None, None),
        P(),
        P(),
        P(),
        P(),
    )
    devices = mesh.devices
    folded = jax.sharding.Mesh(devices.reshape(devices.shape[0] // 2, 2, devices.shape[1]), EVERY)
    return jax.shard_map(
        on_device, mesh=folded, in_specs=in_specs, out_specs=out_specs, check_vma=False
    )
```

```python
import functools
import math

import jax
import jax.numpy as jnp
from jax import lax
from jax.experimental import pallas as pl
from jax.experimental.pallas import tpu as pltpu
from jax.sharding import PartitionSpec as P

EXACT = lax.Precision.HIGHEST
SHELL_START = 0.8
SHELL_SPACING = 0.28
SHELL_SHARPNESS = 8.0
CUTOFF_RADIUS = 5.0
MOMENTUM = 0.5
LEARNING_RATE = 0.25
NEWTON_A = 3.4445
NEWTON_B = -4.775
NEWTON_C = 2.0315
NEWTON_CENTRES = (0.0, 0.0, 0.5, 1.0, 1.0)
QUARTERS = 4
GROUP = 8
SOURCES = 2
LANES = 128
FAR = 100.0
VMEM_BYTES = 60 * 1024 * 1024
F32 = jnp.float32
BF16 = jnp.bfloat16
NN = (((1,), (0,)), ((), ()))
NT = (((1,), (1,)), ((), ()))
TN = (((0,), (0,)), ((), ()))


def dot(left, right, dims, precision=None):
    return lax.dot_general(left, right, dims, precision=precision, preferred_element_type=F32)


def iota(shape, dim):
    return lax.broadcasted_iota(jnp.int32, shape, dim)


def round_up(size, multiple):
    return -(-size // multiple) * multiple


def params():
    return pltpu.CompilerParams(vmem_limit_bytes=VMEM_BYTES)


def cost(flops, read_bytes):
    return pl.CostEstimate(flops=int(flops), bytes_accessed=int(read_bytes), transcendentals=0)


def shape_of(shape, dtype):
    return jax.ShapeDtypeStruct(shape, dtype)


def at_step(shape, axis):
    block = tuple(1 if dim == axis else size for dim, size in enumerate(shape))
    return pl.BlockSpec(block, lambda step: tuple(step if dim == axis else 0 for dim in range(len(shape))))


def whole(shape):
    return pl.BlockSpec(shape, lambda *step: (0,) * len(shape))


def columns(rows):
    count, atoms = rows.shape
    return jnp.concatenate([rows, jnp.zeros((LANES - count, atoms), F32)], axis=0).T


def eight_rows(rows):
    return jnp.concatenate([rows, jnp.zeros((8 - rows.shape[0], rows.shape[1]), F32)], axis=0)


def add_columns(values, first):
    return jnp.concatenate([values[:, :LANES] + first, values[:, LANES:]], axis=1)


def source_of(hidden, charge_cols, mixing, channels):
    for channel in range(channels):
        hidden = hidden + charge_cols[:, channel : channel + 1] * mixing[channel : channel + 1, :]
    return hidden.astype(BF16)


def store_source(source, source_ref, first_ref, last_ref):
    rim = first_ref.shape[1]
    source_ref[0] = source
    first_ref[0] = source[:rim]
    last_ref[0] = source[source.shape[0] - rim :]


def atom_spec(values, which=0):
    holders, _, _, cap, width = values.shape
    return pl.BlockSpec((holders, 1, 1, cap, width), lambda step: (0, which, step, 0, 0))


def start_kernel(
    sizes, elem_ref, feat_ref, charge_ref, cotf_ref, cotc_ref, mixing_ref,
    place_ref, place_t_ref, packed_ref, source_ref, first_ref, last_ref,
):
    owners, per_owner, cap = sizes
    slots, atoms = place_ref.shape[1:]
    channels = charge_ref.shape[1]
    row = elem_ref[pl.ds(pl.program_id(0), 1), :]
    before = iota((atoms, atoms), 0)
    after = iota((atoms, atoms), 1)
    hot = (iota((LANES, atoms), 0) == row).astype(F32)
    rank = dot(hot.astype(BF16), (before < after).astype(F32).astype(BF16), NN)
    rank = jnp.sum(rank * hot, axis=0, keepdims=True)
    holder = lax.rem(row, per_owner) * owners + lax.div(row, per_owner)
    slot = holder.astype(F32) * cap + rank
    place = (iota((slots, atoms), 0) == slot.astype(jnp.int32)).astype(F32).astype(BF16)
    slot_t = jnp.broadcast_to(slot, (LANES, atoms)).T[:, :1].astype(jnp.int32)
    place_t = (iota((atoms, slots), 1) == slot_t).astype(F32).astype(BF16)
    place_ref[0] = place
    place_t_ref[0] = place_t
    features = feat_ref[0]
    grad = add_columns(cotf_ref[0].astype(F32), columns(cotc_ref[0])).astype(BF16)
    holders, _, _, _, width = packed_ref.shape
    for which, values in enumerate((features, grad)):
        packed = dot(place, values, NN).astype(BF16)
        packed_ref[:, which] = packed.reshape(holders, 1, cap, width)
    store_source(
        source_of(features.astype(F32), columns(charge_ref[0]), mixing_ref[0], channels),
        source_ref, first_ref, last_ref,
    )


def start(elements, features, charges, cot_features, cot_charges, mixing, rim, sizes):
    batches, atoms, width = features.shape
    owners, per_owner, cap = sizes
    holders = owners * per_owner
    packed_shape = (holders, 2, batches, cap, width)
    args = (elements, features, charges, cot_features, cot_charges, mixing)
    outs = (
        shape_of((batches, holders * cap, atoms), BF16),
        shape_of((batches, atoms, holders * cap), BF16),
        shape_of(packed_shape, BF16),
        shape_of((batches, atoms, width), BF16),
        shape_of((batches, rim, width), BF16),
        shape_of((batches, rim, width), BF16),
    )
    return pl.pallas_call(
        functools.partial(start_kernel, sizes),
        grid=(batches,),
        in_specs=[whole(elements.shape)]
        + [at_step(arg.shape, 0) for arg in args[1:-1]]
        + [whole(mixing.shape)],
        out_specs=[
            at_step(outs[0].shape, 0),
            at_step(outs[1].shape, 0),
            at_step(packed_shape, 2),
        ]
        + [at_step(out.shape, 0) for out in outs[3:]],
        out_shape=outs,
        compiler_params=params(),
        cost_estimate=cost(6e8, 8e6),
        name="start",
    )(*args)


def bands_kernel(shells, dist_ref, near_ref, band_ref, band_t_ref):
    groups, pairs = dist_ref.shape[1:]
    slots = pairs // GROUP
    per_quarter = groups // QUARTERS
    window = band_ref.shape[2]
    rows = shells * GROUP
    sub = iota((GROUP, pairs), 0)
    lane = iota((GROUP, pairs), 1)
    own = ((lane >= sub * slots) & (lane < (sub + 1) * slots)).astype(F32)
    centres = SHELL_START + SHELL_SPACING * iota((shells, 1), 0).astype(F32)
    target = iota((window, pairs), 0)
    distance_all = dist_ref[0]
    envelope_all = 0.5 * (jnp.cos(math.pi * distance_all / CUTOFF_RADIUS) + 1.0)
    for group in range(groups):
        distance = distance_all[group : group + 1]
        spread = distance - centres
        basis = jnp.exp(-SHELL_SHARPNESS * spread * spread) * envelope_all[group : group + 1]
        spaced = (basis[:, None, :] * own[None]).reshape(rows, pairs).astype(BF16)
        hot = (target == near_ref[0, group : group + 1, :]).astype(F32).astype(BF16)
        band_ref[0, group * rows : (group + 1) * rows, :] = dot(spaced, hot, NT).astype(BF16)
        quarter, inner = group // per_quarter, group % per_quarter
        band_t_ref[0, quarter, :, inner * rows : (inner + 1) * rows] = dot(hot, spaced, NT).astype(BF16)


def make_bands(distances, neighbours, counts, shells, rim):
    batches, slots, atoms = distances.shape
    groups = atoms // GROUP
    block = atoms // QUARTERS
    window = block + 2 * rim
    live = iota(distances.shape, 1) < counts[:, None, :]
    distance = jnp.where(live, distances, FAR)
    local = neighbours - (iota(neighbours.shape, 2) // block) * block

    def grouped(values):
        return jnp.transpose(values, (0, 2, 1)).reshape(batches, groups, GROUP * slots)

    args = (grouped(distance), grouped(local))
    rows = shells * GROUP
    outs = (
        shape_of((batches, groups * rows, window), BF16),
        shape_of((batches, QUARTERS, window, groups // QUARTERS * rows), BF16),
    )
    return pl.pallas_call(
        functools.partial(bands_kernel, shells),
        grid=(batches,),
        in_specs=[at_step(arg.shape, 0) for arg in args],
        out_specs=[at_step(out.shape, 0) for out in outs],
        out_shape=outs,
        compiler_params=params(),
        cost_estimate=cost(3e9, 8e6),
        name="bands",
    )(*args)


def edge_forward_kernel(source_ref, left_ref, right_ref, band_ref, radial_ref, place_ref, packed_ref):
    atoms, width = source_ref.shape[1:]
    shells = radial_ref.shape[1]
    rim = left_ref.shape[1]
    block = atoms // QUARTERS
    window = block + 2 * rim
    per_quarter = block // GROUP
    extended = jnp.concatenate([left_ref[0], source_ref[0], right_ref[0]], axis=0)
    radial = jnp.broadcast_to(radial_ref[0][:, None, :], (shells, GROUP, width))
    rows = block * shells
    pieces = []
    for quarter in range(QUARTERS):
        near = extended[quarter * block : quarter * block + window]
        sums = dot(band_ref[0, quarter * rows : (quarter + 1) * rows, :], near, NN)
        sums = sums.reshape(per_quarter, shells, GROUP, width) * radial[None]
        pieces.append(jnp.sum(sums, axis=1).reshape(block, width))
    message = jnp.concatenate(pieces, axis=0).astype(BF16)
    packed = dot(place_ref[0], message, NN).astype(BF16)
    packed_ref[...] = packed.reshape(packed_ref.shape)


def edge_forward(source, left, right, band, radial, layer, place, sizes):
    batches, atoms, width = source.shape
    owners, per_owner, cap = sizes
    packed_shape = (owners * per_owner, 1, batches, cap, width)
    return pl.pallas_call(
        edge_forward_kernel,
        grid=(batches,),
        in_specs=[at_step(arg.shape, 0) for arg in (source, left, right, band)]
        + [pl.BlockSpec((1,) + radial.shape[1:], lambda step: (layer, 0, 0)), at_step(place.shape, 0)],
        out_specs=at_step(packed_shape, 2),
        out_shape=shape_of(packed_shape, BF16),
        compiler_params=params(),
        cost_estimate=cost(1.2e9, 6e6),
        name="edge_forward",
    )(source, left, right, band, radial, place)


def edge_backward_kernel(
    grad_ref, place_t_ref, source_ref, left_ref, right_ref, band_ref, band_t_ref, radial_ref,
    inner_ref, to_left_ref, to_right_ref, radial_grad_ref, total,
):
    atoms, width = source_ref.shape[1:]
    shells = radial_ref.shape[1]
    rim = left_ref.shape[1]
    block = atoms // QUARTERS
    window = block + 2 * rim
    per_quarter = block // GROUP
    rows = block * shells
    step = pl.program_id(0)
    slots = place_t_ref.shape[2]
    grad = dot(place_t_ref[0], grad_ref[...].reshape(slots, width), NN)
    extended = jnp.concatenate([left_ref[0], source_ref[0], right_ref[0]], axis=0)
    radial = jnp.broadcast_to(radial_ref[0][:, None, :], (shells, GROUP, width))
    total[...] = jnp.zeros_like(total)
    radial_sum = jnp.zeros((shells, GROUP, width), F32)
    for quarter in range(QUARTERS):
        near = extended[quarter * block : quarter * block + window]
        sums = dot(band_ref[0, quarter * rows : (quarter + 1) * rows, :], near, NN)
        piece = grad[quarter * block : (quarter + 1) * block].reshape(per_quarter, 1, GROUP, width)
        radial_sum = radial_sum + jnp.sum(
            sums.reshape(per_quarter, shells, GROUP, width) * piece, axis=0
        )
        scaled = (radial[None] * piece).reshape(rows, width).astype(BF16)
        total[quarter * block : quarter * block + window] += dot(band_t_ref[0, quarter], scaled, NN)
    inner_ref[0] = total[rim : rim + atoms]
    to_left_ref[0] = total[:rim].astype(BF16)
    to_right_ref[0] = total[rim + atoms :].astype(BF16)
    radial_here = jnp.sum(radial_sum, axis=1)

    @pl.when(step == 0)
    def _():
        radial_grad_ref[...] = radial_here

    @pl.when(step > 0)
    def _():
        radial_grad_ref[...] += radial_here


def edge_backward(grad, place_t, source, left, right, band, band_t, radial, layer):
    batches, atoms, width = source.shape
    rim = left.shape[1]
    shells = radial.shape[1]
    outs = (
        shape_of((batches, atoms, width), F32),
        shape_of(left.shape, BF16),
        shape_of(left.shape, BF16),
        shape_of((shells, width), F32),
    )
    return pl.pallas_call(
        edge_backward_kernel,
        grid=(batches,),
        in_specs=[atom_spec(grad), at_step(place_t.shape, 0)]
        + [at_step(arg.shape, 0) for arg in (source, left, right, band, band_t)]
        + [pl.BlockSpec((1,) + radial.shape[1:], lambda step: (layer, 0, 0))],
        out_specs=[at_step(out.shape, 0) for out in outs[:3]] + [whole(outs[3].shape)],
        out_shape=outs,
        scratch_shapes=[pltpu.VMEM((atoms + 2 * rim, width), F32)],
        compiler_params=params(),
        cost_estimate=cost(2.5e9, 10e6),
        name="edge_backward",
    )(grad, place_t, source, left, right, band, band_t, radial)


def update_kernel(back_ref, place_t_ref, hidden_ref, charge_ref, *rest):
    mixing_ref, hidden_out_ref, charge_out_ref, *sources = rest if len(rest) > 2 else (None, *rest)
    slots, width = place_t_ref.shape[2], hidden_ref.shape[2]
    channels = charge_ref.shape[1]
    update = dot(place_t_ref[0], back_ref[...].reshape(slots, width), NN)
    hidden = hidden_ref[0].astype(F32) + update
    charge = charge_ref[0] + update[:, :LANES].T[:channels]
    hidden_out_ref[0] = hidden
    charge_out_ref[0] = charge
    if sources:
        store_source(source_of(hidden, columns(charge), mixing_ref[0], channels), *sources)


def update_atoms(back, which, place_t, hidden, charge, mixing=None, layer=0, rim=0):
    batches, atoms, width = hidden.shape
    outs = [shape_of((batches, atoms, width), F32), shape_of(charge.shape, F32)]
    args = [back, place_t, hidden, charge]
    specs = [atom_spec(back, which)] + [at_step(arg.shape, 0) for arg in args[1:]]
    if mixing is not None:
        args.append(mixing)
        specs.append(pl.BlockSpec((1,) + mixing.shape[1:], lambda step: (layer, 0, 0)))
        outs += [shape_of((batches, rows, width), BF16) for rows in (atoms, rim, rim)]
    return pl.pallas_call(
        update_kernel,
        grid=(batches,),
        in_specs=specs,
        out_specs=[at_step(out.shape, 0) for out in outs],
        out_shape=outs,
        compiler_params=params(),
        cost_estimate=cost(2e8, 4e6),
        name="update_atoms",
    )(*args)


def finish_kernel(
    repack, inner_ref, from_left_ref, from_right_ref, back_ref, place_t_ref, grad_ref, grad_charge_ref,
    charge_ref, mixing_ref, radial_grad_ref, *rest,
):
    if repack:
        place_ref, grad_out_ref, charge_out_ref, small_ref, packed_ref = rest
    else:
        earlier_ref, late_ref, hidden_ref, late_charge_ref, *rest = rest
        grad_out_ref, charge_out_ref, joined_ref, hidden_out_ref, late_charge_out_ref, small_ref = rest
    atoms, width = inner_ref.shape[1:]
    rim = from_left_ref.shape[1]
    channels = charge_ref.shape[1]
    slots = place_t_ref.shape[2]
    shells = radial_grad_ref.shape[0]
    step = pl.program_id(0)
    inner = inner_ref[0]
    source_grad = jnp.concatenate(
        [
            inner[:rim] + from_left_ref[0].astype(F32),
            inner[rim : atoms - rim],
            inner[atoms - rim :] + from_right_ref[0].astype(F32),
        ],
        axis=0,
    )
    mixing_grad = dot(eight_rows(charge_ref[0]), source_grad, NN, EXACT)
    charge_term = dot(eight_rows(mixing_ref[0]), source_grad, NT, EXACT)
    joined = dot(place_t_ref[0], back_ref[...].reshape(slots, width), NN)
    grad = grad_ref[0].astype(F32) + joined + source_grad
    grad_charge = grad_charge_ref[0] + charge_term[:channels]
    grad_out_ref[0] = grad
    charge_out_ref[0] = grad_charge

    @pl.when(step == 0)
    def _():
        small_ref[:shells] = radial_grad_ref[...]
        small_ref[shells:] = mixing_grad

    @pl.when(step > 0)
    def _():
        small_ref[shells:] += mixing_grad

    if not repack:
        update = dot(place_t_ref[0], late_ref[...].reshape(slots, width), NN)
        hidden_out_ref[0] = hidden_ref[0] + update
        late_charge_out_ref[0] = late_charge_ref[0] + update[:, :LANES].T[:channels]

        @pl.when(step == pl.num_programs(0) - 1)
        def _():
            joined_ref[...] = jnp.concatenate([small_ref[...], earlier_ref[...]], axis=0).astype(BF16)

    else:
        sent = add_columns(grad, columns(grad_charge)).astype(BF16)
        packed = dot(place_ref[0], sent, NN).astype(BF16)
        packed_ref[...] = packed.reshape(packed_ref.shape)


def finish(inner, from_left, from_right, back, place_t, grad, grad_charge, charge, mixing, layer, radial_grad, place=None, last=None):
    batches, atoms, width = inner.shape
    args = [inner, from_left, from_right, back, place_t, grad, grad_charge, charge, mixing, radial_grad]
    specs = [at_step(arg.shape, 0) for arg in args]
    specs[3] = atom_spec(back)
    specs[8] = pl.BlockSpec((1,) + mixing.shape[1:], lambda step: (layer, 0, 0))
    specs[9] = whole(radial_grad.shape)
    small = (radial_grad.shape[0] + 8, width)
    outs = [shape_of(inner.shape, F32), shape_of(charge.shape, F32), shape_of(small, F32)]
    out_specs = [at_step(outs[0].shape, 0), at_step(outs[1].shape, 0), whole(small)]
    scratch = []
    if place is None:
        earlier, hidden, late_charge = last
        args += [earlier, back, hidden, late_charge]
        specs += [whole(earlier.shape), atom_spec(back, 1), at_step(hidden.shape, 0), at_step(charge.shape, 0)]
        joined = (small[0] + earlier.shape[0], width)
        outs[2], out_specs[2] = shape_of(joined, BF16), whole(joined)
        outs += outs[:2]
        out_specs += out_specs[:2]
        scratch.append(pltpu.VMEM(small, F32))
    else:
        args.append(place)
        specs.append(at_step(place.shape, 0))
        outs.append(shape_of(back.shape[:1] + (1,) + back.shape[2:], BF16))
        out_specs.append(atom_spec(back))
    return pl.pallas_call(
        functools.partial(finish_kernel, place is not None),
        grid=(batches,),
        in_specs=specs,
        out_specs=out_specs,
        out_shape=outs,
        scratch_shapes=scratch,
        compiler_params=params(),
        cost_estimate=cost(6e8, 6e6),
        name="finish",
    )(*args)


def gelu_parts(value):
    scale = math.sqrt(2.0 / math.pi)
    square = value * value
    bent = jnp.tanh(scale * (value + 0.044715 * value * square))
    half = 0.5 * (1.0 + bent)
    slope = half + 0.5 * value * (1.0 - bent * bent) * scale * (1.0 + 3.0 * 0.044715 * square)
    return value * half, slope


def rows_spec(values, which=0, sources=SOURCES):
    _, _, rows, width = values.shape
    return pl.BlockSpec((sources, 1, rows, width), lambda step: (step, which, 0, 0))


def saved_spec(shape, steps):
    return pl.BlockSpec((shape[0] // steps, shape[1]), lambda step: (step, 0))


def weight_specs(weights, layer):
    return [pl.BlockSpec((1,) + w.shape[1:], lambda step: (layer, 0, 0)) for w in weights]


def forward_through(hidden, message, first_ref, middle_ref, last_ref):
    width = hidden.shape[1]
    pre_one = dot(hidden, first_ref[0, :, :width], NT) + dot(message, first_ref[0, :, width:], NT)
    act_one = gelu_parts(pre_one)[0].astype(BF16)
    pre_two = dot(act_one, middle_ref[0], NN)
    act_two = gelu_parts(pre_two)[0].astype(BF16)
    return dot(act_two, last_ref[0], NN).astype(BF16), pre_one, pre_two


def back_through(grad, pre_one, pre_two, first_ref, middle_ref, last_ref, span, outs):
    width = grad.shape[1]
    act_one_ref, act_two_ref, grad_one_ref, grad_two_ref = outs
    act_one, slope_one = gelu_parts(pre_one)
    act_two, slope_two = gelu_parts(pre_two)
    act_one_ref[span] = act_one.astype(BF16)
    act_two_ref[span] = act_two.astype(BF16)
    grad_two = (slope_two * dot(grad, last_ref[0], NT)).astype(BF16)
    grad_two_ref[span] = grad_two
    grad_one = (slope_one * dot(grad_two, middle_ref[0], NT)).astype(BF16)
    grad_one_ref[span] = grad_one
    return (
        dot(grad_one, first_ref[0, :, :width], NN).astype(BF16),
        dot(grad_one, first_ref[0, :, width:], NN).astype(BF16),
    )


def network_forward_kernel(
    feat_ref, message_ref, first_ref, middle_ref, last_ref, result_ref, pre_one_ref, pre_two_ref
):
    sources, _, rows, _ = feat_ref.shape
    for source in range(sources):
        span = slice(source * rows, (source + 1) * rows)
        result_ref[source, 0], pre_one_ref[span], pre_two_ref[span] = forward_through(
            feat_ref[source, 0], message_ref[source, 0], first_ref, middle_ref, last_ref
        )


def network_forward(arrived, message, weights, layer):
    holders, _, rows, width = message.shape
    steps = holders // SOURCES
    saved = (holders * rows, weights[1].shape[1])
    return pl.pallas_call(
        network_forward_kernel,
        grid=(steps,),
        in_specs=[rows_spec(arrived), rows_spec(message)] + weight_specs(weights, layer),
        out_specs=[rows_spec(message)] + [saved_spec(saved, steps)] * 2,
        out_shape=(shape_of(message.shape, BF16), shape_of(saved, F32), shape_of(saved, F32)),
        compiler_params=params(),
        cost_estimate=cost(1.4e9, 8e6),
        name="network_forward",
    )(arrived, message, *weights)


def network_turn_kernel(
    feat_ref, result_ref, message_ref, grad_ref, first_ref, middle_ref, last_ref,
    result_out_ref, rows_ref, grad_hidden_ref, grad_message_ref, *saved,
):
    sources, _, rows, _ = feat_ref.shape
    for source in range(sources):
        span = slice(source * rows, (source + 1) * rows)
        hidden = feat_ref[source, 0].astype(F32) + result_ref[source, 0].astype(F32)
        hidden = hidden.astype(BF16)
        rows_ref[source, 0] = hidden
        result_out_ref[source, 0], pre_one, pre_two = forward_through(
            hidden, message_ref[source, 0], first_ref, middle_ref, last_ref
        )
        grad_hidden_ref[source, 0], grad_message_ref[source, 0] = back_through(
            grad_ref[source, 0], pre_one, pre_two, first_ref, middle_ref, last_ref, span, saved
        )


def network_turn(arrived, result, message, weights, layer):
    holders, _, rows, width = message.shape
    steps = holders // SOURCES
    saved = (holders * rows, weights[1].shape[1])
    spec = rows_spec(message)
    return pl.pallas_call(
        network_turn_kernel,
        grid=(steps,),
        in_specs=[rows_spec(arrived), spec, spec, rows_spec(arrived, 1)] + weight_specs(weights, layer),
        out_specs=[spec] * 4 + [saved_spec(saved, steps)] * 4,
        out_shape=[shape_of(message.shape, BF16)] * 4 + [shape_of(saved, BF16)] * 4,
        compiler_params=params(),
        cost_estimate=cost(2.8e9, 12e6),
        name="network_turn",
    )(arrived, result, message, arrived, *weights)


def network_backward_kernel(
    grad_ref, pre_one_ref, pre_two_ref, late_ref, first_ref, middle_ref, last_ref,
    grad_message_ref, both_ref, *saved,
):
    sources, _, rows, _ = grad_ref.shape
    both_ref[:, 1] = late_ref[:, 0]
    for source in range(sources):
        span = slice(source * rows, (source + 1) * rows)
        both_ref[source, 0], grad_message_ref[source, 0] = back_through(
            grad_ref[source, 0], pre_one_ref[span], pre_two_ref[span],
            first_ref, middle_ref, last_ref, span, saved,
        )


def network_backward(grad, pre_one, pre_two, late, weights, layer):
    holders, _, rows, width = grad.shape
    steps = holders // SOURCES
    saved = pre_one.shape
    spec = rows_spec(grad)
    both = pl.BlockSpec((SOURCES, 2, rows, width), lambda step: (step, 0, 0, 0))
    return pl.pallas_call(
        network_backward_kernel,
        grid=(steps,),
        in_specs=[spec] + [saved_spec(saved, steps)] * 2 + [spec] + weight_specs(weights, layer),
        out_specs=[spec, both] + [saved_spec(saved, steps)] * 4,
        out_shape=[shape_of(grad.shape, BF16), shape_of((holders, 2, rows, width), BF16)]
        + [shape_of(saved, BF16)] * 4,
        compiler_params=params(),
        cost_estimate=cost(1.4e9, 12e6),
        name="network_backward",
    )(grad, pre_one, pre_two, late, *weights)


def flat_blocks(width, hidden_width):
    return 2 * width // LANES, hidden_width // LANES, width // LANES


def flat_blocks_of(flat_rows, padded):
    width_blocks = (flat_rows // padded - padded // LANES) // 3
    return 2 * width_blocks, padded // LANES, width_blocks


def store_blocks(ref, base, values):
    rows = values.shape[0]
    for block in range(values.shape[1] // LANES):
        ref[(base + block) * rows : (base + block + 1) * rows, :] = values[
            :, block * LANES : (block + 1) * LANES
        ].astype(ref.dtype)


def weight_grad_kernel(
    pieces, place_ref, hidden_ref, message_ref, grad_ref, act_one_ref, act_two_ref, grad_one_ref, grad_two_ref, *rest
):
    *out_refs, first_sum, middle_sum, last_sum, flat = rest
    sources, _, rows, width = hidden_ref.shape
    count = sources * rows
    step = pl.program_id(0)
    grad_one = grad_one_ref[...]
    parts = (
        (first_sum.at[:, :width], dot(grad_one, hidden_ref[...].reshape(count, width), TN)),
        (first_sum.at[:, width:], dot(grad_one, message_ref[...].reshape(count, width), TN)),
        (middle_sum, dot(act_one_ref[...], grad_two_ref[...], TN)),
        (last_sum, dot(act_two_ref[...], grad_ref[...].reshape(count, width), TN)),
    )

    @pl.when(step == 0)
    def _():
        for total, part in parts:
            total[...] = part

    @pl.when(step > 0)
    def _():
        for total, part in parts:
            total[...] += part

    @pl.when(step == pl.num_programs(0) - 1)
    def _():
        base = 0
        for total in (first_sum, middle_sum, last_sum):
            store_blocks(flat, base, total[...])
            base += total.shape[1] // LANES
        live = base * first_sum.shape[0]
        if flat.shape[0] > live:
            flat[live:] = jnp.zeros((flat.shape[0] - live, LANES), F32)
        here = place_ref[0]
        if not pieces:
            (out_ref,) = out_refs
            for owned in range(out_ref.shape[0]):
                out_ref[owned] = jnp.where(owned == here, flat[...], 0.0).astype(BF16)
        for shift, piece_ref in enumerate(out_refs if pieces else ()):
            rows_each = piece_ref.shape[0]
            target = lax.rem(here + shift, pieces)
            piece_ref[...] = flat[pl.ds(pl.multiple_of(target * rows_each, 16), rows_each), :].astype(BF16)


def weight_grad(place, hidden, message, grad, which, saved, shape, pieces=0):
    holders, _, rows, width = message.shape
    hidden_width = saved[0].shape[1]
    steps = 2
    sources = holders // steps

    def rows_of(values, kind):
        return pl.BlockSpec(
            (sources, 1) + values.shape[2:], lambda step, place: (step, kind, 0, 0)
        )

    saved_rows = pl.BlockSpec((saved[0].shape[0] // steps, hidden_width), lambda step, place: (step, 0))
    flat_rows = shape[-2] * max(pieces, 1)
    return pl.pallas_call(
        functools.partial(weight_grad_kernel, pieces),
        grid_spec=pltpu.PrefetchScalarGridSpec(
            num_scalar_prefetch=1,
            grid=(steps,),
            in_specs=[rows_of(hidden, 0), rows_of(message, 0), rows_of(grad, which)] + [saved_rows] * 4,
            out_specs=[whole(shape)] * max(pieces, 1),
            scratch_shapes=[
                pltpu.VMEM((hidden_width, cols), F32) for cols in (2 * width, hidden_width, width)
            ]
            + [pltpu.VMEM((flat_rows, LANES), F32)],
        ),
        out_shape=[shape_of(shape, BF16)] * max(pieces, 1),
        compiler_params=params(),
        cost_estimate=cost(1.4e9, 8e6),
        name="weight_grad",
    )(place, hidden, message, grad, *saved)


def newton_step(current, tall, centre, eye_ref):
    high = current.astype(BF16)
    rest = dot(high, high, TN if tall else NT)
    if centre:
        size = rest.shape[0]
        rest = rest - centre * eye_ref[:size, :size]
    rest_low = rest.astype(BF16)
    linear = NEWTON_B + 2.0 * NEWTON_C * centre
    poly = (linear * rest + NEWTON_C * dot(rest_low, rest_low, NN)).astype(BF16)
    step = dot(high, poly, NN) if tall else dot(poly, high, NN)
    return (NEWTON_A + NEWTON_B * centre + NEWTON_C * centre * centre) * current + step


def unit(moment):
    return moment / (jnp.sqrt(jnp.sum(moment * moment)) + 1e-07)


def native(values, which, fill=True):
    cols = values.shape[2 if which == 0 else 3]
    padded = LANES * (1 << (round_up(cols, LANES) // LANES - 1).bit_length())
    if padded > cols and fill:
        values = jnp.pad(values, ((0, 0), (0, 0), (0, 0), (0, padded - cols)))
    values = jnp.transpose(values, (0, 3, 1, 2) if which == 0 else (0, 2, 1, 3))
    if padded > cols and not fill:
        return values
    layers, rows, per_owner, _ = values.shape
    values = values.reshape(layers, rows, per_owner, padded // LANES, LANES)
    return jnp.transpose(values, (0, 1, 3, 2, 4)).reshape(layers, -1, LANES)


def from_native(values, which, per_owner, rows):
    if values.ndim == 3:
        layers = values.shape[0]
        values = values.reshape(layers, rows, -1, per_owner, LANES)
        values = jnp.transpose(values, (0, 1, 3, 2, 4)).reshape(layers, rows, per_owner, -1)
    return jnp.transpose(values, (0, 2, 3, 1) if which == 0 else (0, 2, 1, 3))


class Lying:
    def __init__(self, ref, rows, per_owner, blocks):
        self.ref, self.rows, self.per_owner, self.blocks = ref, rows, per_owner, blocks
        self.spread = ref.shape[1] // rows if len(ref.shape) == 3 else 0

    def place(self, block, owned):
        if self.spread:
            return (0, pl.ds(block * self.per_owner + owned, self.rows, stride=self.spread), slice(None))
        return (0, slice(None), owned, slice(block * LANES, block * LANES + self.lanes(block)))

    def lanes(self, block):
        return LANES if self.spread else min(LANES, self.ref.shape[3] - block * LANES)

    def read(self, block, owned):
        return self.ref[self.place(block, owned)]

    def write(self, block, owned, value):
        self.ref[self.place(block, owned)] = value[:, : self.lanes(block)]


def lying(refs, rows, per_owner):
    blocks = [ref.shape[1] // rows // per_owner for ref in refs]
    blocks[1] = round_up(rows, LANES) // LANES
    return [Lying(ref, rows, per_owner, count) for ref, count in zip(refs, blocks)]


def half_kernel(rows, per_owner, *refs):
    moms, flat_ref = lying(refs[:3], rows, per_owner), refs[3]
    padded = round_up(rows, LANES)
    base = 0
    for mom in moms:
        for block in range(mom.blocks):
            begin = base * padded
            for owned in range(per_owner):
                flat_ref[owned, begin : begin + padded] = jnp.zeros((padded, LANES), F32)
                flat_ref[owned, begin : begin + rows, : mom.lanes(block)] = MOMENTUM * mom.read(block, owned)
            base += 1


def half_moments(moms, rows, per_owner, flat_rows):
    layers = moms[0].shape[0]
    return pl.pallas_call(
        functools.partial(half_kernel, rows, per_owner),
        grid=(layers,),
        in_specs=[at_step(mom.shape, 0) for mom in moms],
        out_specs=pl.BlockSpec((per_owner, flat_rows, LANES), lambda step: (step, 0, 0)),
        out_shape=shape_of((layers * per_owner, flat_rows, LANES), F32),
        compiler_params=params(),
        cost_estimate=cost(4e6, 14e6),
        name="half_moments",
    )(*moms)


def cast_kernel(rows, per_owner, mine_ref, *refs):
    olds, lows, scratches = lying(refs[:3], rows, per_owner), refs[3:6], refs[6:]
    for old, low, scratch in zip(olds, lows, scratches):
        scratch[rows:] = jnp.zeros((scratch.shape[0] - rows, scratch.shape[1]), F32)
        for block in range(old.blocks):
            scratch[:rows, block * LANES : (block + 1) * LANES] = old.read(block, mine_ref[0])
        low[0] = scratch[...].astype(BF16)


def cast_weights(mine, weights, rows, per_owner, width):
    layers = weights[0].shape[0]
    padded = round_up(rows, LANES)
    shapes = [(padded, blocks * LANES) for blocks in flat_blocks(width, padded)]
    layer_spec = lambda shape: pl.BlockSpec(
        (1,) + shape[1:], lambda step, mine: (step,) + (0,) * (len(shape) - 1)
    )
    return pl.pallas_call(
        functools.partial(cast_kernel, rows, per_owner),
        grid_spec=pltpu.PrefetchScalarGridSpec(
            num_scalar_prefetch=1,
            grid=(layers,),
            in_specs=[layer_spec(w.shape) for w in weights],
            out_specs=[layer_spec((layers,) + shape) for shape in shapes],
            scratch_shapes=[pltpu.VMEM(shape, F32) for shape in shapes],
        ),
        out_shape=[shape_of((layers,) + shape, BF16) for shape in shapes],
        compiler_params=params(),
        cost_estimate=cost(4e6, 11e6),
        name="cast_weights",
    )(mine, *weights)


def sum_kernel(*refs):
    total = refs[0][...].astype(F32)
    for ref in refs[1:-1]:
        total = total + ref[...].astype(F32)
    total = total.astype(BF16)
    for copy in range(refs[-1].shape[0]):
        refs[-1][copy] = total


def sum_arrays(parts, copies=1):
    shape = parts[0].shape
    return pl.pallas_call(
        sum_kernel,
        grid=(1,),
        in_specs=[whole(shape)] * len(parts),
        out_specs=whole((copies,) + shape),
        out_shape=shape_of((copies,) + shape, BF16),
        compiler_params=params(),
        cost_estimate=cost(1e6, 2e6),
        name="sum_arrays",
    )(*parts)


def join_kernel(slab_ref, *refs):
    *parts, whole_ref = refs
    rows = parts[0].shape[0]
    for shift, part in enumerate(parts):
        origin = lax.rem(slab_ref[0] - shift + len(parts), len(parts))
        whole_ref[pl.ds(pl.multiple_of(origin * rows, 16), rows), :] = part[...]


def join(slab, parts):
    rows, lanes = parts[0].shape
    shape = (rows * len(parts), lanes)
    return pl.pallas_call(
        join_kernel,
        grid_spec=pltpu.PrefetchScalarGridSpec(
            num_scalar_prefetch=1,
            grid=(1,),
            in_specs=[whole((rows, lanes))] * len(parts),
            out_specs=whole(shape),
        ),
        out_shape=shape_of(shape, BF16),
        compiler_params=params(),
        cost_estimate=cost(1e6, 2e6),
        name="join",
    )(slab, *parts)


def muon_kernel(rows, task_ref, half_ref, grad_ref, step_ref, eye_ref):
    padded = round_up(rows, LANES)
    eye_ref[...] = (iota(eye_ref.shape, 0) == iota(eye_ref.shape, 1)).astype(F32)
    base = 0
    values = []
    blocks = flat_blocks_of(half_ref.shape[1], padded)
    for count in blocks:
        parts = []
        for block in range(base, base + count):
            span = slice(block * padded, (block + 1) * padded)
            parts.append(half_ref[0, span] + grad_ref[span].astype(F32))
        base += count
        values.append(unit(jnp.concatenate(parts, axis=1)))
    for centre in NEWTON_CENTRES:
        values = [newton_step(value, which == 2, centre, eye_ref) for which, value in enumerate(values)]
    base = 0
    for count, value in zip(blocks, values):
        longest = rows if count == padded // LANES else max(count * LANES, rows)
        store_blocks(step_ref, base, value * (LEARNING_RATE * 0.2 * math.sqrt(longest)))
        base += count


def layer_of(values, layer):
    return pl.BlockSpec(
        (1,) + values.shape[1:], lambda step, *scalars: (layer,) + (0,) * (values.ndim - 1)
    )


def muon_step(task, grads, halves, rows):
    block = (1,) + halves.shape[1:]
    padded = round_up(rows, LANES)
    return pl.pallas_call(
        functools.partial(muon_kernel, rows),
        grid_spec=pltpu.PrefetchScalarGridSpec(
            num_scalar_prefetch=1,
            grid=(1,),
            in_specs=[pl.BlockSpec(block, lambda step, task: (task[0], 0, 0)), whole(grads.shape)],
            out_specs=whole(block[1:]),
            scratch_shapes=[pltpu.VMEM((padded, padded), F32)],
        ),
        out_shape=shape_of(block[1:], BF16),
        compiler_params=params(),
        cost_estimate=cost(7e9, 4e6),
        name="muon",
    )(task, halves, grads)


def apply_kernel(rows, per_owner, mine_ref, half_ref, *refs):
    steps, grads, weights = refs[:2], refs[2:4], lying(refs[4:7], rows, per_owner)
    new_moms, new_weights = lying(refs[-6:-3], rows, per_owner), lying(refs[-3:], rows, per_owner)
    mine = mine_ref[0]
    padded = round_up(rows, LANES)
    base = 0
    for weight, new_mom, new_weight in zip(weights, new_moms, new_weights):
        for block in range(weight.blocks):
            span = slice(base * padded, base * padded + rows)
            both_grads = [ref[span].astype(F32) for ref in grads]
            both_steps = [ref[span].astype(F32) for ref in steps]
            for owned in range(per_owner):
                grad = jnp.where(mine == owned, *both_grads)
                step = jnp.where(mine == owned, *both_steps)
                new_mom.write(block, owned, half_ref[owned, span] + grad)
                new_weight.write(block, owned, weight.read(block, owned) - step)
            base += 1


def apply_layer(mine, grads, steps, halves, weights, news, layer, rows, per_owner, partial=None):
    args = [mine, halves, *steps, *grads, *weights]
    in_specs = [pl.BlockSpec((per_owner,) + halves.shape[1:], lambda step, mine: (layer, 0, 0))]
    in_specs += [whole(value.shape) for value in (*steps, *grads)]
    in_specs += [layer_of(weight, layer) for weight in weights]
    aliases = {}
    if partial is not None:
        aliases = {len(args) + which: which for which in range(len(news))}
        args += list(partial)
        in_specs += [pl.BlockSpec(memory_space=pl.ANY)] * len(news)
    return pl.pallas_call(
        functools.partial(apply_kernel, rows, per_owner),
        grid_spec=pltpu.PrefetchScalarGridSpec(
            num_scalar_prefetch=1,
            grid=(1,),
            in_specs=in_specs,
            out_specs=[layer_of(new, layer) for new in news],
        ),
        out_shape=[shape_of(new.shape, F32) for new in news],
        input_output_aliases=aliases,
        compiler_params=params(),
        cost_estimate=cost(2e6, 18e6),
        name="apply_layer",
    )(*args)


def small_kernel(count_parts, *refs):
    parts, refs = refs[:count_parts], refs[count_parts:]
    radial_ref, radial_mom_ref, mixing_ref, mixing_mom_ref, *outs = refs
    new_radial_ref, new_radial_mom_ref, new_mixing_ref, new_mixing_mom_ref = outs
    layers, shells, width = radial_ref.shape
    channels = mixing_ref.shape[1]
    values = []
    total = parts[0][...].astype(F32)
    for part in parts[1:]:
        total = total + part[...].astype(F32)
    each = total.shape[0] // layers
    for layer in range(layers):
        total_here = total[layer * each : (layer + 1) * each]
        moment = MOMENTUM * radial_mom_ref[layer] + total_here[:shells]
        new_radial_mom_ref[layer] = moment
        values.append(unit(moment))
        moment = eight_rows(MOMENTUM * mixing_mom_ref[layer]) + total_here[shells:]
        new_mixing_mom_ref[layer] = moment[:channels]
        values.append(unit(moment))
    for _ in NEWTON_CENTRES:
        grams = [dot(value, value, NT, EXACT) for value in values]
        polys = [NEWTON_B * gram + NEWTON_C * dot(gram, gram, NN, EXACT) for gram in grams]
        values = [NEWTON_A * value + dot(poly, value, NN, EXACT) for value, poly in zip(values, polys)]
    for layer in range(layers):
        lift = LEARNING_RATE * 0.2 * math.sqrt(max(shells, width))
        new_radial_ref[layer] = radial_ref[layer] - lift * values[2 * layer]
        lift = LEARNING_RATE * 0.2 * math.sqrt(max(channels, width))
        new_mixing_ref[layer] = mixing_ref[layer] - lift * values[2 * layer + 1][:channels]


def small_step(parts, radial, radial_mom, mixing, mixing_mom):
    args = (*parts, radial, radial_mom, mixing, mixing_mom)
    outs = [radial, radial_mom, mixing, mixing_mom]
    return pl.pallas_call(
        functools.partial(small_kernel, len(parts)),
        grid=(1,),
        in_specs=[whole(arg.shape) for arg in args],
        out_specs=[whole(out.shape) for out in outs],
        out_shape=[shape_of(out.shape, F32) for out in outs],
        compiler_params=params(),
        cost_estimate=cost(1e8, 3e6),
        name="small_step",
    )(*args)


EVERY = ("slab", "pair", "elem")
HOLDERS = ("pair", "elem")


def swap(values):
    return lax.all_to_all(values, HOLDERS, split_axis=0, concat_axis=0, tiled=True)


def to_both_sides(to_left, to_right):
    count = lax.axis_size(EVERY)
    up = [(i, (i + 1) % count) for i in range(count)]
    down = [((i + 1) % count, i) for i in range(count)]
    return lax.ppermute(to_right, EVERY, up), lax.ppermute(to_left, EVERY, down)


def other_of_pair(values):
    return lax.ppermute(values, "pair", [(0, 1), (1, 0)])


def shifted(values, shift, axis):
    count = lax.axis_size(axis)
    return lax.ppermute(values, axis, [(i, (i + shift) % count) for i in range(count)])


def exchange(pieces, axis="slab"):
    return [piece if shift == 0 else shifted(piece, shift, axis) for shift, piece in enumerate(pieces)]


def to_all(piece, axis="slab"):
    return exchange([piece] * lax.axis_size(axis), axis)


def on_device(
    features,
    charges,
    elements,
    neighbours,
    counts,
    distances,
    radial,
    radial_mom,
    mixing,
    mixing_mom,
    w_in,
    w_mid,
    w_out,
    mom_in,
    mom_mid,
    mom_out,
    cot_features,
    cot_charges,
):
    batches, atoms, width = features.shape
    per_owner, hidden_width = w_in.shape[1], w_in.shape[3]
    owners = lax.axis_size("elem")
    shells = radial.shape[1]
    holders = per_owner * owners
    cap = 2 * atoms // holders
    rim = atoms // 8
    sizes = (owners, per_owner, cap)
    by_rows = (holders, 1, batches * cap, width)
    by_atom = (holders, 1, batches, cap, width)
    barrier = lax.optimization_barrier
    mine = lax.axis_index("pair").astype(jnp.int32)[None]
    slab = lax.axis_index("slab").astype(jnp.int32)[None]
    slabs = lax.axis_size("slab")
    padded = round_up(hidden_width, LANES)
    flat_rows = sum(flat_blocks(width, padded)) * padded
    piece = round_up(-(-flat_rows // slabs), 16)

    place, place_t, packed, source, first, last = start(
        elements, features, charges, cot_features, cot_charges, mixing, rim, sizes
    )
    arrived = swap(packed).reshape(holders, 2, batches * cap, width)
    left, right = to_both_sides(first, last)
    band, band_t = make_bands(distances, neighbours, counts, shells, rim)
    old_weights = [native(w, which) for which, w in enumerate((w_in, w_mid, w_out))]
    old_moms = [native(m, which, False) for which, m in enumerate((mom_in, mom_mid, mom_out))]
    weights = cast_weights(mine, old_weights, hidden_width, per_owner, width)

    message = edge_forward(source, left, right, band, radial, 0, place, sizes)
    message, arrived = barrier((message, arrived))
    message = swap(message).reshape(by_rows)
    result, pre_one, pre_two = network_forward(arrived, message, weights, 0)
    back, halves = barrier(
        (swap(result).reshape(by_atom), half_moments(old_moms, hidden_width, per_owner, flat_rows))
    )
    hidden_one, charge_one, source_one, first, last = update_atoms(
        back, 0, place_t, features, charges, mixing, 1, rim
    )

    left_one, right_one = to_both_sides(first, last)
    message_one = edge_forward(source_one, left_one, right_one, band, radial, 1, place, sizes)
    message_one = swap(message_one).reshape(by_rows)
    result_one, rows_one, grad_hidden, grad_message, *saved = network_turn(
        arrived, result, message_one, weights, 1
    )
    grad_message = swap(grad_message).reshape(by_atom)
    pieces = weight_grad(slab, rows_one, message_one, arrived, 1, saved, (piece, LANES), slabs)
    grad_message, grad_hidden, pieces = barrier((grad_message, grad_hidden, pieces))
    grad_hidden = swap(grad_hidden).reshape(by_atom)
    pieces_one = exchange(pieces)
    inner, to_left, to_right, radial_grad = edge_backward(
        grad_message, place_t, source_one, left_one, right_one, band, band_t, radial, 1
    )
    to_left, to_right, pieces_one[1] = barrier((to_left, to_right, pieces_one[1]))
    from_left, from_right = to_both_sides(to_left, to_right)
    from_left, pieces_one[-1] = barrier((from_left, pieces_one[-1]))
    grad, grad_charge, small_one, packed = finish(
        inner, from_left, from_right, grad_hidden, place_t, cot_features, cot_charges, charge_one,
        mixing, 1, radial_grad, place,
    )

    grad_update = swap(packed).reshape(by_rows)
    grad_update, piece_one = barrier((grad_update, sum_arrays(pieces_one)[0]))
    totals_one = to_all(piece_one)
    grad_message, both, *saved = network_backward(grad_update, pre_one, pre_two, result_one, weights, 0)
    grad_message, totals_one[1] = barrier((grad_message, totals_one[1]))
    grad_message = swap(grad_message).reshape(by_atom)
    pieces = weight_grad(slab, arrived, message, grad_update, 0, saved, (piece, LANES), slabs)
    grad_message, both, pieces = barrier((grad_message, both, pieces))
    pieces_zero = exchange(pieces)
    both = swap(both).reshape(holders, 2, batches, cap, width)
    inner, to_left, to_right, radial_grad = edge_backward(
        grad_message, place_t, source, left, right, band, band_t, radial, 0
    )
    total_one, pieces_zero[1], inner = barrier((join(slab, totals_one), pieces_zero[1], inner))
    from_left, from_right = to_both_sides(to_left, to_right)
    task = lambda layer: layer * per_owner + mine
    step = muon_step(task(1), total_one, halves, hidden_width)
    pieces_zero, from_left, from_right, _ = barrier((pieces_zero, from_left, from_right, step))
    step, other_one = barrier((step, other_of_pair(total_one)))
    steps_one = (step, other_of_pair(step))
    copies, from_left = barrier((sum_arrays(pieces_zero, slabs), from_left))
    total_zero = lax.all_to_all(copies, "slab", split_axis=0, concat_axis=0, tiled=True)
    total_zero = total_zero.reshape(slabs * piece, LANES)
    grad_features, grad_charges, smalls, features_out, charges_out = finish(
        inner, from_left, from_right, both, place_t, grad, grad_charge, charges, mixing, 0, radial_grad,
        last=(small_one, hidden_one, charge_one),
    )
    (smalls,) = sum_arrays(to_all(smalls, "elem"))
    total_zero, steps_one, smalls = barrier((total_zero, steps_one, smalls))
    news = [native(jnp.zeros(m.shape, F32), which, False) for which, m in enumerate((mom_in, mom_mid, mom_out))]
    news = [shape_of(new.shape, F32) for new in news] * 2
    sizes = (hidden_width, per_owner)
    done = apply_layer(mine, (total_one, other_one), steps_one, halves, old_weights, news, 1, *sizes)
    step = muon_step(task(0), total_zero, halves, hidden_width)
    step, other, smalls = barrier((step, other_of_pair(total_zero), to_all(smalls)))
    steps = (step, other_of_pair(step))
    (smalls,) = sum_arrays(smalls)
    new_radial, new_radial_mom, new_mixing, new_mixing_mom = small_step(
        (smalls, other_of_pair(smalls)), radial, radial_mom, mixing, mixing_mom
    )
    done = apply_layer(mine, (total_zero, other), steps, halves, old_weights, news, 0, *sizes, done)
    news = [from_native(value, which % 3, per_owner, hidden_width) for which, value in enumerate(done)]
    return (
        features_out,
        charges_out,
        grad_features,
        grad_charges,
        *news[3:],
        *news[:3],
        new_radial,
        new_radial_mom,
        new_mixing,
        new_mixing_mom,
    )


def solution(mesh):
    in_specs = (
        P(None, EVERY, None),
        P(None, None, EVERY),
        P(None, EVERY),
        P(None, None, EVERY),
        P(None, EVERY),
        P(None, None, EVERY),
        P(),
        P(),
        P(),
        P(),
        P(None, "elem", None, None),
        P(None, "elem", None, None),
        P(None, "elem", None, None),
        P(None, "elem", None, None),
        P(None, "elem", None, None),
        P(None, "elem", None, None),
        P(None, EVERY, None),
        P(None, None, EVERY),
    )
    out_specs = (
        P(None, EVERY, None),
        P(None, None, EVERY),
        P(None, EVERY, None),
        P(None, None, EVERY),
        P(None, "elem", None, None),
        P(None, "elem", None, None),
        P(None, "elem", None, None),
        P(None, "elem", None, None),
        P(None, "elem", None, None),
        P(None, "elem", None, None),
        P(),
        P(),
        P(),
        P(),
    )
    devices = mesh.devices
    folded = jax.sharding.Mesh(devices.reshape(devices.shape[0] // 2, 2, devices.shape[1]), EVERY)
    return jax.shard_map(
        on_device, mesh=folded, in_specs=in_specs, out_specs=out_specs, check_vma=False
    )
```
